32 devices in a mesh: grp: 2 (over x), tile: 16 (over z, y, core).
Axes of the slice: x: 2, y: 2, z: 4, core: 2. Of those that a mesh axis runs over, the one named last changes fastest.
Arguments:
- subgrids: bfloat16 [8192, 2, 1024], P(('grp', 'tile')), parts along dimension 0, may hold values from -10 to 10
- stations: int32 [8192, 2], P(('grp', 'tile')), parts along dimension 0, may hold values from 0 to 127, as said below
- time_slots: int32 [8192], P(('grp', 'tile')), parts along dimension 0, may hold values from 0 to 7
- assign: int32 [32, 16, 64], P(('grp', 'tile')), parts along dimension 0, may hold values from 0 to 255, as said below
- counts: int32 [32, 16], P(('grp', 'tile')), parts along dimension 0, may hold values from 0 to 64, as said below
- beam_coefs: bfloat16 [256, 8, 256], P(('grp', 'tile')), parts along dimension 0, may hold values from -0.5 to 0.5
- beam_basis: bfloat16 [2, 128, 1024], replicated, may hold values from -6 to 6
- frequencies: float32 [64], P('grp'), parts along dimension 0, may hold values from 0.5 to 2
- uv_tracks: float32 [32, 16, 64, 2, 4], P(('grp', 'tile')), parts along dimension 0, may hold values from -8 to 8
- observed: float32 [32, 16, 64, 2, 128], P(('grp', 'tile')), parts along dimension 0, may hold values from -6 to 6
Outputs:
- residual: float32 [32, 16, 64, 2, 128], P(('grp', 'tile')), parts along dimension 0
The draws below stay inside these ranges and needn't reach their ends.
There are 2 independent parts, one for each index of `grp`. The reference program is written for one: setup_inputs(seed, part) draws one part's arguments, and reference() takes and returns one part's arrays. A program takes and returns all parts, laid end to end along the dimension named above; an argument that names none is the same for every part. Nothing has to cross between parts.
Inputs may be any that keep to these rules, and one draw needn't show every extreme that they name: `assign`: for every source s, the live slots (c < counts[s, d]) of all d together name each of the numbers 0 to 255 exactly once; slots that are not live hold 0. `counts`: each row sums to 256. In every draw one baseline block receives 64 subgrids from every source. The two stations of a row differ.
All inputs are finite; a program needn't handle non-finite values.
Results may differ from the reference program's by a relative error of at most 0.0021.
Values may be sent and summed in bfloat16 or wider, within the bound.
No kernel may reach another device: no remote copies, remote signals or barrier semaphores. Data moves between devices by JAX's collectives and lax.ppermute only.
A program may use at most 64 MiB of HBM per device.

```python
import math
import jax
import jax.numpy as jnp
from jax import lax

SG = 32
K = 128
CHAN = 32
TSTEP = 4
TSLOT = 8
SUB_DEV = 256
TILES = 16
CAP = 64
NSUB = 4096
STATIONS = 128
PIX = 1024
NV = 128


def route_tables(key):
    hot_key, score_key, order_key = jax.random.split(key, 3)
    hottest = jax.random.randint(hot_key, (), 0, TILES)
    targets = jnp.arange(TILES, dtype=jnp.int32)
    ranking = (targets - hottest) % TILES
    slot_ids = jnp.arange(CAP, dtype=jnp.int32)
    leaning = -64 * ranking[:, None] // TILES - 32 * slot_ids[None, :] // CAP
    leaning = leaning + jnp.where(ranking[:, None] == 0, 100000, 0)
    flat_ids = jnp.arange(TILES * CAP, dtype=jnp.int32)

    def one_source(score_part, order_part):
        noise = jax.random.randint(score_part, (TILES, CAP), 0, 64)
        scores = (noise + leaning).reshape(TILES * CAP) * (TILES * CAP) + flat_ids
        top_scores, picked = lax.top_k(scores, SUB_DEV)
        taken = jnp.zeros((TILES * CAP,), jnp.int32).at[picked].set(1).reshape(TILES, CAP)
        totals = jnp.sum(taken, axis=1).astype(jnp.int32)
        live_slots = (slot_ids[None, :] < totals[:, None]).astype(jnp.int32).reshape(TILES * CAP)
        placing = jnp.clip(jnp.cumsum(live_slots) - 1, 0, SUB_DEV - 1)
        ordering = jax.random.permutation(order_part, SUB_DEV).astype(jnp.int32)
        listing = jnp.where(live_slots > 0, ordering[placing], 0)
        return (listing.reshape(TILES, CAP).astype(jnp.int32), totals)
    return jax.vmap(one_source)(jax.random.split(score_key, TILES), jax.random.split(order_key, TILES))


def draw_assign(key, part):
    tables = route_tables(key)
    return tables[0]


def draw_counts(key, part):
    tables = route_tables(key)
    return tables[1]


def draw_stations(key, part):
    key = jax.random.fold_in(key, 13)
    first_key, gap_key = jax.random.split(key)
    first_station = jax.random.randint(first_key, (NSUB,), 0, STATIONS)
    station_gap = jax.random.randint(gap_key, (NSUB,), 1, STATIONS)
    second_station = (first_station + station_gap) % STATIONS
    return jnp.stack([first_station, second_station], axis=1).astype(jnp.int32)


def draw_subgrids(key, part):
    key = jax.random.fold_in(key, 21)
    noise_key, row_key, col_key, amp_key, angle_key = jax.random.split(key, 5)
    noise = 0.5 * jax.random.normal(noise_key, (NSUB, 2, SG, SG), jnp.float32)
    row_pick = jax.random.randint(row_key, (NSUB,), 0, SG)
    col_pick = jax.random.randint(col_key, (NSUB,), 0, SG)
    amplitude = jax.random.uniform(amp_key, (NSUB, 2), jnp.float32, 2.5, 4.0)
    angles = jax.random.uniform(angle_key, (NSUB, 2), jnp.float32, -math.pi, math.pi)
    cells = jnp.arange(SG, dtype=jnp.int32)
    on_row = (cells[None, :] == row_pick[:, None]).astype(jnp.float32)[:, :, None]
    on_col = (cells[None, :] == col_pick[:, None]).astype(jnp.float32)[:, None, :]
    row_re = (amplitude[:, 0] * jnp.cos(angles[:, 0]))[:, None, None]
    row_im = (amplitude[:, 0] * jnp.sin(angles[:, 0]))[:, None, None]
    col_re = (amplitude[:, 1] * jnp.cos(angles[:, 1]))[:, None, None]
    col_im = (amplitude[:, 1] * jnp.sin(angles[:, 1]))[:, None, None]
    lines_re = row_re * on_row + col_re * on_col
    lines_im = row_im * on_row + col_im * on_col
    grids = noise + jnp.stack([lines_re, lines_im], axis=1)
    grids = jnp.clip(grids, -10.0, 10.0)
    return grids.reshape(NSUB, 2, SG * SG).astype(jnp.bfloat16)


def draw_beam_coefs(key, part):
    key = jax.random.fold_in(key, 22)
    common_key, own_key = jax.random.split(key)
    spread = (5.0 * K) ** (-0.5)
    common = jax.random.normal(common_key, (1, TSLOT, 2 * K), jnp.float32)
    own = jax.random.normal(own_key, (STATIONS, TSLOT, 2 * K), jnp.float32)
    values = spread * (common + 0.5 * own)
    return jnp.clip(values, -0.5, 0.5).astype(jnp.bfloat16)


def touch_ends(drawn, key, least, largest):
    dims = drawn.shape
    place = [jax.random.randint(jax.random.fold_in(key, axis), (), 0, dims[axis]) for axis in range(len(dims))]
    drawn = drawn.at[tuple(place)].set(least)
    longest = dims.index(max(dims))
    place[longest] = (place[longest] + 1) % dims[longest]
    return drawn.at[tuple(place)].set(largest)


def levels(key, extent, cuts, least, top_value):
    level = 1.0
    for dim, blocks in cuts:
        heights = jax.random.uniform(jax.random.fold_in(jax.random.fold_in(key, 6), dim), (blocks,), jnp.float32, least / len(cuts), top_value / len(cuts))
        level = level * jnp.repeat(jnp.exp(heights), extent[dim] // blocks).reshape((-1,) + (1,) * (len(extent) - 1 - dim))
    return level


def scatter_about(rng, dims, deviation, limit, cuts=(), held_as=jnp.bfloat16):
    values = jax.random.normal(rng, dims, jnp.float32) * deviation
    if len(cuts) > 0:
        values = levels(rng, dims, cuts, -0.22, 0.18) * values
    return jnp.clip(values, min=-limit, max=limit).astype(held_as)


def setup_inputs(seed: int = 0, part: int = 0) -> dict:
    seeds = jax.random.split(jax.random.key(seed), 11)
    part_splits = jax.random.split(jax.random.fold_in(seeds[10], part), 11)
    subgrids = draw_subgrids(jax.random.fold_in(jax.random.fold_in(seeds[10], part), 71), part)
    stations = draw_stations(jax.random.fold_in(jax.random.fold_in(seeds[10], part), 71), part)
    time_slots = touch_ends(jax.random.randint(part_splits[2], (NSUB,), 0, TSLOT), jax.random.fold_in(part_splits[2], 1), 0, TSLOT - 1).astype(jnp.int32)
    assign = draw_assign(jax.random.fold_in(jax.random.fold_in(seeds[10], part), 71), part)
    counts = draw_counts(jax.random.fold_in(jax.random.fold_in(seeds[10], part), 71), part)
    beam_coefs = draw_beam_coefs(jax.random.fold_in(jax.random.fold_in(seeds[10], part), 71), part)
    beam_basis = scatter_about(seeds[6], (2, K, PIX), 1.0, 6.0)
    frequencies = jnp.clip(jnp.exp(jax.random.uniform(part_splits[7], (CHAN,), jnp.float32, math.log(0.5), math.log(2.0))), 0.5, 2.0)
    uv_tracks = jnp.clip(jax.random.uniform(part_splits[8], (TILES, TILES, CAP, 2, TSTEP), jnp.float32, -8.0, 8.0) * levels(part_splits[8], (TILES, TILES, CAP, 2, TSTEP), ((0, 16),), -0.4, 0.0), -8.0, 8.0)
    observed = scatter_about(part_splits[9], (TILES, TILES, CAP, 2, NV), 1.0, 6.0, ((0, 16),), jnp.float32)
    return dict(subgrids=subgrids, stations=stations, time_slots=time_slots, assign=assign, counts=counts, beam_coefs=beam_coefs, beam_basis=beam_basis, frequencies=frequencies, uv_tracks=uv_tracks, observed=observed)


TWO_PI = 2.0 * math.pi


def beam_matrix(beam_basis):
    real_part = beam_basis[0]
    imag_part = beam_basis[1]
    upper = jnp.concatenate([real_part, imag_part], axis=1)
    lower = jnp.concatenate([-imag_part, real_part], axis=1)
    return jnp.concatenate([upper, lower], axis=0)


def images_of(subgrids):
    grid_re = subgrids[:, 0].astype(jnp.float32).reshape(NSUB, SG, SG)
    grid_im = subgrids[:, 1].astype(jnp.float32).reshape(NSUB, SG, SG)
    transformed = jnp.fft.ifft2(grid_re + 1j * grid_im)
    stacked = jnp.stack([jnp.real(transformed), jnp.imag(transformed)], axis=1)
    return stacked.reshape(NSUB, 2, PIX).astype(jnp.bfloat16)


def predict_block(images, first_rows, second_rows, tracks, table, matrix, frequencies):
    number = images.shape[0]
    beam_first = jnp.dot(table[first_rows], matrix, preferred_element_type=jnp.float32)
    beam_second = jnp.dot(table[second_rows], matrix, preferred_element_type=jnp.float32)
    first_re = beam_first[:, :PIX]
    first_im = beam_first[:, PIX:]
    second_re = beam_second[:, :PIX]
    second_im = beam_second[:, PIX:]
    gain_re = first_re * second_re + first_im * second_im
    gain_im = first_im * second_re - first_re * second_im
    image_re = images[:, 0].astype(jnp.float32)
    image_im = images[:, 1].astype(jnp.float32)
    weighted_re = (image_re * gain_re - image_im * gain_im).astype(jnp.bfloat16).reshape(number, SG, SG)
    weighted_im = (image_re * gain_im + image_im * gain_re).astype(jnp.bfloat16).reshape(number, SG, SG)
    weighted = jnp.concatenate([weighted_re, weighted_im], axis=2)
    u_coord = (tracks[:, 0, :, None] * frequencies[None, None, :]).reshape(number, NV)
    v_coord = (tracks[:, 1, :, None] * frequencies[None, None, :]).reshape(number, NV)
    offsets = jnp.arange(SG, dtype=jnp.float32) - 0.5 * SG
    angle_u = (-TWO_PI / SG) * offsets[None, :, None] * u_coord[:, None, :]
    cos_u = jnp.cos(angle_u).astype(jnp.bfloat16)
    sin_u = jnp.sin(angle_u).astype(jnp.bfloat16)
    phase = jnp.concatenate([jnp.concatenate([cos_u, sin_u], axis=2), jnp.concatenate([-sin_u, cos_u], axis=2)], axis=1)
    partial_sums = jnp.einsum("byx,bxj->byj", weighted.astype(jnp.float32), phase.astype(jnp.float32))
    part_re = partial_sums[:, :, :NV]
    part_im = partial_sums[:, :, NV:]
    angle_v = (-TWO_PI / SG) * offsets[None, :, None] * v_coord[:, None, :]
    cos_v = jnp.cos(angle_v)
    sin_v = jnp.sin(angle_v)
    model_re = jnp.sum(part_re * cos_v - part_im * sin_v, axis=1)
    model_im = jnp.sum(part_re * sin_v + part_im * cos_v, axis=1)
    return jnp.stack([model_re, model_im], axis=1)


def reference(subgrids, stations, time_slots, assign, counts, beam_coefs, beam_basis, frequencies, uv_tracks, observed):
    table = beam_coefs.reshape(STATIONS * TSLOT, 2 * K)
    matrix = beam_matrix(beam_basis)
    first_rows = (stations[:, 0] * TSLOT + time_slots).astype(jnp.int32)
    second_rows = (stations[:, 1] * TSLOT + time_slots).astype(jnp.int32)
    images = images_of(subgrids)
    live = jnp.arange(CAP, dtype=jnp.int32)[None, None, :] < counts[:, :, None]
    flat_assign = assign.reshape(TILES, TILES * CAP)
    flat_live = live.reshape(TILES, TILES * CAP)
    local_ids = jnp.arange(SUB_DEV, dtype=jnp.int32)
    matches = (flat_assign[:, None, :] == local_ids[None, :, None]) & flat_live[:, None, :]
    slot_ids = jnp.arange(TILES * CAP, dtype=jnp.int32)
    position = jnp.sum(jnp.where(matches, slot_ids[None, None, :], 0), axis=2).astype(jnp.int32)
    target = position // CAP
    within = position % CAP
    source = jnp.broadcast_to(jnp.arange(TILES, dtype=jnp.int32)[:, None], (TILES, SUB_DEV))
    tracks_sub = uv_tracks[target, source, within].reshape(NSUB, 2, TSTEP)
    block_len = math.gcd(NSUB, 64)
    groups = NSUB // block_len

    def one_block(members):
        return predict_block(members[0], members[1], members[2], members[3], table, matrix, frequencies)

    models = lax.map(one_block, (images.reshape(groups, block_len, 2, PIX), first_rows.reshape(groups, block_len), second_rows.reshape(groups, block_len), tracks_sub.reshape(groups, block_len, 2, TSTEP)))
    models = models.reshape(NSUB, 2, NV)
    picked = (jnp.arange(TILES, dtype=jnp.int32)[:, None, None] * SUB_DEV + assign).astype(jnp.int32)
    model_slots = models[picked] * live.astype(jnp.float32)[:, :, :, None, None]
    return observed - jnp.transpose(model_slots, (1, 0, 2, 3, 4))
```

```python
import functools
import math

import jax
import jax.numpy as jnp
import ml_dtypes
import numpy as np
from jax import lax
from jax.experimental import pallas as pl
from jax.experimental.pallas import tpu as pltpu
from jax.sharding import PartitionSpec as P

TWO_PI = 2.0 * math.pi
F32 = jnp.float32
BF16 = jnp.bfloat16
VMEM_LIMIT = 56 * 1024 * 1024
NT = (((1,), (1,)), ((), ()))
TN = (((0,), (0,)), ((), ()))


def dot(a, b, dims=(((1,), (0,)), ((), ()))):
    return lax.dot_general(a, b, dims, preferred_element_type=F32)


def transform_matrices(edge):
    low = edge // 8
    b = np.arange(low)[:, None, None, None]
    a = np.arange(edge)[None, :, None, None]
    inner = np.arange(low)[None, None, :, None]
    x = np.arange(edge)[None, None, None, :]
    kept = []
    for outer in range(8):
        turns = (b * (outer + 8 * inner) + a * x) % edge
        angle = (TWO_PI / edge * turns).reshape(low * edge, low * edge)
        c, s = np.cos(angle) / edge**2, np.sin(angle) / edge**2
        kept.append(np.block([[c, s], [-s, c]]))
    full = np.stack(kept)
    high = full.astype(ml_dtypes.bfloat16)
    rest = (full - high.astype(np.float64)).astype(ml_dtypes.bfloat16)
    return high, rest


def eight_point(re, im):
    half = math.sqrt(0.5)

    def four(r, i):
        s0r, s0i, d0r, d0i = r[0] + r[2], i[0] + i[2], r[0] - r[2], i[0] - i[2]
        s1r, s1i, d1r, d1i = r[1] + r[3], i[1] + i[3], r[1] - r[3], i[1] - i[3]
        return (
            [s0r + s1r, d0r - d1i, s0r - s1r, d0r + d1i],
            [s0i + s1i, d0i + d1r, s0i - s1i, d0i - d1r],
        )

    er, ei = four(re[0::2], im[0::2])
    orr, oi = four(re[1::2], im[1::2])
    tr = [orr[0], half * (orr[1] - oi[1]), -oi[2], -half * (orr[3] + oi[3])]
    ti = [oi[0], half * (orr[1] + oi[1]), orr[2], half * (orr[3] - oi[3])]
    out_re = [er[m] + tr[m] for m in range(4)] + [er[m] - tr[m] for m in range(4)]
    out_im = [ei[m] + ti[m] for m in range(4)] + [ei[m] - ti[m] for m in range(4)]
    return out_re, out_im


def transform_kernel(cells, high, rest, image, sum_high, sum_rest):
    number = cells.shape[2]
    lanes = cells.shape[3]
    step = 16

    @pl.loop(0, number // step)
    def _(n):
        rows = pl.ds(pl.multiple_of(n * step, step), step)
        re = [cells[0, k, rows, :].astype(F32) for k in range(8)]
        im = [cells[1, k, rows, :].astype(F32) for k in range(8)]
        out_re, out_im = eight_point(re, im)
        for m in range(8):
            for part, value in ((0, out_re[m]), (1, out_im[m])):
                top = value.astype(BF16)
                cols = slice(part * lanes, (part + 1) * lanes)
                sum_high[m, rows, cols] = top
                sum_rest[m, rows, cols] = (value - top.astype(F32)).astype(BF16)

    @pl.loop(0, 8)
    def _(m):
        a, b = sum_high[m], sum_rest[m]
        total = dot(a, high[m]) + (dot(b, high[m]) + dot(a, rest[m]))
        image[m] = total.astype(BF16)


def unit_powers(turns):
    turns = turns - jnp.round(turns)
    angle = (0.5 * math.pi) * turns
    sq = angle * angle
    s = angle * (
        1.0 + sq * (-1.0 / 6 + sq * (1.0 / 120 + sq * (-1.0 / 5040 + sq * (1.0 / 362880))))
    )
    c = 1.0 + sq * (
        -0.5 + sq * (1.0 / 24 + sq * (-1.0 / 720 + sq * (1.0 / 40320 - sq * (1.0 / 3628800))))
    )
    for _ in range(2):
        c, s = 1.0 - 2.0 * (s * s), 2.0 * (s * c)
    return c, s


def cmul(ar, ai, br, bi):
    return ar * br - ai * bi, ar * bi + ai * br


def predict_kernel(
    table,
    slot_row,
    stations,
    time_slots,
    tracks,
    freq,
    basis,
    image,
    payload,
    route,
    weights,
    coef_first,
    coef_second,
    wre,
    wim,
    pure,
    puim,
    zrow,
    hre,
    him,
    zv,
    interleaved,
    *,
    slot_count,
):
    number = image.shape[1]
    slots = slot_row.shape[1]
    rows_all = table.shape[0]
    chan = freq.shape[1]
    steps = tracks.shape[0] // 2
    terms = basis.shape[1]

    down = lax.broadcasted_iota(jnp.int32, (number, slots), 0)
    route[...] = (slot_row[...] == down).astype(F32).astype(BF16)

    tr = tracks[...]
    t_hi = tr.astype(BF16)
    left = tr - t_hi.astype(F32)
    t_mid = left.astype(BF16)
    t_lo = (left - t_mid.astype(F32)).astype(BF16)
    pieces = jnp.concatenate(
        [t_hi.astype(F32), t_mid.astype(F32), t_lo.astype(F32)], axis=0
    ).astype(BF16)
    per_sub = dot(route[...], pieces, NT).astype(BF16)
    wide = 2 * steps * chan
    from_row = lax.broadcasted_iota(jnp.int32, (6 * steps, wide), 0) % (2 * steps)
    to_lane = lax.broadcasted_iota(jnp.int32, (6 * steps, wide), 1) // chan
    spread = (from_row == to_lane).astype(F32).astype(BF16)
    uv = dot(per_sub, spread)
    vis = steps * chan
    fr = jnp.concatenate([freq[...]] * steps, axis=1)
    scale = -1.0 / 32.0
    ur, ui = unit_powers(uv[:, :vis] * fr * scale)
    vr, vi = unit_powers(uv[:, vis:] * fr * scale)

    pure[pl.ds(0, number, stride=8), :] = jnp.ones_like(ur)
    puim[pl.ds(0, number, stride=8), :] = jnp.zeros_like(ur)
    pure[pl.ds(1, number, stride=8), :] = ur
    puim[pl.ds(1, number, stride=8), :] = ui
    cr, ci = ur, ui
    for k in range(2, 8):
        cr, ci = cmul(cr, ci, ur, ui)
        pure[pl.ds(k, number, stride=8), :] = cr
        puim[pl.ds(k, number, stride=8), :] = ci
    cr, ci = cmul(cr, ci, ur, ui)
    zrow[0] = cr
    zrow[1] = ci
    cr, ci = cmul(cr, ci, cr, ci)
    zrow[2] = cr
    zrow[3] = ci
    zv[0] = vr
    zv[1] = vi
    cr, ci = vr, vi
    for _ in range(3):
        cr, ci = cmul(cr, ci, cr, ci)
    zrow[4] = cr
    zrow[5] = ci

    index = (stations[...] * slot_count + time_slots[...]).astype(F32)
    index = jnp.concatenate([index, jnp.zeros((6, number), F32)], axis=0).T
    index = index.astype(jnp.int32)
    across = lax.broadcasted_iota(jnp.int32, (number, rows_all), 1)
    for which, coef in ((0, coef_first), (1, coef_second)):
        pick = (index[:, which : which + 1] == across).astype(F32).astype(BF16)
        coef[...] = dot(pick, table[...]).astype(BF16)

    for m in range(8):
        cols = slice(m * 128, (m + 1) * 128)
        b_re, b_im = basis[0, :, cols], basis[1, :, cols]
        weights[m, :terms, :128] = b_re
        weights[m, :terms, 128:] = b_im
        weights[m, terms:, :128] = -b_im
        weights[m, terms:, 128:] = b_re

    block = 64
    for m in range(8):
        @pl.loop(0, number // block)
        def _(n, m=m):
            rows = pl.ds(pl.multiple_of(n * block, block), block)
            first = dot(coef_first[rows, :], weights[m])
            second = dot(coef_second[rows, :], weights[m])
            f_re, f_im, s_re, s_im = first[:, :128], first[:, 128:], second[:, :128], second[:, 128:]
            g_re = f_re * s_re + f_im * s_im
            g_im = f_im * s_re - f_re * s_im
            i_re = image[m, rows, :128].astype(F32)
            i_im = image[m, rows, 128:].astype(F32)
            to = pl.ds(n * (block * 8) + m, block, stride=8)
            wre[to, :] = i_re * g_re - i_im * g_im
            wim[to, :] = i_re * g_im + i_im * g_re

    lane = lax.broadcasted_iota(jnp.int32, (8, 256), 1)
    inner = (lane // 32) % 4
    masks = [inner == j for j in range(4)]
    unroll = 4

    def one(g):
        at = pl.ds(pl.multiple_of(g * 8, 8), 8)
        w = jnp.concatenate([wre[at, :], wim[at, :]], axis=1)
        lhs = jnp.concatenate([jnp.where(k, w, 0.0) for k in masks], axis=0).astype(BF16)
        p_re, p_im = pure[at, :], puim[at, :]
        z = [jnp.broadcast_to(zrow[k, pl.ds(g, 1), :], (8, 128)) for k in range(6)]
        rr, ii, ri, ir = p_re * z[0], p_im * z[1], p_re * z[1], p_im * z[0]
        up_re, up_im = rr - ii, ri + ir
        dn_re, dn_im = rr + ii, ir - ri
        rr, ii, ri, ir = p_re * z[2], p_im * z[3], p_re * z[3], p_im * z[2]
        lo_re, lo_im = rr + ii, ir - ri
        c = jnp.concatenate([lo_re, dn_re, p_re, up_re], axis=0).astype(BF16)
        s = jnp.concatenate([lo_im, dn_im, p_im, up_im], axis=0).astype(BF16)
        top = jnp.concatenate([c, s], axis=1)
        low = jnp.concatenate([-s, c], axis=1)
        rhs = jnp.concatenate([top] * 4 + [low] * 4, axis=0)
        out = dot(lhs, rhs)
        h_re, h_im = out[24:32, :128], out[24:32, 128:]
        for j in (2, 1, 0):
            n_re = h_re * z[4] - h_im * z[5] + out[8 * j : 8 * j + 8, :128]
            h_im = h_re * z[5] + h_im * z[4] + out[8 * j : 8 * j + 8, 128:]
            h_re = n_re
        hre[at, :] = h_re
        him[at, :] = h_im

    @pl.loop(0, number // unroll)
    def _(n):
        for k in range(unroll):
            one(n * unroll + k)

    vr, vi = zv[0], zv[1]
    a_re = hre[pl.ds(7, number, stride=8), :]
    a_im = him[pl.ds(7, number, stride=8), :]
    for k in range(6, -1, -1):
        n_re = a_re * vr - a_im * vi + hre[pl.ds(k, number, stride=8), :]
        a_im = a_re * vi + a_im * vr + him[pl.ds(k, number, stride=8), :]
        a_re = n_re
    cr, ci = cmul(zrow[4], zrow[5], zrow[4], zrow[5])
    m_re, m_im = a_re * cr + a_im * ci, a_im * cr - a_re * ci
    models = jnp.concatenate([m_re, m_im], axis=1).astype(BF16)
    sent = dot(route[...], models, TN)
    interleaved[pl.ds(0, slots, stride=2), :] = sent[:, :128]
    interleaved[pl.ds(1, slots, stride=2), :] = sent[:, 128:]
    payload[...] = interleaved[...].astype(BF16)


def per_device(
    subgrids,
    stations,
    time_slots,
    assign,
    counts,
    beam_coefs,
    beam_basis,
    frequencies,
    uv_tracks,
    observed,
):
    tiles = lax.axis_size("tile")
    capacity = assign.shape[2]
    slots = tiles * capacity
    number = subgrids.shape[0]
    pixels = subgrids.shape[2]
    edge = math.isqrt(pixels)
    slot_count = beam_coefs.shape[1]
    terms2 = beam_coefs.shape[2]
    steps = uv_tracks.shape[4]
    chan = frequencies.shape[0]
    vis = steps * chan
    vmem = pl.BlockSpec(memory_space=pltpu.VMEM)
    params = pltpu.CompilerParams(vmem_limit_bytes=VMEM_LIMIT)

    own_tracks = jnp.transpose(uv_tracks[0], (0, 2, 3, 1)).reshape(tiles, 2 * steps, capacity)
    tracks = lax.all_to_all(own_tracks, "tile", split_axis=0, concat_axis=0, tiled=True)
    tracks = jnp.transpose(tracks, (1, 0, 2)).reshape(2 * steps, slots)
    table = lax.all_gather(beam_coefs, "tile", axis=0, tiled=True)
    table = table.reshape(table.shape[0] * slot_count, terms2)

    cells = jnp.transpose(subgrids.reshape(number, 2, 8, 128), (1, 2, 0, 3))
    high, rest = transform_matrices(edge)
    image = pl.pallas_call(
        transform_kernel,
        out_shape=jax.ShapeDtypeStruct((8, number, 256), BF16),
        in_specs=[vmem] * 3,
        out_specs=vmem,
        scratch_shapes=[
            pltpu.VMEM((8, number, 256), BF16),
            pltpu.VMEM((8, number, 256), BF16),
        ],
        compiler_params=params,
        name="transform",
    )(cells, jnp.asarray(high), jnp.asarray(rest))

    basis = jnp.transpose(
        beam_basis.reshape(2, terms2 // 2, 4, 8, edge), (0, 1, 3, 2, 4)
    ).reshape(2, terms2 // 2, pixels)
    live = jnp.arange(capacity, dtype=jnp.int32)[None, :] < counts[0][:, None]
    slot_row = jnp.where(live, assign[0], -1).reshape(1, slots)
    payload = pl.pallas_call(
        functools.partial(predict_kernel, slot_count=slot_count),
        out_shape=jax.ShapeDtypeStruct((2 * slots, vis), BF16),
        in_specs=[vmem] * 8,
        out_specs=vmem,
        scratch_shapes=[
            pltpu.VMEM((number, slots), BF16),
            pltpu.VMEM((8, 256, 256), BF16),
            pltpu.VMEM((number, terms2), BF16),
            pltpu.VMEM((number, terms2), BF16),
            pltpu.VMEM((number * 8, 128), F32),
            pltpu.VMEM((number * 8, 128), F32),
            pltpu.VMEM((number * 8, vis), F32),
            pltpu.VMEM((number * 8, vis), F32),
            pltpu.VMEM((6, number, vis), F32),
            pltpu.VMEM((number * 8, vis), F32),
            pltpu.VMEM((number * 8, vis), F32),
            pltpu.VMEM((2, number, vis), F32),
            pltpu.VMEM((2 * slots, vis), F32),
        ],
        compiler_params=params,
        name="predict",
    )(
        table,
        slot_row,
        stations.T,
        time_slots.reshape(1, number),
        tracks,
        frequencies.reshape(1, chan),
        basis,
        image,
    )
    arrived = lax.all_to_all(
        payload.reshape(tiles, 2 * capacity, vis), "tile", split_axis=0, concat_axis=0, tiled=True
    )
    residual = observed - arrived.reshape(observed.shape).astype(F32)
    return residual


def solution(mesh):
    return jax.shard_map(
        per_device,
        mesh=mesh,
        in_specs=(
            P(("grp", "tile"), None, None),
            P(("grp", "tile"), None),
            P(("grp", "tile")),
            P(("grp", "tile"), None, None),
            P(("grp", "tile"), None),
            P(("grp", "tile"), None, None),
            P(),
            P("grp"),
            P(("grp", "tile"), None, None, None, None),
            P(("grp", "tile"), None, None, None, None),
        ),
        out_specs=P(("grp", "tile"), None, None, None, None),
        check_vma=False,
    )
```

```python
import functools
import math

import jax
import jax.numpy as jnp
import ml_dtypes
import numpy as np
from jax import lax
from jax.experimental import pallas as pl
from jax.experimental.pallas import tpu as pltpu
from jax.sharding import PartitionSpec as P

TWO_PI = 2.0 * math.pi
F32 = jnp.float32
BF16 = jnp.bfloat16
VMEM_LIMIT = 56 * 1024 * 1024
NT = (((1,), (1,)), ((), ()))
TN = (((0,), (0,)), ((), ()))


def dot(a, b, dims=(((1,), (0,)), ((), ()))):
    return lax.dot_general(a, b, dims, preferred_element_type=F32)


def transform_matrices(edge):
    low = edge // 8
    b = np.arange(low)[:, None, None, None]
    a = np.arange(edge)[None, :, None, None]
    inner = np.arange(low)[None, None, :, None]
    x = np.arange(edge)[None, None, None, :]
    kept = []
    for outer in range(8):
        turns = (b * (outer + 8 * inner) + a * x) % edge
        angle = (TWO_PI / edge * turns).reshape(low * edge, low * edge)
        c, s = np.cos(angle) / edge**2, np.sin(angle) / edge**2
        kept.append(np.block([[c, s], [-s, c]]))
    full = np.stack(kept)
    high = full.astype(ml_dtypes.bfloat16)
    rest = (full - high.astype(np.float64)).astype(ml_dtypes.bfloat16)
    return high, rest


def eight_point(re, im):
    half = math.sqrt(0.5)

    def four(r, i):
        s0r, s0i, d0r, d0i = r[0] + r[2], i[0] + i[2], r[0] - r[2], i[0] - i[2]
        s1r, s1i, d1r, d1i = r[1] + r[3], i[1] + i[3], r[1] - r[3], i[1] - i[3]
        return (
            [s0r + s1r, d0r - d1i, s0r - s1r, d0r + d1i],
            [s0i + s1i, d0i + d1r, s0i - s1i, d0i - d1r],
        )

    er, ei = four(re[0::2], im[0::2])
    orr, oi = four(re[1::2], im[1::2])
    tr = [orr[0], half * (orr[1] - oi[1]), -oi[2], -half * (orr[3] + oi[3])]
    ti = [oi[0], half * (orr[1] + oi[1]), orr[2], half * (orr[3] - oi[3])]
    out_re = [er[m] + tr[m] for m in range(4)] + [er[m] - tr[m] for m in range(4)]
    out_im = [ei[m] + ti[m] for m in range(4)] + [ei[m] - ti[m] for m in range(4)]
    return out_re, out_im


def transform_kernel(cells, high, rest, image, sum_high, sum_rest):
    number = cells.shape[2]
    lanes = cells.shape[3]
    step = 16

    @pl.loop(0, number // step)
    def _(n):
        rows = pl.ds(pl.multiple_of(n * step, step), step)
        re = [cells[0, k, rows, :].astype(F32) for k in range(8)]
        im = [cells[1, k, rows, :].astype(F32) for k in range(8)]
        out_re, out_im = eight_point(re, im)
        for m in range(8):
            for part, value in ((0, out_re[m]), (1, out_im[m])):
                top = value.astype(BF16)
                cols = slice(part * lanes, (part + 1) * lanes)
                sum_high[m, rows, cols] = top
                sum_rest[m, rows, cols] = (value - top.astype(F32)).astype(BF16)

    @pl.loop(0, 8)
    def _(m):
        a, b = sum_high[m], sum_rest[m]
        total = dot(a, high[m]) + (dot(b, high[m]) + dot(a, rest[m]))
        image[m] = total.astype(BF16)


def unit_powers(turns):
    turns = turns - jnp.round(turns)
    angle = (0.5 * math.pi) * turns
    sq = angle * angle
    s = angle * (
        1.0 + sq * (-1.0 / 6 + sq * (1.0 / 120 + sq * (-1.0 / 5040 + sq * (1.0 / 362880))))
    )
    c = 1.0 + sq * (
        -0.5 + sq * (1.0 / 24 + sq * (-1.0 / 720 + sq * (1.0 / 40320 - sq * (1.0 / 3628800))))
    )
    for _ in range(2):
        c, s = 1.0 - 2.0 * (s * s), 2.0 * (s * c)
    return c, s


def cmul(ar, ai, br, bi):
    return ar * br - ai * bi, ar * bi + ai * br


def pack_kernel(me, coefs, tracks, *out):
    capacity = tracks.shape[2]
    rows = coefs.shape[0]
    width = coefs.shape[1]
    for r in range(len(out)):
        plane = (me[0] // 4) ^ r
        tr = [tracks[plane * 4 + k] for k in range(4)]
        if 4 * capacity < width:
            tr.append(jnp.zeros((tr[0].shape[0], width - 4 * capacity), F32))
        tr = jnp.concatenate(tr, axis=1)
        t_hi = tr.astype(BF16).astype(F32)
        t_mid = (tr - t_hi).astype(BF16).astype(F32)
        t_lo = tr - t_hi - t_mid
        pieces = jnp.concatenate([t_hi, t_mid, t_lo, jnp.zeros_like(tr)], axis=0)
        out[r][:rows, :] = coefs[...]
        out[r][rows:, :] = pieces.astype(BF16)


def predict_kernel(me, counts, *refs, tiles, slot_count):
    blocks = refs[:tiles]
    (assign, stations, time_slots, freq, basis, image) = refs[tiles : tiles + 6]
    payload = refs[tiles + 6 : 2 * tiles + 6]
    (
        table,
        route,
        weights,
        coef_first,
        coef_second,
        wre,
        wim,
        pure,
        puim,
        zrow,
        hre,
        him,
        zv,
        interleaved,
    ) = refs[2 * tiles + 6 :]
    number = image.shape[1]
    capacity = assign.shape[1]
    slots = tiles * capacity
    rows_all = table.shape[0]
    rows_own = rows_all // tiles
    chan = freq.shape[1]
    pieces_rows = blocks[0].shape[0] - rows_own
    kinds = pieces_rows // 4
    steps = kinds // 2
    terms = basis.shape[1]
    mine = me[0]

    per = 128 // capacity
    down = lax.broadcasted_iota(jnp.int32, (number, 128), 0)
    slot = lax.broadcasted_iota(jnp.int32, (1, capacity), 1)
    held = []
    for n in range(tiles // per):
        chosen, tracks = [], []
        for r in range(n * per, (n + 1) * per):
            other = mine ^ r
            chosen.append(
                jnp.where(slot < counts[0, other], assign[pl.ds(other, 1), :], -1)
            )
            whole = blocks[r][rows_own:, :].astype(F32)
            piece = whole
            for k in range(1, 4):
                piece = jnp.where(
                    mine % 4 == k,
                    pltpu.roll(whole, whole.shape[1] - k * capacity, 1),
                    piece,
                )
            tracks.append(piece[:, :capacity])
            table[r * rows_own : (r + 1) * rows_own, :] = blocks[r][:rows_own, :]
        chosen = jnp.concatenate(chosen, axis=1)
        route[:, n * 128 : (n + 1) * 128] = (chosen == down).astype(F32).astype(BF16)
        held.append(jnp.concatenate(tracks, axis=1).astype(BF16))
    pieces = jnp.concatenate(held, axis=1)

    per_sub = dot(route[...], pieces, NT).astype(BF16)
    wide = 2 * steps * chan
    from_row = lax.broadcasted_iota(jnp.int32, (pieces_rows, wide), 0) % kinds
    to_lane = lax.broadcasted_iota(jnp.int32, (pieces_rows, wide), 1) // chan
    spread = (from_row == to_lane).astype(F32).astype(BF16)
    uv = dot(per_sub, spread)
    vis = steps * chan
    fr = jnp.concatenate([freq[...]] * steps, axis=1)
    scale = -1.0 / 32.0
    ur, ui = unit_powers(uv[:, :vis] * fr * scale)
    vr, vi = unit_powers(uv[:, vis:] * fr * scale)

    pure[pl.ds(0, number, stride=8), :] = jnp.ones_like(ur)
    puim[pl.ds(0, number, stride=8), :] = jnp.zeros_like(ur)
    pure[pl.ds(1, number, stride=8), :] = ur
    puim[pl.ds(1, number, stride=8), :] = ui
    cr, ci = ur, ui
    for k in range(2, 8):
        cr, ci = cmul(cr, ci, ur, ui)
        pure[pl.ds(k, number, stride=8), :] = cr
        puim[pl.ds(k, number, stride=8), :] = ci
    cr, ci = cmul(cr, ci, ur, ui)
    zrow[0] = cr
    zrow[1] = ci
    cr, ci = cmul(cr, ci, cr, ci)
    zrow[2] = cr
    zrow[3] = ci
    zv[0] = vr
    zv[1] = vi
    cr, ci = vr, vi
    for _ in range(3):
        cr, ci = cmul(cr, ci, cr, ci)
    zrow[4] = cr
    zrow[5] = ci

    each = rows_own // slot_count
    index = (
        ((stations[...] // each) ^ mine) * rows_own
        + stations[...] % each * slot_count
        + time_slots[...]
    ).astype(F32)
    index = jnp.concatenate([index, jnp.zeros((6, number), F32)], axis=0).T
    index = index.astype(jnp.int32)
    across = lax.broadcasted_iota(jnp.int32, (number, rows_all), 1)
    for which, coef in ((0, coef_first), (1, coef_second)):
        pick = (index[:, which : which + 1] == across).astype(F32).astype(BF16)
        coef[...] = dot(pick, table[...]).astype(BF16)

    for m in range(8):
        cols = slice(m * 128, (m + 1) * 128)
        b_re, b_im = basis[0, :, cols], basis[1, :, cols]
        weights[m, :terms, :128] = b_re
        weights[m, :terms, 128:] = b_im
        weights[m, terms:, :128] = -b_im
        weights[m, terms:, 128:] = b_re

    block = 64
    for m in range(8):
        @pl.loop(0, number // block)
        def _(n, m=m):
            rows = pl.ds(pl.multiple_of(n * block, block), block)
            first = dot(coef_first[rows, :], weights[m])
            second = dot(coef_second[rows, :], weights[m])
            f_re, f_im, s_re, s_im = first[:, :128], first[:, 128:], second[:, :128], second[:, 128:]
            g_re = f_re * s_re + f_im * s_im
            g_im = f_im * s_re - f_re * s_im
            i_re = image[m, rows, :128].astype(F32)
            i_im = image[m, rows, 128:].astype(F32)
            to = pl.ds(n * (block * 8) + m, block, stride=8)
            wre[to, :] = i_re * g_re - i_im * g_im
            wim[to, :] = i_re * g_im + i_im * g_re

    lane = lax.broadcasted_iota(jnp.int32, (8, 256), 1)
    inner = (lane // 32) % 4
    masks = [inner == j for j in range(4)]
    unroll = 4

    def one(g):
        at = pl.ds(pl.multiple_of(g * 8, 8), 8)
        w = jnp.concatenate([wre[at, :], wim[at, :]], axis=1)
        lhs = jnp.concatenate([jnp.where(k, w, 0.0) for k in masks], axis=0).astype(BF16)
        p_re, p_im = pure[at, :], puim[at, :]
        z = [jnp.broadcast_to(zrow[k, pl.ds(g, 1), :], (8, 128)) for k in range(6)]
        rr, ii, ri, ir = p_re * z[0], p_im * z[1], p_re * z[1], p_im * z[0]
        up_re, up_im = rr - ii, ri + ir
        dn_re, dn_im = rr + ii, ir - ri
        rr, ii, ri, ir = p_re * z[2], p_im * z[3], p_re * z[3], p_im * z[2]
        lo_re, lo_im = rr + ii, ir - ri
        c = jnp.concatenate([lo_re, dn_re, p_re, up_re], axis=0).astype(BF16)
        s = jnp.concatenate([lo_im, dn_im, p_im, up_im], axis=0).astype(BF16)
        top = jnp.concatenate([c, s], axis=1)
        low = jnp.concatenate([-s, c], axis=1)
        rhs = jnp.concatenate([top] * 4 + [low] * 4, axis=0)
        out = dot(lhs, rhs)
        h_re, h_im = out[24:32, :128], out[24:32, 128:]
        for j in (2, 1, 0):
            n_re = h_re * z[4] - h_im * z[5] + out[8 * j : 8 * j + 8, :128]
            h_im = h_re * z[5] + h_im * z[4] + out[8 * j : 8 * j + 8, 128:]
            h_re = n_re
        hre[at, :] = h_re
        him[at, :] = h_im

    @pl.loop(0, number // unroll)
    def _(n):
        for k in range(unroll):
            one(n * unroll + k)

    vr, vi = zv[0], zv[1]
    a_re = hre[pl.ds(7, number, stride=8), :]
    a_im = him[pl.ds(7, number, stride=8), :]
    for k in range(6, -1, -1):
        n_re = a_re * vr - a_im * vi + hre[pl.ds(k, number, stride=8), :]
        a_im = a_re * vi + a_im * vr + him[pl.ds(k, number, stride=8), :]
        a_re = n_re
    cr, ci = cmul(zrow[4], zrow[5], zrow[4], zrow[5])
    m_re, m_im = a_re * cr + a_im * ci, a_im * cr - a_re * ci
    models = jnp.concatenate([m_re, m_im], axis=1).astype(BF16)
    sent = dot(route[...], models, TN)
    interleaved[pl.ds(0, slots, stride=2), :] = sent[:, :128]
    interleaved[pl.ds(1, slots, stride=2), :] = sent[:, 128:]
    for r in range(tiles):
        rows = slice(2 * capacity * r, 2 * capacity * (r + 1))
        payload[r][...] = interleaved[rows, :].astype(BF16)


def residual_kernel(me, observed, *refs):
    arrived, residual = refs[:-1], refs[-1]
    for r in range(len(arrived)):
        source = me[0] ^ r
        residual[source] = observed[source] - arrived[r][...].astype(F32)


def exchange(value, step, tiles):
    return lax.ppermute(value, "tile", [(i, i ^ step) for i in range(tiles)])


def per_device(
    subgrids,
    stations,
    time_slots,
    assign,
    counts,
    beam_coefs,
    beam_basis,
    frequencies,
    uv_tracks,
    observed,
):
    tiles = lax.axis_size("tile")
    capacity = assign.shape[2]
    slots = tiles * capacity
    number = subgrids.shape[0]
    pixels = subgrids.shape[2]
    edge = math.isqrt(pixels)
    slot_count = beam_coefs.shape[1]
    terms2 = beam_coefs.shape[2]
    steps = uv_tracks.shape[4]
    chan = frequencies.shape[0]
    vis = steps * chan
    vmem = pl.BlockSpec(memory_space=pltpu.VMEM)
    params = pltpu.CompilerParams(vmem_limit_bytes=VMEM_LIMIT)

    smem = pl.BlockSpec(memory_space=pltpu.SMEM)
    me = lax.axis_index("tile").astype(jnp.int32).reshape(1)
    own_tracks = jnp.transpose(uv_tracks[0], (0, 2, 3, 1)).reshape(tiles, 2 * steps, capacity)
    own_rows = beam_coefs.shape[0] * slot_count
    outer = tiles // 4
    block = jax.ShapeDtypeStruct((own_rows + 8 * steps, terms2), BF16)
    packed = pl.pallas_call(
        pack_kernel,
        out_shape=[block] * outer,
        in_specs=[smem, vmem, vmem],
        out_specs=[vmem] * outer,
        compiler_params=params,
        name="pack",
    )(me, beam_coefs.reshape(own_rows, terms2), own_tracks)
    blocks = {0: packed[0]}
    for r in range(1, outer):
        blocks[4 * r] = exchange(packed[r], 4 * r, tiles)
    for r in range(outer):
        blocks[4 * r + 2] = exchange(blocks[4 * r], 2, tiles)
    for r in range(0, tiles, 2):
        blocks[r + 1] = exchange(blocks[r], 1, tiles)

    cells = jnp.transpose(subgrids.reshape(number, 2, 8, 128), (1, 2, 0, 3))
    high, rest = transform_matrices(edge)
    image = pl.pallas_call(
        transform_kernel,
        out_shape=jax.ShapeDtypeStruct((8, number, 256), BF16),
        in_specs=[vmem] * 3,
        out_specs=vmem,
        scratch_shapes=[
            pltpu.VMEM((8, number, 256), BF16),
            pltpu.VMEM((8, number, 256), BF16),
        ],
        compiler_params=params,
        name="transform",
    )(cells, jnp.asarray(high), jnp.asarray(rest))

    basis = jnp.transpose(
        beam_basis.reshape(2, terms2 // 2, 4, 8, edge), (0, 1, 3, 2, 4)
    ).reshape(2, terms2 // 2, pixels)
    payload = pl.pallas_call(
        functools.partial(predict_kernel, tiles=tiles, slot_count=slot_count),
        out_shape=[jax.ShapeDtypeStruct((2 * capacity, vis), BF16)] * tiles,
        in_specs=[smem] * 2 + [vmem] * (tiles + 6),
        out_specs=[vmem] * tiles,
        scratch_shapes=[
            pltpu.VMEM((tiles * own_rows, terms2), BF16),
            pltpu.VMEM((number, slots), BF16),
            pltpu.VMEM((8, 256, 256), BF16),
            pltpu.VMEM((number, terms2), BF16),
            pltpu.VMEM((number, terms2), BF16),
            pltpu.VMEM((number * 8, 128), F32),
            pltpu.VMEM((number * 8, 128), F32),
            pltpu.VMEM((number * 8, vis), F32),
            pltpu.VMEM((number * 8, vis), F32),
            pltpu.VMEM((6, number, vis), F32),
            pltpu.VMEM((number * 8, vis), F32),
            pltpu.VMEM((number * 8, vis), F32),
            pltpu.VMEM((2, number, vis), F32),
            pltpu.VMEM((2 * slots, vis), F32),
        ],
        compiler_params=params,
        name="predict",
    )(
        me,
        counts,
        *[blocks[r] for r in range(tiles)],
        assign[0],
        stations.T,
        time_slots.reshape(1, number),
        frequencies.reshape(1, chan),
        basis,
        image,
    )
    arrived = [payload[0]] + [exchange(payload[r], r, tiles) for r in range(1, tiles)]
    residual = pl.pallas_call(
        residual_kernel,
        out_shape=jax.ShapeDtypeStruct((tiles, 2 * capacity, vis), F32),
        in_specs=[smem] + [vmem] * (tiles + 1),
        out_specs=vmem,
        compiler_params=params,
        name="residual",
    )(me, observed.reshape(tiles, 2 * capacity, vis), *arrived)
    return residual.reshape(observed.shape)


def solution(mesh):
    return jax.shard_map(
        per_device,
        mesh=mesh,
        in_specs=(
            P(("grp", "tile"), None, None),
            P(("grp", "tile"), None),
            P(("grp", "tile")),
            P(("grp", "tile"), None, None),
            P(("grp", "tile"), None),
            P(("grp", "tile"), None, None),
            P(),
            P("grp"),
            P(("grp", "tile"), None, None, None, None),
            P(("grp", "tile"), None, None, None, None),
        ),
        out_specs=P(("grp", "tile"), None, None, None, None),
        check_vma=False,
    )
```

```python
import functools
import math

import jax
import jax.numpy as jnp
import ml_dtypes
import numpy as np
from jax import lax
from jax.experimental import pallas as pl
from jax.experimental.pallas import tpu as pltpu
from jax.sharding import PartitionSpec as P

TWO_PI = 2.0 * math.pi
F32 = jnp.float32
BF16 = jnp.bfloat16
VMEM_LIMIT = 36 * 1024 * 1024
NT = (((1,), (1,)), ((), ()))
TN = (((0,), (0,)), ((), ()))


def dot(a, b, dims=(((1,), (0,)), ((), ()))):
    return lax.dot_general(a, b, dims, preferred_element_type=F32)


def transform_matrices(edge):
    low = edge // 8
    b = np.arange(low)[:, None, None, None]
    a = np.arange(edge)[None, :, None, None]
    inner = np.arange(low)[None, None, :, None]
    x = np.arange(edge)[None, None, None, :]
    kept = []
    for outer in range(8):
        turns = (b * (outer + 8 * inner) + a * x) % edge
        angle = (TWO_PI / edge * turns).reshape(low * edge, low * edge)
        c, s = np.cos(angle) / edge**2, np.sin(angle) / edge**2
        kept.append(np.block([[c, s], [-s, c]]))
    full = np.stack(kept)
    high = full.astype(ml_dtypes.bfloat16)
    rest = (full - high.astype(np.float64)).astype(ml_dtypes.bfloat16)
    return high, rest


def eight_point(re, im):
    half = math.sqrt(0.5)

    def four(r, i):
        s0r, s0i, d0r, d0i = r[0] + r[2], i[0] + i[2], r[0] - r[2], i[0] - i[2]
        s1r, s1i, d1r, d1i = r[1] + r[3], i[1] + i[3], r[1] - r[3], i[1] - i[3]
        return (
            [s0r + s1r, d0r - d1i, s0r - s1r, d0r + d1i],
            [s0i + s1i, d0i + d1r, s0i - s1i, d0i - d1r],
        )

    er, ei = four(re[0::2], im[0::2])
    orr, oi = four(re[1::2], im[1::2])
    tr = [orr[0], half * (orr[1] - oi[1]), -oi[2], -half * (orr[3] + oi[3])]
    ti = [oi[0], half * (orr[1] + oi[1]), orr[2], half * (orr[3] - oi[3])]
    out_re = [er[m] + tr[m] for m in range(4)] + [er[m] - tr[m] for m in range(4)]
    out_im = [ei[m] + ti[m] for m in range(4)] + [ei[m] - ti[m] for m in range(4)]
    return out_re, out_im


def transform_kernel(cells, high, rest, image, wide, sums):
    number = image.shape[1]
    step = 16

    @pl.loop(0, number // step, unroll=2)
    def _(n):
        rows = pl.ds(pl.multiple_of(n * step, step), step)
        span = pl.ds(pl.multiple_of(n * step * 16, step * 16), step * 16)
        wide[span, :] = cells[span, :].astype(F32)
        re = [wide[pl.ds(n * step * 16 + 2 * k, step, stride=16), :] for k in range(8)]
        im = [wide[pl.ds(n * step * 16 + 2 * k + 1, step, stride=16), :] for k in range(8)]
        out_re, out_im = eight_point(re, im)
        for m in range(8):
            value = jnp.concatenate([out_re[m], out_im[m]], axis=1)
            top = value.astype(BF16)
            sums[m, rows, :256] = top
            sums[m, rows, 256:] = (value - top.astype(F32)).astype(BF16)

    for m in range(8):
        both = sums[m]
        left = jnp.concatenate([both, both[:, :256]], axis=1)
        right = jnp.concatenate([high[m], high[m], rest[m]], axis=0)
        image[m] = dot(left, right).astype(BF16)


def unit_powers(turns):
    turns = turns - jnp.round(turns)
    angle = (0.5 * math.pi) * turns
    sq = angle * angle
    s = angle * (
        1.0 + sq * (-1.0 / 6 + sq * (1.0 / 120 + sq * (-1.0 / 5040 + sq * (1.0 / 362880))))
    )
    c = 1.0 + sq * (
        -0.5 + sq * (1.0 / 24 + sq * (-1.0 / 720 + sq * (1.0 / 40320 - sq * (1.0 / 3628800))))
    )
    for _ in range(2):
        c, s = 1.0 - 2.0 * (s * s), 2.0 * (s * c)
    return c, s


def cmul(ar, ai, br, bi):
    return ar * br - ai * bi, ar * bi + ai * br


def pack_kernel(coefs, tracks, out):
    capacity = tracks.shape[2]
    rows = coefs.shape[0]
    for d in range(tracks.shape[0]):
        tr = tracks[d]
        t_hi = tr.astype(BF16).astype(F32)
        t_mid = (tr - t_hi).astype(BF16).astype(F32)
        t_lo = tr - t_hi - t_mid
        pieces = jnp.concatenate(
            [
                jnp.concatenate([t_hi, t_mid], axis=1),
                jnp.concatenate([t_lo, jnp.zeros_like(tr)], axis=1),
            ],
            axis=0,
        )
        if 2 * capacity < 128:
            blank = jnp.zeros((pieces.shape[0], 128 - 2 * capacity), F32)
            pieces = jnp.concatenate([pieces, blank], axis=1)
        out[d, :rows, :] = coefs[:, :128]
        out[d, rows : 2 * rows, :] = coefs[:, 128:]
        out[d, 2 * rows :, :] = pieces.astype(BF16)


def predict_kernel(
    counts,
    packed,
    assign,
    stations,
    time_slots,
    freq,
    basis,
    image,
    payload,
    table,
    route,
    weights,
    coef,
    wre,
    wim,
    pure,
    puim,
    zrow,
    hre,
    him,
    zv,
    interleaved,
    *,
    slot_count,
):
    number = image.shape[1]
    tiles, capacity = assign.shape
    slots = tiles * capacity
    rows_all = table.shape[0]
    rows_own = rows_all // tiles
    chan = freq.shape[1]
    kinds = (packed.shape[1] - 2 * rows_own) // 2
    steps = kinds // 2
    terms = basis.shape[1]

    per = 128 // capacity
    down = lax.broadcasted_iota(jnp.int32, (number, 128), 0)
    slot = lax.broadcasted_iota(jnp.int32, (1, capacity), 1)
    held = []
    for n in range(tiles // per):
        chosen, tracks = [], []
        for d in range(n * per, (n + 1) * per):
            chosen.append(jnp.where(slot < counts[0, d], assign[d : d + 1, :], -1))
            piece = packed[d, 2 * rows_own :, :].astype(F32)
            tracks.append(
                jnp.concatenate(
                    [
                        piece[:kinds, :capacity],
                        piece[:kinds, capacity : 2 * capacity],
                        piece[kinds:, :capacity],
                        jnp.zeros((kinds, capacity), F32),
                    ],
                    axis=0,
                )
            )
            at = slice(d * rows_own, (d + 1) * rows_own)
            table[at, :128] = packed[d, :rows_own, :]
            table[at, 128:] = packed[d, rows_own : 2 * rows_own, :]
        chosen = jnp.concatenate(chosen, axis=1)
        route[:, n * 128 : (n + 1) * 128] = (chosen == down).astype(F32).astype(BF16)
        held.append(jnp.concatenate(tracks, axis=1).astype(BF16))
    pieces = jnp.concatenate(held, axis=1)

    per_sub = dot(route[...], pieces, NT).astype(BF16)
    wide = 2 * steps * chan
    from_row = lax.broadcasted_iota(jnp.int32, (4 * kinds, wide), 0) % kinds
    to_lane = lax.broadcasted_iota(jnp.int32, (4 * kinds, wide), 1) // chan
    spread = (from_row == to_lane).astype(F32).astype(BF16)
    uv = dot(per_sub, spread)
    vis = steps * chan
    fr = jnp.concatenate([freq[...]] * steps, axis=1)
    scale = -1.0 / 32.0
    ur, ui = unit_powers(uv[:, :vis] * fr * scale)
    vr, vi = unit_powers(uv[:, vis:] * fr * scale)

    pure[pl.ds(0, number, stride=8), :] = jnp.ones_like(ur)
    puim[pl.ds(0, number, stride=8), :] = jnp.zeros_like(ur)
    pure[pl.ds(1, number, stride=8), :] = ur
    puim[pl.ds(1, number, stride=8), :] = ui
    cr, ci = ur, ui
    for k in range(2, 8):
        cr, ci = cmul(cr, ci, ur, ui)
        pure[pl.ds(k, number, stride=8), :] = cr
        puim[pl.ds(k, number, stride=8), :] = ci
    cr, ci = cmul(cr, ci, ur, ui)
    zrow[0] = cr
    zrow[1] = ci
    cr, ci = cmul(cr, ci, cr, ci)
    zrow[2] = cr
    zrow[3] = ci
    zv[0] = vr
    zv[1] = vi
    cr, ci = vr, vi
    for _ in range(3):
        cr, ci = cmul(cr, ci, cr, ci)
    zrow[4] = cr
    zrow[5] = ci

    index = (stations[...] * slot_count + time_slots[...]).astype(F32)
    index = jnp.concatenate([index, jnp.zeros((6, number), F32)], axis=0).T
    index = index.astype(jnp.int32)
    across = lax.broadcasted_iota(jnp.int32, (number, rows_all), 1)
    for which in range(2):
        pick = (index[:, which : which + 1] == across).astype(F32).astype(BF16)
        coef[which * number : (which + 1) * number, :] = dot(pick, table[...]).astype(BF16)

    for m in range(8):
        cols = slice(m * 128, (m + 1) * 128)
        b_re, b_im = basis[0, :, cols], basis[1, :, cols]
        weights[m, :terms, :128] = b_re
        weights[m, :terms, 128:] = b_im
        weights[m, terms:, :128] = -b_im
        weights[m, terms:, 128:] = b_re

    block = 32
    for m in range(8):
        beams = dot(coef[...], weights[m])
        for n in range(0, number, block):
            first = beams[n : n + block, :]
            second = beams[number + n : number + n + block, :]
            f_re, f_im, s_re, s_im = first[:, :128], first[:, 128:], second[:, :128], second[:, 128:]
            g_re = f_re * s_re + f_im * s_im
            g_im = f_im * s_re - f_re * s_im
            i_re = image[m, n : n + block, :128].astype(F32)
            i_im = image[m, n : n + block, 128:].astype(F32)
            to = pl.ds(n * 8 + m, block, stride=8)
            wre[to, :] = i_re * g_re - i_im * g_im
            wim[to, :] = i_re * g_im + i_im * g_re

    lane = lax.broadcasted_iota(jnp.int32, (8, 256), 1)
    inner = (lane // 32) % 4
    masks = [inner == j for j in range(4)]
    unroll = 16

    def one(g):
        at = pl.ds(pl.multiple_of(g * 8, 8), 8)
        w = jnp.concatenate([wre[at, :], wim[at, :]], axis=1)
        lhs = jnp.concatenate([jnp.where(k, w, 0.0) for k in masks], axis=0).astype(BF16)
        p_re, p_im = pure[at, :], puim[at, :]
        z = [jnp.broadcast_to(zrow[k, pl.ds(g, 1), :], (8, 128)) for k in range(6)]
        rr, ii, ri, ir = p_re * z[0], p_im * z[1], p_re * z[1], p_im * z[0]
        up_re, up_im = rr - ii, ri + ir
        dn_re, dn_im = rr + ii, ir - ri
        rr, ii, ri, ir = p_re * z[2], p_im * z[3], p_re * z[3], p_im * z[2]
        lo_re, lo_im = rr + ii, ir - ri
        c = jnp.concatenate([lo_re, dn_re, p_re, up_re], axis=0).astype(BF16)
        s = jnp.concatenate([lo_im, dn_im, p_im, up_im], axis=0).astype(BF16)
        top = jnp.concatenate([c, s], axis=1)
        low = jnp.concatenate([-s, c], axis=1)
        rhs = jnp.concatenate([top] * 4 + [low] * 4, axis=0)
        out = dot(lhs, rhs)
        h_re, h_im = out[24:32, :128], out[24:32, 128:]
        for j in (2, 1, 0):
            n_re = h_re * z[4] - h_im * z[5] + out[8 * j : 8 * j + 8, :128]
            h_im = h_re * z[5] + h_im * z[4] + out[8 * j : 8 * j + 8, 128:]
            h_re = n_re
        hre[at, :] = h_re
        him[at, :] = h_im

    @pl.loop(0, number // unroll)
    def _(n):
        for k in range(unroll):
            one(n * unroll + k)

    vr, vi = zv[0], zv[1]
    a_re = hre[pl.ds(7, number, stride=8), :]
    a_im = him[pl.ds(7, number, stride=8), :]
    for k in range(6, -1, -1):
        n_re = a_re * vr - a_im * vi + hre[pl.ds(k, number, stride=8), :]
        a_im = a_re * vi + a_im * vr + him[pl.ds(k, number, stride=8), :]
        a_re = n_re
    cr, ci = cmul(zrow[4], zrow[5], zrow[4], zrow[5])
    m_re, m_im = a_re * cr + a_im * ci, a_im * cr - a_re * ci
    models = jnp.concatenate([m_re, m_im], axis=1).astype(BF16)
    sent = dot(route[...], models, TN)
    interleaved[pl.ds(0, slots, stride=2), :] = sent[:, :128]
    interleaved[pl.ds(1, slots, stride=2), :] = sent[:, 128:]
    payload[...] = interleaved[...].astype(BF16)


def per_device(
    subgrids,
    stations,
    time_slots,
    assign,
    counts,
    beam_coefs,
    beam_basis,
    frequencies,
    uv_tracks,
    observed,
):
    tiles = lax.axis_size("tile")
    capacity = assign.shape[2]
    slots = tiles * capacity
    number = subgrids.shape[0]
    pixels = subgrids.shape[2]
    edge = math.isqrt(pixels)
    slot_count = beam_coefs.shape[1]
    terms2 = beam_coefs.shape[2]
    steps = uv_tracks.shape[4]
    chan = frequencies.shape[0]
    vis = steps * chan
    vmem = pl.BlockSpec(memory_space=pltpu.VMEM)
    own_tracks = jnp.transpose(uv_tracks[0], (0, 2, 3, 1)).reshape(tiles, 2 * steps, capacity)
    own_rows = beam_coefs.shape[0] * slot_count
    packed = pl.pallas_call(
        pack_kernel,
        out_shape=jax.ShapeDtypeStruct((tiles, 2 * own_rows + 4 * steps, 128), BF16),
        in_specs=[vmem, vmem],
        out_specs=vmem,
        name="pack",
    )(beam_coefs.reshape(own_rows, terms2), own_tracks)
    packed = lax.all_to_all(packed, "tile", split_axis=0, concat_axis=0, tiled=True)

    cells = jnp.transpose(subgrids.reshape(number, 2, 8, 128), (0, 2, 1, 3))
    cells = cells.reshape(number * 16, 128)
    high, rest = transform_matrices(edge)
    image = pl.pallas_call(
        transform_kernel,
        out_shape=jax.ShapeDtypeStruct((8, number, 256), BF16),
        in_specs=[vmem] * 3,
        out_specs=vmem,
        scratch_shapes=[
            pltpu.VMEM((number * 16, 128), F32),
            pltpu.VMEM((8, number, 512), BF16),
        ],
        compiler_params=pltpu.CompilerParams(vmem_limit_bytes=20 * 1024 * 1024),
        name="transform",
    )(cells, jnp.asarray(high), jnp.asarray(rest))

    basis = jnp.transpose(
        beam_basis.reshape(2, terms2 // 2, 4, 8, edge), (0, 1, 3, 2, 4)
    ).reshape(2, terms2 // 2, pixels)
    smem = pl.BlockSpec(memory_space=pltpu.SMEM)
    payload = pl.pallas_call(
        functools.partial(predict_kernel, slot_count=slot_count),
        out_shape=jax.ShapeDtypeStruct((2 * slots, vis), BF16),
        in_specs=[smem] + [vmem] * 7,
        out_specs=vmem,
        scratch_shapes=[
            pltpu.VMEM((tiles * own_rows, terms2), BF16),
            pltpu.VMEM((number, slots), BF16),
            pltpu.VMEM((8, 256, 256), BF16),
            pltpu.VMEM((2 * number, terms2), BF16),
            pltpu.VMEM((number * 8, 128), F32),
            pltpu.VMEM((number * 8, 128), F32),
            pltpu.VMEM((number * 8, vis), F32),
            pltpu.VMEM((number * 8, vis), F32),
            pltpu.VMEM((6, number, vis), F32),
            pltpu.VMEM((number * 8, vis), F32),
            pltpu.VMEM((number * 8, vis), F32),
            pltpu.VMEM((2, number, vis), F32),
            pltpu.VMEM((2 * slots, vis), F32),
        ],
        compiler_params=pltpu.CompilerParams(vmem_limit_bytes=VMEM_LIMIT),
        name="predict",
    )(
        counts,
        packed,
        assign[0],
        stations.T,
        time_slots.reshape(1, number),
        frequencies.reshape(1, chan),
        basis,
        image,
    )
    arrived = lax.all_to_all(
        payload.reshape(tiles, 2 * capacity, vis), "tile", split_axis=0, concat_axis=0, tiled=True
    )
    return observed - arrived.reshape(observed.shape).astype(F32)


def solution(mesh):
    return jax.shard_map(
        per_device,
        mesh=mesh,
        in_specs=(
            P(("grp", "tile"), None, None),
            P(("grp", "tile"), None),
            P(("grp", "tile")),
            P(("grp", "tile"), None, None),
            P(("grp", "tile"), None),
            P(("grp", "tile"), None, None),
            P(),
            P("grp"),
            P(("grp", "tile"), None, None, None, None),
            P(("grp", "tile"), None, None, None, None),
        ),
        out_specs=P(("grp", "tile"), None, None, None, None),
        check_vma=False,
    )
```

```python
import functools
import math

import jax
import jax.numpy as jnp
import ml_dtypes
import numpy as np
from jax import lax
from jax.experimental import pallas as pl
from jax.experimental.pallas import tpu as pltpu
from jax.sharding import PartitionSpec as P

TWO_PI = 2.0 * math.pi
F32 = jnp.float32
BF16 = jnp.bfloat16
VMEM_LIMIT = 36 * 1024 * 1024
NT = (((1,), (1,)), ((), ()))


def dot(a, b, dims=(((1,), (0,)), ((), ()))):
    return lax.dot_general(a, b, dims, preferred_element_type=F32)


def transform_matrices(edge):
    low = edge // 8
    b = np.arange(low)[:, None, None, None]
    a = np.arange(edge)[None, :, None, None]
    inner = np.arange(low)[None, None, :, None]
    x = np.arange(edge)[None, None, None, :]
    kept = []
    for outer in range(8):
        turns = (b * (outer + 8 * inner) + a * x) % edge
        angle = (TWO_PI / edge * turns).reshape(low * edge, low * edge)
        c, s = np.cos(angle) / edge**2, np.sin(angle) / edge**2
        kept.append(np.block([[c, s], [-s, c]]))
    full = np.stack(kept)
    high = full.astype(ml_dtypes.bfloat16)
    rest = (full - high.astype(np.float64)).astype(ml_dtypes.bfloat16)
    return high, rest


def eight_point(re, im):
    half = math.sqrt(0.5)

    def four(r, i):
        s0r, s0i, d0r, d0i = r[0] + r[2], i[0] + i[2], r[0] - r[2], i[0] - i[2]
        s1r, s1i, d1r, d1i = r[1] + r[3], i[1] + i[3], r[1] - r[3], i[1] - i[3]
        return (
            [s0r + s1r, d0r - d1i, s0r - s1r, d0r + d1i],
            [s0i + s1i, d0i + d1r, s0i - s1i, d0i - d1r],
        )

    er, ei = four(re[0::2], im[0::2])
    orr, oi = four(re[1::2], im[1::2])
    tr = [orr[0], half * (orr[1] - oi[1]), -oi[2], -half * (orr[3] + oi[3])]
    ti = [oi[0], half * (orr[1] + oi[1]), orr[2], half * (orr[3] - oi[3])]
    out_re = [er[m] + tr[m] for m in range(4)] + [er[m] - tr[m] for m in range(4)]
    out_im = [ei[m] + ti[m] for m in range(4)] + [ei[m] - ti[m] for m in range(4)]
    return out_re, out_im


def prepare_kernel(
    counts, cells, high, rest, assign, stations, time_slots, basis, image, route, back, pick, weights, wide, sums, *, slot_count
):
    number = image.shape[1]
    tiles, capacity = assign.shape
    step = 16

    @pl.loop(0, number // step, unroll=2)
    def _(n):
        rows = pl.ds(pl.multiple_of(n * step, step), step)
        span = pl.ds(pl.multiple_of(n * step * 16, step * 16), step * 16)
        wide[span, :] = cells[span, :].astype(F32)
        re = [wide[pl.ds(n * step * 16 + 2 * k, step, stride=16), :] for k in range(8)]
        im = [wide[pl.ds(n * step * 16 + 2 * k + 1, step, stride=16), :] for k in range(8)]
        out_re, out_im = eight_point(re, im)
        for m in range(8):
            value = jnp.concatenate([out_re[m], out_im[m]], axis=1)
            top = value.astype(BF16)
            sums[m, rows, :256] = top
            sums[m, rows, 256:] = (value - top.astype(F32)).astype(BF16)

    for m in range(8):
        both = sums[m]
        left = jnp.concatenate([both, both[:, :256]], axis=1)
        right = jnp.concatenate([high[m], high[m], rest[m]], axis=0)
        image[m] = dot(left, right).astype(BF16)

    per = 128 // capacity
    down = lax.broadcasted_iota(jnp.int32, (number, 128), 0)
    slot = lax.broadcasted_iota(jnp.int32, (1, capacity), 1)
    for n in range(tiles // per):
        chosen = [
            jnp.where(slot < counts[0, d], assign[d : d + 1, :], -1)
            for d in range(n * per, (n + 1) * per)
        ]
        hot = (jnp.concatenate(chosen, axis=1) == down).astype(F32)
        route[:, n * 128 : (n + 1) * 128] = hot.astype(BF16)
        back[n * 128 : (n + 1) * 128, :] = hot.T.astype(BF16)

    index = (stations[...] * slot_count + time_slots[...]).astype(F32)
    index = jnp.concatenate([index, jnp.zeros((6, number), F32)], axis=0).T
    index = index.astype(jnp.int32)
    across = lax.broadcasted_iota(jnp.int32, (number, pick.shape[1]), 1)
    for which in range(2):
        hot = (index[:, which : which + 1] == across).astype(F32)
        pick[which * number : (which + 1) * number, :] = hot.astype(BF16)

    terms = basis.shape[1]
    for m in range(8):
        cols = slice(m * 128, (m + 1) * 128)
        b_re, b_im = basis[0, :, cols], basis[1, :, cols]
        weights[m, :terms, :128] = b_re
        weights[m, :terms, 128:] = b_im
        weights[m, terms:, :128] = -b_im
        weights[m, terms:, 128:] = b_re


def unit_powers(turns):
    turns = turns - jnp.round(turns)
    angle = (0.5 * math.pi) * turns
    sq = angle * angle
    s = angle * (
        1.0 + sq * (-1.0 / 6 + sq * (1.0 / 120 + sq * (-1.0 / 5040 + sq * (1.0 / 362880))))
    )
    c = 1.0 + sq * (
        -0.5 + sq * (1.0 / 24 + sq * (-1.0 / 720 + sq * (1.0 / 40320 - sq * (1.0 / 3628800))))
    )
    for _ in range(2):
        c, s = 1.0 - 2.0 * (s * s), 2.0 * (s * c)
    return c, s


def cmul(ar, ai, br, bi):
    return ar * br - ai * bi, ar * bi + ai * br


def pack_kernel(me, coefs, tracks, *out):
    capacity = tracks.shape[2]
    rows = coefs.shape[0]
    for r in range(len(out)):
        plane = (me[0] // 4) ^ r
        kept = []
        for k in (0, 2):
            tr = jnp.concatenate([tracks[plane * 4 + k], tracks[plane * 4 + k + 1]], axis=1)
            t_hi = tr.astype(BF16).astype(F32)
            t_mid = (tr - t_hi).astype(BF16).astype(F32)
            kept += [t_hi, t_mid, tr - t_hi - t_mid]
        pieces = jnp.concatenate(kept, axis=0)
        if 2 * capacity < 128:
            blank = jnp.zeros((pieces.shape[0], 128 - 2 * capacity), F32)
            pieces = jnp.concatenate([pieces, blank], axis=1)
        out[r][:rows, :] = coefs[:, :128]
        out[r][rows : 2 * rows, :] = coefs[:, 128:]
        out[r][2 * rows :, :] = pieces.astype(BF16)


def stack_kernel(*refs):
    blocks, out = refs[:-2], refs[-1]
    for r, block in enumerate(blocks):
        out[r] = block[...]


def predict_kernel(
    me,
    near,
    over_y,
    over_core,
    over_both,
    route,
    back,
    pick,
    weights,
    freq,
    image,
    payload,
    table,
    lanes,
    coef,
    wre,
    wim,
    pure,
    puim,
    zrow,
    hre,
    him,
    zv,
    interleaved,
):
    number = image.shape[1]
    tiles, kinds3, capacity = lanes.shape
    slots = tiles * capacity
    rows_own = table.shape[0] // tiles
    chan = freq.shape[1]
    kinds = kinds3 // 3
    steps = kinds // 2
    mine = me[0]

    for arrived, flip in ((near, 0), (over_y, 2), (over_core, 1), (over_both, 3)):
        for r in range(arrived.shape[0]):
            owner = mine ^ (4 * r + flip)
            at = pl.ds(pl.multiple_of(owner * rows_own, rows_own), rows_own)
            table[at, :128] = arrived[r, :rows_own, :]
            table[at, 128:] = arrived[r, rows_own : 2 * rows_own, :]
            piece = arrived[r, 2 * rows_own :, :].astype(F32)
            piece = jnp.where(mine & 2 == 0, piece[:kinds3, :], piece[kinds3:, :])
            moved = jnp.where(mine & 1 == 0, piece, pltpu.roll(piece, 128 - capacity, 1))
            lanes[owner] = moved[:, :capacity]
    per = 128 // capacity
    pieces = jnp.concatenate(
        [
            jnp.concatenate([lanes[d] for d in range(n * per, (n + 1) * per)], axis=1)
            for n in range(tiles // per)
        ],
        axis=1,
    )
    pieces = jnp.concatenate([pieces, jnp.zeros((kinds, slots), F32)], axis=0).astype(BF16)

    per_sub = dot(route[...], pieces, NT).astype(BF16)
    wide = 2 * steps * chan
    from_row = lax.broadcasted_iota(jnp.int32, (4 * kinds, wide), 0) % kinds
    to_lane = lax.broadcasted_iota(jnp.int32, (4 * kinds, wide), 1) // chan
    spread = (from_row == to_lane).astype(F32).astype(BF16)
    uv = dot(per_sub, spread)
    vis = steps * chan
    fr = jnp.concatenate([freq[...]] * steps, axis=1)
    scale = -1.0 / 32.0
    ur, ui = unit_powers(uv[:, :vis] * fr * scale)
    vr, vi = unit_powers(uv[:, vis:] * fr * scale)

    pure[pl.ds(0, number, stride=8), :] = jnp.ones_like(ur)
    puim[pl.ds(0, number, stride=8), :] = jnp.zeros_like(ur)
    pure[pl.ds(1, number, stride=8), :] = ur
    puim[pl.ds(1, number, stride=8), :] = ui
    cr, ci = ur, ui
    for k in range(2, 8):
        cr, ci = cmul(cr, ci, ur, ui)
        pure[pl.ds(k, number, stride=8), :] = cr
        puim[pl.ds(k, number, stride=8), :] = ci
    cr, ci = cmul(cr, ci, ur, ui)
    zrow[0] = cr
    zrow[1] = ci
    cr, ci = cmul(cr, ci, cr, ci)
    zrow[2] = cr
    zrow[3] = ci
    zv[0] = vr
    zv[1] = vi
    cr, ci = vr, vi
    for _ in range(3):
        cr, ci = cmul(cr, ci, cr, ci)
    zrow[4] = cr
    zrow[5] = ci

    coef[...] = dot(pick[...], table[...]).astype(BF16)

    block = 32
    for m in range(8):
        beams = dot(coef[...], weights[m])
        for n in range(0, number, block):
            first = beams[n : n + block, :]
            second = beams[number + n : number + n + block, :]
            f_re, f_im, s_re, s_im = first[:, :128], first[:, 128:], second[:, :128], second[:, 128:]
            g_re = f_re * s_re + f_im * s_im
            g_im = f_im * s_re - f_re * s_im
            i_re = image[m, n : n + block, :128].astype(F32)
            i_im = image[m, n : n + block, 128:].astype(F32)
            to = pl.ds(n * 8 + m, block, stride=8)
            wre[to, :] = i_re * g_re - i_im * g_im
            wim[to, :] = i_re * g_im + i_im * g_re

    lane = lax.broadcasted_iota(jnp.int32, (8, 256), 1)
    inner = (lane // 32) % 4
    masks = [inner == j for j in range(4)]
    unroll = 16

    def one(g):
        at = pl.ds(pl.multiple_of(g * 8, 8), 8)
        w = jnp.concatenate([wre[at, :], wim[at, :]], axis=1)
        lhs = jnp.concatenate([jnp.where(k, w, 0.0) for k in masks], axis=0).astype(BF16)
        p_re, p_im = pure[at, :], puim[at, :]
        z = [jnp.broadcast_to(zrow[k, pl.ds(g, 1), :], (8, 128)) for k in range(6)]
        rr, ii, ri, ir = p_re * z[0], p_im * z[1], p_re * z[1], p_im * z[0]
        up_re, up_im = rr - ii, ri + ir
        dn_re, dn_im = rr + ii, ir - ri
        rr, ii, ri, ir = p_re * z[2], p_im * z[3], p_re * z[3], p_im * z[2]
        lo_re, lo_im = rr + ii, ir - ri
        c = jnp.concatenate([lo_re, dn_re, p_re, up_re], axis=0).astype(BF16)
        s = jnp.concatenate([lo_im, dn_im, p_im, up_im], axis=0).astype(BF16)
        top = jnp.concatenate([c, s], axis=1)
        low = jnp.concatenate([-s, c], axis=1)
        rhs = jnp.concatenate([top] * 4 + [low] * 4, axis=0)
        out = dot(lhs, rhs)
        h_re, h_im = out[24:32, :128], out[24:32, 128:]
        for j in (2, 1, 0):
            n_re = h_re * z[4] - h_im * z[5] + out[8 * j : 8 * j + 8, :128]
            h_im = h_re * z[5] + h_im * z[4] + out[8 * j : 8 * j + 8, 128:]
            h_re = n_re
        hre[at, :] = h_re
        him[at, :] = h_im

    @pl.loop(0, number // unroll)
    def _(n):
        for k in range(unroll):
            one(n * unroll + k)

    vr, vi = zv[0], zv[1]
    a_re = hre[pl.ds(7, number, stride=8), :]
    a_im = him[pl.ds(7, number, stride=8), :]
    for k in range(6, -1, -1):
        n_re = a_re * vr - a_im * vi + hre[pl.ds(k, number, stride=8), :]
        a_im = a_re * vi + a_im * vr + him[pl.ds(k, number, stride=8), :]
        a_re = n_re
    cr, ci = cmul(zrow[4], zrow[5], zrow[4], zrow[5])
    m_re, m_im = a_re * cr + a_im * ci, a_im * cr - a_re * ci
    models = jnp.concatenate([m_re, m_im], axis=1).astype(BF16)
    sent = dot(back[...], models)
    interleaved[pl.ds(0, slots, stride=2), :] = sent[:, :128]
    interleaved[pl.ds(1, slots, stride=2), :] = sent[:, 128:]
    payload[...] = interleaved[...].astype(BF16)


def exchange(value, step, tiles):
    return lax.ppermute(value, "tile", [(i, i ^ step) for i in range(tiles)])


def per_device(
    subgrids,
    stations,
    time_slots,
    assign,
    counts,
    beam_coefs,
    beam_basis,
    frequencies,
    uv_tracks,
    observed,
):
    tiles = lax.axis_size("tile")
    capacity = assign.shape[2]
    slots = tiles * capacity
    number = subgrids.shape[0]
    pixels = subgrids.shape[2]
    edge = math.isqrt(pixels)
    slot_count = beam_coefs.shape[1]
    terms2 = beam_coefs.shape[2]
    steps = uv_tracks.shape[4]
    chan = frequencies.shape[0]
    vis = steps * chan
    vmem = pl.BlockSpec(memory_space=pltpu.VMEM)
    own_tracks = jnp.transpose(uv_tracks[0], (0, 2, 3, 1)).reshape(tiles, 2 * steps, capacity)
    own_rows = beam_coefs.shape[0] * slot_count
    smem = pl.BlockSpec(memory_space=pltpu.SMEM)
    anywhere = pl.BlockSpec(memory_space=pl.ANY)
    outer = tiles // 4
    me = lax.axis_index("tile").astype(jnp.int32).reshape(1)
    block = jax.ShapeDtypeStruct((2 * own_rows + 12 * steps, 128), BF16)
    packed = pl.pallas_call(
        pack_kernel,
        out_shape=[block] * outer,
        in_specs=[smem, vmem, vmem],
        out_specs=[vmem] * outer,
        name="pack",
    )(me, beam_coefs.reshape(own_rows, terms2), own_tracks)
    along = [packed[0]] + [exchange(packed[r], 4 * r, tiles) for r in range(1, outer)]

    cells = jnp.transpose(subgrids.reshape(number, 2, 8, 128), (0, 2, 1, 3))
    cells = cells.reshape(number * 16, 128)
    basis = jnp.transpose(
        beam_basis.reshape(2, terms2 // 2, 4, 8, edge), (0, 1, 3, 2, 4)
    ).reshape(2, terms2 // 2, pixels)
    high, rest = transform_matrices(edge)
    image, route, back, pick, weights = pl.pallas_call(
        functools.partial(prepare_kernel, slot_count=slot_count),
        out_shape=[
            jax.ShapeDtypeStruct((8, number, 256), BF16),
            jax.ShapeDtypeStruct((number, slots), BF16),
            jax.ShapeDtypeStruct((slots, number), BF16),
            jax.ShapeDtypeStruct((2 * number, tiles * own_rows), BF16),
            jax.ShapeDtypeStruct((8, terms2, 256), BF16),
        ],
        in_specs=[smem] + [vmem] * 7,
        out_specs=[vmem] * 5,
        scratch_shapes=[
            pltpu.VMEM((number * 16, 128), F32),
            pltpu.VMEM((8, number, 512), BF16),
        ],
        compiler_params=pltpu.CompilerParams(vmem_limit_bytes=24 * 1024 * 1024),
        name="prepare",
    )(
        counts,
        cells,
        jnp.asarray(high),
        jnp.asarray(rest),
        assign[0],
        stations.T,
        time_slots.reshape(1, number),
        basis,
    )

    near = pl.pallas_call(
        stack_kernel,
        out_shape=jax.ShapeDtypeStruct((outer,) + block.shape, BF16),
        in_specs=[vmem] * outer + [anywhere],
        out_specs=vmem,
        name="stack",
    )(*along, image)
    over_y = exchange(near, 2, tiles)
    over_core = exchange(near, 1, tiles)
    over_both = exchange(over_y, 1, tiles)

    payload = pl.pallas_call(
        predict_kernel,
        out_shape=jax.ShapeDtypeStruct((2 * slots, vis), BF16),
        in_specs=[smem] + [vmem] * 10,
        out_specs=vmem,
        scratch_shapes=[
            pltpu.VMEM((tiles * own_rows, terms2), BF16),
            pltpu.VMEM((tiles, 6 * steps, capacity), F32),
            pltpu.VMEM((2 * number, terms2), BF16),
            pltpu.VMEM((number * 8, 128), F32),
            pltpu.VMEM((number * 8, 128), F32),
            pltpu.VMEM((number * 8, vis), F32),
            pltpu.VMEM((number * 8, vis), F32),
            pltpu.VMEM((6, number, vis), F32),
            pltpu.VMEM((number * 8, vis), F32),
            pltpu.VMEM((number * 8, vis), F32),
            pltpu.VMEM((2, number, vis), F32),
            pltpu.VMEM((2 * slots, vis), F32),
        ],
        compiler_params=pltpu.CompilerParams(vmem_limit_bytes=VMEM_LIMIT),
        name="predict",
    )(
        me,
        near,
        over_y,
        over_core,
        over_both,
        route,
        back,
        pick,
        weights,
        frequencies.reshape(1, chan),
        image,
    )
    arrived = lax.all_to_all(
        payload.reshape(tiles, 2 * capacity, vis), "tile", split_axis=0, concat_axis=0, tiled=True
    )
    return observed - arrived.reshape(observed.shape).astype(F32)


def solution(mesh):
    return jax.shard_map(
        per_device,
        mesh=mesh,
        in_specs=(
            P(("grp", "tile"), None, None),
            P(("grp", "tile"), None),
            P(("grp", "tile")),
            P(("grp", "tile"), None, None),
            P(("grp", "tile"), None),
            P(("grp", "tile"), None, None),
            P(),
            P("grp"),
            P(("grp", "tile"), None, None, None, None),
            P(("grp", "tile"), None, None, None, None),
        ),
        out_specs=P(("grp", "tile"), None, None, None, None),
        check_vma=False,
    )
```

```python
import functools
import math

import jax
import jax.numpy as jnp
import ml_dtypes
import numpy as np
from jax import lax
from jax.experimental import pallas as pl
from jax.experimental.pallas import tpu as pltpu
from jax.sharding import PartitionSpec as P

TWO_PI = 2.0 * math.pi
F32 = jnp.float32
BF16 = jnp.bfloat16
MIB = 1024 * 1024
NT = (((1,), (1,)), ((), ()))


def dot(a, b, dims=(((1,), (0,)), ((), ()))):
    return lax.dot_general(a, b, dims, preferred_element_type=F32)


def transform_matrices(edge):
    low = edge // 8
    b = np.arange(low)[:, None, None, None]
    a = np.arange(edge)[None, :, None, None]
    inner = np.arange(low)[None, None, :, None]
    x = np.arange(edge)[None, None, None, :]
    kept = []
    for outer in range(8):
        turns = (b * (outer + 8 * inner) + a * x) % edge
        angle = (TWO_PI / edge * turns).reshape(low * edge, low * edge)
        c, s = np.cos(angle) / edge**2, np.sin(angle) / edge**2
        kept.append(np.block([[c, s], [-s, c]]))
    full = np.stack(kept)
    high = full.astype(ml_dtypes.bfloat16)
    rest = (full - high.astype(np.float64)).astype(ml_dtypes.bfloat16)
    return high, rest


def eight_point(re, im):
    half = math.sqrt(0.5)

    def four(r, i):
        s0r, s0i, d0r, d0i = r[0] + r[2], i[0] + i[2], r[0] - r[2], i[0] - i[2]
        s1r, s1i, d1r, d1i = r[1] + r[3], i[1] + i[3], r[1] - r[3], i[1] - i[3]
        return (
            [s0r + s1r, d0r - d1i, s0r - s1r, d0r + d1i],
            [s0i + s1i, d0i + d1r, s0i - s1i, d0i - d1r],
        )

    er, ei = four(re[0::2], im[0::2])
    orr, oi = four(re[1::2], im[1::2])
    tr = [orr[0], half * (orr[1] - oi[1]), -oi[2], -half * (orr[3] + oi[3])]
    ti = [oi[0], half * (orr[1] + oi[1]), orr[2], half * (orr[3] - oi[3])]
    out_re = [er[m] + tr[m] for m in range(4)] + [er[m] - tr[m] for m in range(4)]
    out_im = [ei[m] + ti[m] for m in range(4)] + [ei[m] - ti[m] for m in range(4)]
    return out_re, out_im


def prepare_kernel(
    counts, cells, high, rest, assign, stations, time_slots, basis, image, route, back, pick, weights, wide, sums, *, slot_count
):
    number = image.shape[1]
    tiles, capacity = assign.shape
    step = 16

    @pl.loop(0, number // step, unroll=2)
    def _(n):
        rows = pl.ds(pl.multiple_of(n * step, step), step)
        span = pl.ds(pl.multiple_of(n * step * 16, step * 16), step * 16)
        wide[span, :] = cells[span, :].astype(F32)
        re = [wide[pl.ds(n * step * 16 + 2 * k, step, stride=16), :] for k in range(8)]
        im = [wide[pl.ds(n * step * 16 + 2 * k + 1, step, stride=16), :] for k in range(8)]
        out_re, out_im = eight_point(re, im)
        for m in range(8):
            value = jnp.concatenate([out_re[m], out_im[m]], axis=1)
            top = value.astype(BF16)
            sums[m, rows, :256] = top
            sums[m, rows, 256:] = (value - top.astype(F32)).astype(BF16)

    for m in range(8):
        both = sums[m]
        left = jnp.concatenate([both, both[:, :256]], axis=1)
        right = jnp.concatenate([high[m], high[m], rest[m]], axis=0)
        image[m] = dot(left, right).astype(BF16)

    per = 128 // capacity
    down = lax.broadcasted_iota(jnp.int32, (number, 128), 0)
    slot = lax.broadcasted_iota(jnp.int32, (1, capacity), 1)
    for n in range(tiles // per):
        chosen = [
            jnp.where(slot < counts[0, d], assign[d : d + 1, :], -1)
            for d in range(n * per, (n + 1) * per)
        ]
        hot = (jnp.concatenate(chosen, axis=1) == down).astype(F32)
        route[:, n * 128 : (n + 1) * 128] = hot.astype(BF16)
        back[n * 128 : (n + 1) * 128, :] = hot.T.astype(BF16)

    index = (stations[...] * slot_count + time_slots[...]).astype(F32)
    index = jnp.concatenate([index, jnp.zeros((6, number), F32)], axis=0).T
    index = index.astype(jnp.int32)
    across = lax.broadcasted_iota(jnp.int32, (number, pick.shape[1]), 1)
    for which in range(2):
        hot = (index[:, which : which + 1] == across).astype(F32)
        pick[which * number : (which + 1) * number, :] = hot.astype(BF16)

    terms = basis.shape[1]
    for m in range(8):
        cols = slice(m * 128, (m + 1) * 128)
        b_re, b_im = basis[0, :, cols], basis[1, :, cols]
        weights[m, :terms, :128] = b_re
        weights[m, :terms, 128:] = b_im
        weights[m, terms:, :128] = -b_im
        weights[m, terms:, 128:] = b_re


def unit_powers(turns):
    turns = turns - jnp.round(turns)
    angle = (0.5 * math.pi) * turns
    sq = angle * angle
    s = angle * (
        1.0 + sq * (-1.0 / 6 + sq * (1.0 / 120 + sq * (-1.0 / 5040 + sq * (1.0 / 362880))))
    )
    c = 1.0 + sq * (
        -0.5 + sq * (1.0 / 24 + sq * (-1.0 / 720 + sq * (1.0 / 40320 - sq * (1.0 / 3628800))))
    )
    for _ in range(2):
        c, s = 1.0 - 2.0 * (s * s), 2.0 * (s * c)
    return c, s


def cmul(ar, ai, br, bi):
    return ar * br - ai * bi, ar * bi + ai * br


def pack_kernel(me, coefs, tracks, *out):
    capacity = tracks.shape[2]
    rows = coefs.shape[0]
    for r in range(len(out)):
        plane = (me[0] // 4) ^ r
        kept = []
        for k in (0, 2):
            tr = jnp.concatenate([tracks[plane * 4 + k], tracks[plane * 4 + k + 1]], axis=1)
            t_hi = tr.astype(BF16).astype(F32)
            t_mid = (tr - t_hi).astype(BF16).astype(F32)
            kept += [t_hi, t_mid, tr - t_hi - t_mid]
        pieces = jnp.concatenate(kept, axis=0)
        if 2 * capacity < 128:
            blank = jnp.zeros((pieces.shape[0], 128 - 2 * capacity), F32)
            pieces = jnp.concatenate([pieces, blank], axis=1)
        out[r][:rows, :] = coefs[:, :128]
        out[r][rows : 2 * rows, :] = coefs[:, 128:]
        out[r][2 * rows :, :] = pieces.astype(BF16)


def stack_kernel(*refs):
    blocks, out = refs[:-2], refs[-1]
    for r, block in enumerate(blocks):
        out[r] = block[...]


def predict_kernel(
    me,
    near,
    over_y,
    over_core,
    over_both,
    route,
    back,
    pick,
    weights,
    freq,
    image,
    sent_a,
    sent_b,
    table,
    lanes,
    coef,
    wre,
    wim,
    pure,
    puim,
    zrow,
    hre,
    him,
    zv,
    interleaved,
):
    number = image.shape[1]
    tiles, kinds3, capacity = lanes.shape
    slots = tiles * capacity
    rows_own = table.shape[0] // tiles
    chan = freq.shape[1]
    kinds = kinds3 // 3
    steps = kinds // 2
    mine = me[0]

    for arrived, flip in ((near, 0), (over_y, 2), (over_core, 1), (over_both, 3)):
        for r in range(arrived.shape[0]):
            owner = mine ^ (4 * r + flip)
            at = pl.ds(pl.multiple_of(owner * rows_own, rows_own), rows_own)
            table[at, :128] = arrived[r, :rows_own, :]
            table[at, 128:] = arrived[r, rows_own : 2 * rows_own, :]
            piece = arrived[r, 2 * rows_own :, :].astype(F32)
            piece = jnp.where(mine & 2 == 0, piece[:kinds3, :], piece[kinds3:, :])
            moved = jnp.where(mine & 1 == 0, piece, pltpu.roll(piece, 128 - capacity, 1))
            lanes[owner] = moved[:, :capacity]
    per = 128 // capacity
    pieces = jnp.concatenate(
        [
            jnp.concatenate([lanes[d] for d in range(n * per, (n + 1) * per)], axis=1)
            for n in range(tiles // per)
        ],
        axis=1,
    )
    pieces = jnp.concatenate([pieces, jnp.zeros((kinds, slots), F32)], axis=0).astype(BF16)

    per_sub = dot(route[...], pieces, NT).astype(BF16)
    wide = 2 * steps * chan
    from_row = lax.broadcasted_iota(jnp.int32, (4 * kinds, wide), 0) % kinds
    to_lane = lax.broadcasted_iota(jnp.int32, (4 * kinds, wide), 1) // chan
    spread = (from_row == to_lane).astype(F32).astype(BF16)
    uv = dot(per_sub, spread)
    vis = steps * chan
    fr = jnp.concatenate([freq[...]] * steps, axis=1)
    scale = -1.0 / 32.0
    ur, ui = unit_powers(uv[:, :vis] * fr * scale)
    vr, vi = unit_powers(uv[:, vis:] * fr * scale)

    pure[pl.ds(0, number, stride=8), :] = jnp.ones_like(ur)
    puim[pl.ds(0, number, stride=8), :] = jnp.zeros_like(ur)
    pure[pl.ds(1, number, stride=8), :] = ur
    puim[pl.ds(1, number, stride=8), :] = ui
    cr, ci = ur, ui
    for k in range(2, 8):
        cr, ci = cmul(cr, ci, ur, ui)
        pure[pl.ds(k, number, stride=8), :] = cr
        puim[pl.ds(k, number, stride=8), :] = ci
    cr, ci = cmul(cr, ci, ur, ui)
    zrow[0] = cr
    zrow[1] = ci
    cr, ci = cmul(cr, ci, cr, ci)
    zrow[2] = cr
    zrow[3] = ci
    zv[0] = vr
    zv[1] = vi
    cr, ci = vr, vi
    for _ in range(3):
        cr, ci = cmul(cr, ci, cr, ci)
    zrow[4] = cr
    zrow[5] = ci

    coef[...] = dot(pick[...], table[...]).astype(BF16)

    block = 32
    for m in range(8):
        beams = dot(coef[...], weights[m])
        for n in range(0, number, block):
            first = beams[n : n + block, :]
            second = beams[number + n : number + n + block, :]
            f_re, f_im, s_re, s_im = first[:, :128], first[:, 128:], second[:, :128], second[:, 128:]
            g_re = f_re * s_re + f_im * s_im
            g_im = f_im * s_re - f_re * s_im
            i_re = image[m, n : n + block, :128].astype(F32)
            i_im = image[m, n : n + block, 128:].astype(F32)
            to = pl.ds(n * 8 + m, block, stride=8)
            wre[to, :] = i_re * g_re - i_im * g_im
            wim[to, :] = i_re * g_im + i_im * g_re

    lane = lax.broadcasted_iota(jnp.int32, (8, 256), 1)
    inner = (lane // 32) % 4
    masks = [inner == j for j in range(4)]
    unroll = 16

    def one(g):
        at = pl.ds(pl.multiple_of(g * 8, 8), 8)
        w = jnp.concatenate([wre[at, :], wim[at, :]], axis=1)
        lhs = jnp.concatenate([jnp.where(k, w, 0.0) for k in masks], axis=0).astype(BF16)
        p_re, p_im = pure[at, :], puim[at, :]
        z = [jnp.broadcast_to(zrow[k, pl.ds(g, 1), :], (8, 128)) for k in range(6)]
        rr, ii, ri, ir = p_re * z[0], p_im * z[1], p_re * z[1], p_im * z[0]
        up_re, up_im = rr - ii, ri + ir
        dn_re, dn_im = rr + ii, ir - ri
        rr, ii, ri, ir = p_re * z[2], p_im * z[3], p_re * z[3], p_im * z[2]
        lo_re, lo_im = rr + ii, ir - ri
        c = jnp.concatenate([lo_re, dn_re, p_re, up_re], axis=0).astype(BF16)
        s = jnp.concatenate([lo_im, dn_im, p_im, up_im], axis=0).astype(BF16)
        top = jnp.concatenate([c, s], axis=1)
        low = jnp.concatenate([-s, c], axis=1)
        rhs = jnp.concatenate([top] * 4 + [low] * 4, axis=0)
        out = dot(lhs, rhs)
        h_re, h_im = out[24:32, :128], out[24:32, 128:]
        for j in (2, 1, 0):
            n_re = h_re * z[4] - h_im * z[5] + out[8 * j : 8 * j + 8, :128]
            h_im = h_re * z[5] + h_im * z[4] + out[8 * j : 8 * j + 8, 128:]
            h_re = n_re
        hre[at, :] = h_re
        him[at, :] = h_im

    @pl.loop(0, number // unroll)
    def _(n):
        for k in range(unroll):
            one(n * unroll + k)

    vr, vi = zv[0], zv[1]
    a_re = hre[pl.ds(7, number, stride=8), :]
    a_im = him[pl.ds(7, number, stride=8), :]
    for k in range(6, -1, -1):
        n_re = a_re * vr - a_im * vi + hre[pl.ds(k, number, stride=8), :]
        a_im = a_re * vi + a_im * vr + him[pl.ds(k, number, stride=8), :]
        a_re = n_re
    cr, ci = cmul(zrow[4], zrow[5], zrow[4], zrow[5])
    m_re, m_im = a_re * cr + a_im * ci, a_im * cr - a_re * ci
    models = jnp.concatenate([m_re, m_im], axis=1).astype(BF16)
    sent = dot(back[...], models)
    interleaved[pl.ds(0, slots, stride=2), :] = sent[:, :128]
    interleaved[pl.ds(1, slots, stride=2), :] = sent[:, 128:]
    half = capacity
    for d in range(tiles):
        for part, out in enumerate((sent_a, sent_b)):
            rows = slice((2 * d + part) * half, (2 * d + part + 1) * half)
            out[d // 4, d % 4] = interleaved[rows, :].astype(BF16)


def residual_kernel(observed, first, second, residual):
    rows = first.shape[2]
    residual[:, :rows, :] = observed[:, :rows, :] - first[0].astype(F32)
    residual[:, rows:, :] = observed[:, rows:, :] - second[0].astype(F32)


def exchange(value, step, tiles):
    return lax.ppermute(value, "tile", [(i, i ^ step) for i in range(tiles)])


def per_device(
    subgrids,
    stations,
    time_slots,
    assign,
    counts,
    beam_coefs,
    beam_basis,
    frequencies,
    uv_tracks,
    observed,
):
    tiles = lax.axis_size("tile")
    capacity = assign.shape[2]
    slots = tiles * capacity
    number = subgrids.shape[0]
    pixels = subgrids.shape[2]
    edge = math.isqrt(pixels)
    slot_count = beam_coefs.shape[1]
    terms2 = beam_coefs.shape[2]
    steps = uv_tracks.shape[4]
    chan = frequencies.shape[0]
    vis = steps * chan
    vmem = pl.BlockSpec(memory_space=pltpu.VMEM)
    own_tracks = jnp.transpose(uv_tracks[0], (0, 2, 3, 1)).reshape(tiles, 2 * steps, capacity)
    own_rows = beam_coefs.shape[0] * slot_count
    smem = pl.BlockSpec(memory_space=pltpu.SMEM)
    anywhere = pl.BlockSpec(memory_space=pl.ANY)
    outer = tiles // 4
    me = lax.axis_index("tile").astype(jnp.int32).reshape(1)
    block = jax.ShapeDtypeStruct((2 * own_rows + 12 * steps, 128), BF16)
    packed = pl.pallas_call(
        pack_kernel,
        out_shape=[block] * outer,
        in_specs=[smem, vmem, vmem],
        out_specs=[vmem] * outer,
        compiler_params=pltpu.CompilerParams(vmem_limit_bytes=2 * MIB * (1 + tiles // 16)),
        name="pack",
    )(me, beam_coefs.reshape(own_rows, terms2), own_tracks)
    along = [packed[0]] + [exchange(packed[r], 4 * r, tiles) for r in range(1, outer)]

    cells = jnp.transpose(subgrids.reshape(number, 2, 8, 128), (0, 2, 1, 3))
    cells = cells.reshape(number * 16, 128)
    basis = jnp.transpose(
        beam_basis.reshape(2, terms2 // 2, 4, 8, edge), (0, 1, 3, 2, 4)
    ).reshape(2, terms2 // 2, pixels)
    high, rest = transform_matrices(edge)
    image, route, back, pick, weights = pl.pallas_call(
        functools.partial(prepare_kernel, slot_count=slot_count),
        out_shape=[
            jax.ShapeDtypeStruct((8, number, 256), BF16),
            jax.ShapeDtypeStruct((number, slots), BF16),
            jax.ShapeDtypeStruct((slots, number), BF16),
            jax.ShapeDtypeStruct((2 * number, tiles * own_rows), BF16),
            jax.ShapeDtypeStruct((8, terms2, 256), BF16),
        ],
        in_specs=[smem] + [vmem] * 7,
        out_specs=[vmem] * 5,
        scratch_shapes=[
            pltpu.VMEM((number * 16, 128), F32),
            pltpu.VMEM((8, number, 512), BF16),
        ],
        compiler_params=pltpu.CompilerParams(vmem_limit_bytes=16 * MIB * (1 + tiles // 64)),
        name="prepare",
    )(
        counts,
        cells,
        jnp.asarray(high),
        jnp.asarray(rest),
        assign[0],
        stations.T,
        time_slots.reshape(1, number),
        basis,
    )

    near = pl.pallas_call(
        stack_kernel,
        out_shape=jax.ShapeDtypeStruct((outer,) + block.shape, BF16),
        in_specs=[vmem] * outer + [anywhere],
        out_specs=vmem,
        compiler_params=pltpu.CompilerParams(vmem_limit_bytes=2 * MIB * (tiles // 16)),
        name="stack",
    )(*along, image)
    over_y = exchange(near, 2, tiles)
    over_core = exchange(near, 1, tiles)
    over_both = exchange(over_y, 1, tiles)

    first, second = pl.pallas_call(
        predict_kernel,
        out_shape=[jax.ShapeDtypeStruct((outer, 4, capacity, vis), BF16)] * 2,
        in_specs=[smem] + [vmem] * 10,
        out_specs=[vmem] * 2,
        scratch_shapes=[
            pltpu.VMEM((tiles * own_rows, terms2), BF16),
            pltpu.VMEM((tiles, 6 * steps, capacity), F32),
            pltpu.VMEM((2 * number, terms2), BF16),
            pltpu.VMEM((number * 8, 128), F32),
            pltpu.VMEM((number * 8, 128), F32),
            pltpu.VMEM((number * 8, vis), F32),
            pltpu.VMEM((number * 8, vis), F32),
            pltpu.VMEM((6, number, vis), F32),
            pltpu.VMEM((number * 8, vis), F32),
            pltpu.VMEM((number * 8, vis), F32),
            pltpu.VMEM((2, number, vis), F32),
            pltpu.VMEM((2 * slots, vis), F32),
        ],
        compiler_params=pltpu.CompilerParams(vmem_limit_bytes=20 * MIB * (1 + tiles // 64)),
        name="predict",
    )(
        me,
        near,
        over_y,
        over_core,
        over_both,
        route,
        back,
        pick,
        weights,
        frequencies.reshape(1, chan),
        image,
    )
    columns = [[4 * r + k for r in range(outer)] for k in range(4)]
    planes = [[4 * r + k for k in range(4)] for r in range(outer)]

    def swap(value, axis, groups):
        return lax.all_to_all(value, "tile", axis, axis, axis_index_groups=groups, tiled=True)

    first = swap(first, 0, columns)
    second = swap(second, 1, planes)
    first = swap(first, 1, planes)
    second = swap(second, 0, columns)
    residual = pl.pallas_call(
        residual_kernel,
        grid=(outer,),
        out_shape=jax.ShapeDtypeStruct((tiles, 2 * capacity, vis), F32),
        in_specs=[
            pl.BlockSpec((4, 2 * capacity, vis), lambda i: (i, 0, 0)),
            pl.BlockSpec((1, 4, capacity, vis), lambda i: (i, 0, 0, 0)),
            pl.BlockSpec((1, 4, capacity, vis), lambda i: (i, 0, 0, 0)),
        ],
        out_specs=pl.BlockSpec((4, 2 * capacity, vis), lambda i: (i, 0, 0)),
        compiler_params=pltpu.CompilerParams(vmem_limit_bytes=4 * MIB),
        name="residual",
    )(observed.reshape(tiles, 2 * capacity, vis), first, second)
    return residual.reshape(observed.shape)


def solution(mesh):
    return jax.shard_map(
        per_device,
        mesh=mesh,
        in_specs=(
            P(("grp", "tile"), None, None),
            P(("grp", "tile"), None),
            P(("grp", "tile")),
            P(("grp", "tile"), None, None),
            P(("grp", "tile"), None),
            P(("grp", "tile"), None, None),
            P(),
            P("grp"),
            P(("grp", "tile"), None, None, None, None),
            P(("grp", "tile"), None, None, None, None),
        ),
        out_specs=P(("grp", "tile"), None, None, None, None),
        check_vma=False,
    )
```

```python
import functools
import math

import jax
import jax.numpy as jnp
import numpy as np
from jax import lax
from jax.experimental import pallas as pl
from jax.experimental.pallas import tpu as pltpu
from jax.sharding import PartitionSpec as P

TWO_PI = 2.0 * math.pi
F32 = jnp.float32
BF16 = jnp.bfloat16
MIB = 1024 * 1024
NT = (((1,), (1,)), ((), ()))


def dot(a, b, dims=(((1,), (0,)), ((), ()))):
    return lax.dot_general(a, b, dims, preferred_element_type=F32)


def transform_tables(edge):
    low = edge // 8
    outer = np.arange(8)[:, None, None, None]
    b = np.arange(low)[None, :, None, None]
    inner = np.arange(low)[None, None, :, None]
    x = np.arange(edge)
    turns = np.broadcast_to(b * (outer + 8 * inner) % edge, (8, low, low, edge))
    rows = TWO_PI / edge * turns.reshape(8, low, low * edge)
    cells = TWO_PI / edge * np.tile(x[:, None] * x[None, :] % edge, (1, low))
    rows = np.stack([np.cos(rows), np.sin(rows)]).astype(np.float32)
    cells = (np.stack([np.cos(cells), np.sin(cells)]) / edge**2).astype(np.float32)
    return rows.reshape(2, 8 * low, low * edge), cells


def eight_point(re, im):
    half = math.sqrt(0.5)

    def four(r, i):
        s0r, s0i, d0r, d0i = r[0] + r[2], i[0] + i[2], r[0] - r[2], i[0] - i[2]
        s1r, s1i, d1r, d1i = r[1] + r[3], i[1] + i[3], r[1] - r[3], i[1] - i[3]
        return (
            [s0r + s1r, d0r - d1i, s0r - s1r, d0r + d1i],
            [s0i + s1i, d0i + d1r, s0i - s1i, d0i - d1r],
        )

    er, ei = four(re[0::2], im[0::2])
    orr, oi = four(re[1::2], im[1::2])
    tr = [orr[0], half * (orr[1] - oi[1]), -oi[2], -half * (orr[3] + oi[3])]
    ti = [oi[0], half * (orr[1] + oi[1]), orr[2], half * (orr[3] - oi[3])]
    out_re = [er[m] + tr[m] for m in range(4)] + [er[m] - tr[m] for m in range(4)]
    out_im = [ei[m] + ti[m] for m in range(4)] + [ei[m] - ti[m] for m in range(4)]
    return out_re, out_im


def transform_kernel(cells_hbm, row_turns, cell_turns, image, cells, high, rest, wide, sums, sem):
    copy = pltpu.make_async_copy(cells_hbm, cells, sem)
    copy.start()
    number = image.shape[1]
    edge, span = cell_turns.shape[1:]
    low = span // edge
    cell_c, cell_s = cell_turns[0], cell_turns[1]
    for m in range(8):
        for k in range(low):
            at = m * low + k
            row_c, row_s = row_turns[0, at : at + 1, :], row_turns[1, at : at + 1, :]
            c = row_c * cell_c - row_s * cell_s
            s = row_s * cell_c + row_c * cell_s
            c_top, s_top = c.astype(BF16), s.astype(BF16)
            c_left = (c - c_top.astype(F32)).astype(BF16)
            s_left = (s - s_top.astype(F32)).astype(BF16)
            re = slice(k * edge, (k + 1) * edge)
            im = slice(span + k * edge, span + (k + 1) * edge)
            for held, cos_part, sin_part in ((high, c_top, s_top), (rest, c_left, s_left)):
                held[m, re, :span] = cos_part
                held[m, re, span:] = sin_part
                held[m, im, :span] = -sin_part
                held[m, im, span:] = cos_part
    copy.wait()
    step = 16

    @pl.loop(0, number // step, unroll=2)
    def _(n):
        rows = pl.ds(pl.multiple_of(n * step, step), step)
        span = pl.ds(pl.multiple_of(n * step * 16, step * 16), step * 16)
        wide[span, :] = cells[span, :].astype(F32)
        re = [wide[pl.ds(n * step * 16 + 2 * k, step, stride=16), :] for k in range(8)]
        im = [wide[pl.ds(n * step * 16 + 2 * k + 1, step, stride=16), :] for k in range(8)]
        out_re, out_im = eight_point(re, im)
        for m in range(8):
            value = jnp.concatenate([out_re[m], out_im[m]], axis=1)
            top = value.astype(BF16)
            sums[m, rows, :256] = top
            sums[m, rows, 256:] = (value - top.astype(F32)).astype(BF16)

    for m in range(8):
        both = sums[m]
        left = jnp.concatenate([both, both[:, :256]], axis=1)
        right = jnp.concatenate([high[m], high[m], rest[m]], axis=0)
        image[m] = dot(left, right).astype(BF16)


def prepare_kernel(counts, assign, stations, time_slots, basis, after, route, back, pick, weights, *, slot_count):
    number = route.shape[0]
    tiles, capacity = assign.shape

    per = 128 // capacity
    down = lax.broadcasted_iota(jnp.int32, (number, 128), 0)
    slot = lax.broadcasted_iota(jnp.int32, (1, capacity), 1)
    for n in range(tiles // per):
        chosen = [
            jnp.where(slot < counts[0, d], assign[d : d + 1, :], -1)
            for d in range(n * per, (n + 1) * per)
        ]
        hot = (jnp.concatenate(chosen, axis=1) == down).astype(F32)
        route[:, n * 128 : (n + 1) * 128] = hot.astype(BF16)
        back[n * 128 : (n + 1) * 128, :] = hot.T.astype(BF16)

    index = (stations[...] * slot_count + time_slots[...]).astype(F32)
    index = jnp.concatenate([index, jnp.zeros((6, number), F32)], axis=0).T
    index = index.astype(jnp.int32)
    across = lax.broadcasted_iota(jnp.int32, (number, pick.shape[1]), 1)
    for which in range(2):
        hot = (index[:, which : which + 1] == across).astype(F32)
        pick[which * number : (which + 1) * number, :] = hot.astype(BF16)

    terms = basis.shape[1]
    edge = math.isqrt(basis.shape[2])
    for m in range(8):
        starts = [(8 * n + m) * edge for n in range(edge // 8)]
        b_re = jnp.concatenate([basis[0, :, n : n + edge] for n in starts], axis=1)
        b_im = jnp.concatenate([basis[1, :, n : n + edge] for n in starts], axis=1)
        weights[m, :terms, :128] = b_re
        weights[m, :terms, 128:] = b_im
        weights[m, terms:, :128] = -b_im
        weights[m, terms:, 128:] = b_re


def unit_powers(turns):
    turns = turns - jnp.round(turns)
    angle = (0.5 * math.pi) * turns
    sq = angle * angle
    s = angle * (
        1.0 + sq * (-1.0 / 6 + sq * (1.0 / 120 + sq * (-1.0 / 5040 + sq * (1.0 / 362880))))
    )
    c = 1.0 + sq * (
        -0.5 + sq * (1.0 / 24 + sq * (-1.0 / 720 + sq * (1.0 / 40320 - sq * (1.0 / 3628800))))
    )
    for _ in range(2):
        c, s = 1.0 - 2.0 * (s * s), 2.0 * (s * c)
    return c, s


def cmul(ar, ai, br, bi):
    return ar * br - ai * bi, ar * bi + ai * br


def pack_kernel(me, coefs_hbm, tracks_hbm, *refs):
    out, (coefs, tracks, sems) = refs[:-3], refs[-3:]
    copies = [
        pltpu.make_async_copy(coefs_hbm, coefs, sems.at[0]),
        pltpu.make_async_copy(tracks_hbm, tracks, sems.at[1]),
    ]
    for copy in copies:
        copy.start()
    for copy in copies:
        copy.wait()
    capacity = tracks.shape[2]
    rows = coefs.shape[0]
    for r in range(len(out)):
        plane = (me[0] // 4) ^ r
        kept = []
        for k in (0, 2):
            tr = jnp.concatenate([tracks[plane * 4 + k], tracks[plane * 4 + k + 1]], axis=1)
            t_hi = tr.astype(BF16).astype(F32)
            t_mid = (tr - t_hi).astype(BF16).astype(F32)
            kept += [t_hi, t_mid, tr - t_hi - t_mid]
        pieces = jnp.concatenate(kept, axis=0)
        if 2 * capacity < 128:
            blank = jnp.zeros((pieces.shape[0], 128 - 2 * capacity), F32)
            pieces = jnp.concatenate([pieces, blank], axis=1)
        out[r][:rows, :] = coefs[:, :128]
        out[r][rows : 2 * rows, :] = coefs[:, 128:]
        out[r][2 * rows :, :] = pieces.astype(BF16)


def stack_kernel(*refs):
    blocks, out = refs[:-2], refs[-1]
    for r, block in enumerate(blocks):
        out[r] = block[...]


def predict_kernel(
    me,
    near,
    over_y,
    over_core,
    over_both,
    route,
    back,
    pick,
    weights,
    freq,
    image,
    *refs,
):
    table, lanes, coef, wre, wim, pure, puim, zrow, hre, him, zv, interleaved = refs[-12:]
    number = image.shape[1]
    tiles, kinds3, capacity = lanes.shape
    slots = tiles * capacity
    rows_own = table.shape[0] // tiles
    chan = freq.shape[1]
    kinds = kinds3 // 3
    steps = kinds // 2
    mine = me[0]

    for arrived, flip in ((near, 0), (over_y, 2), (over_core, 1), (over_both, 3)):
        for r in range(arrived.shape[0]):
            owner = mine ^ (4 * r + flip)
            at = pl.ds(pl.multiple_of(owner * rows_own, rows_own), rows_own)
            table[at, :128] = arrived[r, :rows_own, :]
            table[at, 128:] = arrived[r, rows_own : 2 * rows_own, :]
            piece = arrived[r, 2 * rows_own :, :].astype(F32)
            piece = jnp.where(mine & 2 == 0, piece[:kinds3, :], piece[kinds3:, :])
            moved = jnp.where(mine & 1 == 0, piece, pltpu.roll(piece, 128 - capacity, 1))
            lanes[owner] = moved[:, :capacity]
    per = 128 // capacity
    pieces = jnp.concatenate(
        [
            jnp.concatenate([lanes[d] for d in range(n * per, (n + 1) * per)], axis=1)
            for n in range(tiles // per)
        ],
        axis=1,
    )
    pieces = jnp.concatenate([pieces, jnp.zeros((kinds, slots), F32)], axis=0).astype(BF16)

    per_sub = dot(route[...], pieces, NT).astype(BF16)
    wide = 2 * steps * chan
    from_row = lax.broadcasted_iota(jnp.int32, (4 * kinds, wide), 0) % kinds
    to_lane = lax.broadcasted_iota(jnp.int32, (4 * kinds, wide), 1) // chan
    spread = (from_row == to_lane).astype(F32).astype(BF16)
    uv = dot(per_sub, spread)
    vis = steps * chan
    fr = jnp.concatenate([freq[...]] * steps, axis=1)
    scale = -1.0 / 32.0
    ur, ui = unit_powers(uv[:, :vis] * fr * scale)
    vr, vi = unit_powers(uv[:, vis:] * fr * scale)

    pure[pl.ds(0, number, stride=8), :] = jnp.ones_like(ur)
    puim[pl.ds(0, number, stride=8), :] = jnp.zeros_like(ur)
    pure[pl.ds(1, number, stride=8), :] = ur
    puim[pl.ds(1, number, stride=8), :] = ui
    cr, ci = ur, ui
    for k in range(2, 8):
        cr, ci = cmul(cr, ci, ur, ui)
        pure[pl.ds(k, number, stride=8), :] = cr
        puim[pl.ds(k, number, stride=8), :] = ci
    cr, ci = cmul(cr, ci, ur, ui)
    zrow[0] = cr
    zrow[1] = ci
    cr, ci = cmul(cr, ci, cr, ci)
    zrow[2] = cr
    zrow[3] = ci
    zv[0] = vr
    zv[1] = vi
    cr, ci = vr, vi
    for _ in range(3):
        cr, ci = cmul(cr, ci, cr, ci)
    zrow[4] = cr
    zrow[5] = ci

    coef[...] = dot(pick[...], table[...]).astype(BF16)

    block = 32
    for m in range(8):
        beams = dot(coef[...], weights[m])
        for n in range(0, number, block):
            first = beams[n : n + block, :]
            second = beams[number + n : number + n + block, :]
            f_re, f_im, s_re, s_im = first[:, :128], first[:, 128:], second[:, :128], second[:, 128:]
            g_re = f_re * s_re + f_im * s_im
            g_im = f_im * s_re - f_re * s_im
            i_re = image[m, n : n + block, :128].astype(F32)
            i_im = image[m, n : n + block, 128:].astype(F32)
            to = pl.ds(n * 8 + m, block, stride=8)
            wre[to, :] = i_re * g_re - i_im * g_im
            wim[to, :] = i_re * g_im + i_im * g_re

    unroll = 16

    def one(g):
        at = pl.ds(pl.multiple_of(g * 8, 8), 8)
        w_re, w_im = wre[at, :], wim[at, :]
        lhs = [
            jnp.concatenate([w_re[:, n : n + 32], w_im[:, n : n + 32]], axis=1)
            for n in range(0, 128, 32)
        ]
        lhs = jnp.concatenate(lhs, axis=0).astype(BF16)
        p_re, p_im = pure[at, :], puim[at, :]
        z = [jnp.broadcast_to(zrow[k, pl.ds(g, 1), :], (8, 128)) for k in range(6)]
        rr, ii, ri, ir = p_re * z[0], p_im * z[1], p_re * z[1], p_im * z[0]
        up_re, up_im = rr - ii, ri + ir
        dn_re, dn_im = rr + ii, ir - ri
        rr, ii, ri, ir = p_re * z[2], p_im * z[3], p_re * z[3], p_im * z[2]
        lo_re, lo_im = rr + ii, ir - ri
        c = jnp.concatenate([lo_re, dn_re, p_re, up_re], axis=0).astype(BF16)
        s = jnp.concatenate([lo_im, dn_im, p_im, up_im], axis=0).astype(BF16)
        top = jnp.concatenate([c, s], axis=1)
        low = jnp.concatenate([-s, c], axis=1)
        rhs = jnp.concatenate([top, low], axis=0)
        out = dot(lhs, rhs)
        h_re, h_im = out[24:32, :128], out[24:32, 128:]
        for j in (2, 1, 0):
            n_re = h_re * z[4] - h_im * z[5] + out[8 * j : 8 * j + 8, :128]
            h_im = h_re * z[5] + h_im * z[4] + out[8 * j : 8 * j + 8, 128:]
            h_re = n_re
        hre[at, :] = h_re
        him[at, :] = h_im

    @pl.loop(0, number // unroll)
    def _(n):
        for k in range(unroll):
            one(n * unroll + k)

    vr, vi = zv[0], zv[1]
    a_re = hre[pl.ds(7, number, stride=8), :]
    a_im = him[pl.ds(7, number, stride=8), :]
    for k in range(6, -1, -1):
        n_re = a_re * vr - a_im * vi + hre[pl.ds(k, number, stride=8), :]
        a_im = a_re * vi + a_im * vr + him[pl.ds(k, number, stride=8), :]
        a_re = n_re
    cr, ci = cmul(zrow[4], zrow[5], zrow[4], zrow[5])
    m_re, m_im = a_re * cr + a_im * ci, a_im * cr - a_re * ci
    models = jnp.concatenate([m_re, m_im], axis=1).astype(BF16)
    sent = dot(back[...], models)
    interleaved[pl.ds(0, slots, stride=2), :] = sent[:, :128]
    interleaved[pl.ds(1, slots, stride=2), :] = sent[:, 128:]
    along_z, in_plane = refs[: tiles // 4], refs[tiles // 4 : tiles // 4 + 4]
    for r in range(tiles // 4):
        for p in range(4):
            start = pl.multiple_of((mine ^ (4 * r + p)) * (2 * capacity), capacity)
            along_z[r][p] = interleaved[pl.ds(start, capacity), :].astype(BF16)
            in_plane[p][r] = interleaved[pl.ds(start + capacity, capacity), :].astype(BF16)


def turn_kernel(*refs):
    count = refs[0].shape[0]
    blocks, out = refs[:-count], refs[-count:]
    for i, block in enumerate(blocks):
        for j in range(count):
            out[j][i] = block[j]


def residual_kernel(me, observed, *refs):
    arrived, residual = refs[:-1], refs[-1]
    by_plane, by_z = arrived[:4], arrived[4:]
    rows = by_plane[0].shape[1]
    for r in range(len(by_z)):
        for p in range(4):
            source = me[0] ^ (4 * r + p)
            residual[source, :rows, :] = observed[source, :rows, :] - by_plane[p][r].astype(F32)
            residual[source, rows:, :] = observed[source, rows:, :] - by_z[r][p].astype(F32)


def exchange(value, step, tiles):
    return lax.ppermute(value, "tile", [(i, i ^ step) for i in range(tiles)])


def per_device(
    subgrids,
    stations,
    time_slots,
    assign,
    counts,
    beam_coefs,
    beam_basis,
    frequencies,
    uv_tracks,
    observed,
):
    tiles = lax.axis_size("tile")
    capacity = assign.shape[2]
    slots = tiles * capacity
    number = subgrids.shape[0]
    pixels = subgrids.shape[2]
    edge = math.isqrt(pixels)
    slot_count = beam_coefs.shape[1]
    terms2 = beam_coefs.shape[2]
    steps = uv_tracks.shape[4]
    chan = frequencies.shape[0]
    vis = steps * chan
    vmem = pl.BlockSpec(memory_space=pltpu.VMEM)
    own_tracks = jnp.transpose(uv_tracks[0], (0, 2, 3, 1)).reshape(tiles, 2 * steps, capacity)
    own_rows = beam_coefs.shape[0] * slot_count
    smem = pl.BlockSpec(memory_space=pltpu.SMEM)
    anywhere = pl.BlockSpec(memory_space=pl.ANY)
    hbm = pl.BlockSpec(memory_space=pltpu.HBM)
    outer = tiles // 4
    me = lax.axis_index("tile").astype(jnp.int32).reshape(1)
    block = jax.ShapeDtypeStruct((2 * own_rows + 12 * steps, 128), BF16)
    packed = pl.pallas_call(
        pack_kernel,
        out_shape=[block] * outer,
        in_specs=[smem, hbm, hbm],
        out_specs=[vmem] * outer,
        scratch_shapes=[
            pltpu.VMEM((own_rows, terms2), BF16),
            pltpu.VMEM((tiles, 2 * steps, capacity), F32),
            pltpu.SemaphoreType.DMA((2,)),
        ],
        compiler_params=pltpu.CompilerParams(vmem_limit_bytes=2 * MIB * (1 + tiles // 16)),
        name="pack",
    )(me, beam_coefs.reshape(own_rows, terms2), own_tracks)
    along = [packed[0]] + [exchange(packed[r], 4 * r, tiles) for r in range(1, outer)]

    cells = jnp.transpose(subgrids.reshape(number, 2, 8, 128), (0, 2, 1, 3))
    cells = cells.reshape(number * 16, 128)
    row_turns, cell_turns = transform_tables(edge)
    image = pl.pallas_call(
        transform_kernel,
        out_shape=jax.ShapeDtypeStruct((8, number, 256), BF16),
        in_specs=[hbm] + [vmem] * 2,
        out_specs=vmem,
        scratch_shapes=[
            pltpu.VMEM((number * 16, 128), BF16),
            pltpu.VMEM((8, 256, 256), BF16),
            pltpu.VMEM((8, 256, 256), BF16),
            pltpu.VMEM((number * 16, 128), F32),
            pltpu.VMEM((8, number, 512), BF16),
            pltpu.SemaphoreType.DMA,
        ],
        compiler_params=pltpu.CompilerParams(vmem_limit_bytes=14 * MIB),
        name="transform",
    )(cells, jnp.asarray(row_turns), jnp.asarray(cell_turns))

    near = pl.pallas_call(
        stack_kernel,
        out_shape=jax.ShapeDtypeStruct((outer,) + block.shape, BF16),
        in_specs=[vmem] * outer + [anywhere],
        out_specs=vmem,
        compiler_params=pltpu.CompilerParams(vmem_limit_bytes=2 * MIB * (tiles // 16)),
        name="stack",
    )(*along, image)
    over_y = exchange(near, 2, tiles)
    over_core = exchange(near, 1, tiles)
    over_both = exchange(over_y, 1, tiles)

    route, back, pick, weights = pl.pallas_call(
        functools.partial(prepare_kernel, slot_count=slot_count),
        out_shape=[
            jax.ShapeDtypeStruct((number, slots), BF16),
            jax.ShapeDtypeStruct((slots, number), BF16),
            jax.ShapeDtypeStruct((2 * number, tiles * own_rows), BF16),
            jax.ShapeDtypeStruct((8, terms2, 256), BF16),
        ],
        in_specs=[smem] + [vmem] * 4 + [anywhere],
        out_specs=[vmem] * 4,
        compiler_params=pltpu.CompilerParams(vmem_limit_bytes=8 * MIB * (1 + tiles // 64)),
        name="prepare",
    )(
        counts,
        assign[0],
        stations.T,
        time_slots.reshape(1, number),
        beam_basis,
        near,
    )

    for_z = jax.ShapeDtypeStruct((4, capacity, vis), BF16)
    for_plane = jax.ShapeDtypeStruct((outer, capacity, vis), BF16)
    models = pl.pallas_call(
        predict_kernel,
        out_shape=[for_z] * outer + [for_plane] * 4,
        in_specs=[smem] + [vmem] * 10,
        out_specs=[vmem] * (outer + 4),
        scratch_shapes=[
            pltpu.VMEM((tiles * own_rows, terms2), BF16),
            pltpu.VMEM((tiles, 6 * steps, capacity), F32),
            pltpu.VMEM((2 * number, terms2), BF16),
            pltpu.VMEM((number * 8, 128), F32),
            pltpu.VMEM((number * 8, 128), F32),
            pltpu.VMEM((number * 8, vis), F32),
            pltpu.VMEM((number * 8, vis), F32),
            pltpu.VMEM((6, number, vis), F32),
            pltpu.VMEM((number * 8, vis), F32),
            pltpu.VMEM((number * 8, vis), F32),
            pltpu.VMEM((2, number, vis), F32),
            pltpu.VMEM((2 * slots, vis), F32),
        ],
        compiler_params=pltpu.CompilerParams(vmem_limit_bytes=20 * MIB * (1 + tiles // 64)),
        name="predict",
    )(
        me,
        near,
        over_y,
        over_core,
        over_both,
        route,
        back,
        pick,
        weights,
        frequencies.reshape(1, chan),
        image,
    )
    def turned(blocks, out_shape):
        return pl.pallas_call(
            turn_kernel,
            out_shape=out_shape,
            in_specs=[vmem] * len(blocks),
            out_specs=[vmem] * len(out_shape),
            compiler_params=pltpu.CompilerParams(vmem_limit_bytes=2 * MIB),
            name="turn",
        )(*blocks)

    first, second = models[:outer], models[outer:]
    second = [second[0]] + [exchange(second[p], p, tiles) for p in range(1, 4)]
    first = [first[0]] + [exchange(first[r], 4 * r, tiles) for r in range(1, outer)]
    second = turned(second, [for_z] * outer)
    second = [second[0]] + [exchange(second[r], 4 * r, tiles) for r in range(1, outer)]
    first = turned(first, [for_plane] * 4)
    first = [first[0]] + [exchange(first[p], p, tiles) for p in range(1, 4)]
    residual = pl.pallas_call(
        residual_kernel,
        out_shape=jax.ShapeDtypeStruct((tiles, 2 * capacity, vis), F32),
        in_specs=[smem] + [vmem] * (5 + outer),
        out_specs=vmem,
        compiler_params=pltpu.CompilerParams(vmem_limit_bytes=6 * MIB),
        name="residual",
    )(me, observed.reshape(tiles, 2 * capacity, vis), *first, *second)
    return residual.reshape(observed.shape)


def solution(mesh):
    return jax.shard_map(
        per_device,
        mesh=mesh,
        in_specs=(
            P(("grp", "tile"), None, None),
            P(("grp", "tile"), None),
            P(("grp", "tile")),
            P(("grp", "tile"), None, None),
            P(("grp", "tile"), None),
            P(("grp", "tile"), None, None),
            P(),
            P("grp"),
            P(("grp", "tile"), None, None, None, None),
            P(("grp", "tile"), None, None, None, None),
        ),
        out_specs=P(("grp", "tile"), None, None, None, None),
        check_vma=False,
    )
```

```python
import functools
import math

import jax
import jax.numpy as jnp
import numpy as np
from jax import lax
from jax.experimental import pallas as pl
from jax.experimental.pallas import tpu as pltpu
from jax.sharding import PartitionSpec as P

TWO_PI = 2.0 * math.pi
F32 = jnp.float32
BF16 = jnp.bfloat16
MIB = 1024 * 1024
NT = (((1,), (1,)), ((), ()))


def dot(a, b, dims=(((1,), (0,)), ((), ()))):
    return lax.dot_general(a, b, dims, preferred_element_type=F32)


def transform_tables(edge):
    low = edge // 8
    outer = np.arange(8)[:, None, None, None]
    b = np.arange(low)[None, :, None, None]
    inner = np.arange(low)[None, None, :, None]
    x = np.arange(edge)
    turns = np.broadcast_to(b * (outer + 8 * inner) % edge, (8, low, low, edge))
    rows = TWO_PI / edge * turns.reshape(8, low, low * edge)
    cells = TWO_PI / edge * np.tile(x[:, None] * x[None, :] % edge, (1, low))
    rows = np.stack([np.cos(rows), np.sin(rows)]).astype(np.float32)
    cells = (np.stack([np.cos(cells), np.sin(cells)]) / edge**2).astype(np.float32)
    return rows.reshape(2, 8 * low, low * edge), cells


def eight_point(re, im):
    half = math.sqrt(0.5)

    def four(r, i):
        s0r, s0i, d0r, d0i = r[0] + r[2], i[0] + i[2], r[0] - r[2], i[0] - i[2]
        s1r, s1i, d1r, d1i = r[1] + r[3], i[1] + i[3], r[1] - r[3], i[1] - i[3]
        return (
            [s0r + s1r, d0r - d1i, s0r - s1r, d0r + d1i],
            [s0i + s1i, d0i + d1r, s0i - s1i, d0i - d1r],
        )

    er, ei = four(re[0::2], im[0::2])
    orr, oi = four(re[1::2], im[1::2])
    tr = [orr[0], half * (orr[1] - oi[1]), -oi[2], -half * (orr[3] + oi[3])]
    ti = [oi[0], half * (orr[1] + oi[1]), orr[2], half * (orr[3] - oi[3])]
    out_re = [er[m] + tr[m] for m in range(4)] + [er[m] - tr[m] for m in range(4)]
    out_im = [ei[m] + ti[m] for m in range(4)] + [ei[m] - ti[m] for m in range(4)]
    return out_re, out_im


def transform_kernel(cells_hbm, row_turns, cell_turns, image, cells, high, rest, wide, sums, sem):
    copy = pltpu.make_async_copy(cells_hbm, cells, sem)
    copy.start()
    number = image.shape[1]
    edge, span = cell_turns.shape[1:]
    low = span // edge
    cell_c, cell_s = cell_turns[0], cell_turns[1]
    for m in range(8):
        for k in range(low):
            at = m * low + k
            row_c, row_s = row_turns[0, at : at + 1, :], row_turns[1, at : at + 1, :]
            c = row_c * cell_c - row_s * cell_s
            s = row_s * cell_c + row_c * cell_s
            c_top, s_top = c.astype(BF16), s.astype(BF16)
            c_left = (c - c_top.astype(F32)).astype(BF16)
            s_left = (s - s_top.astype(F32)).astype(BF16)
            re = slice(k * edge, (k + 1) * edge)
            im = slice(span + k * edge, span + (k + 1) * edge)
            for held, cos_part, sin_part in ((high, c_top, s_top), (rest, c_left, s_left)):
                held[m, re, :span] = cos_part
                held[m, re, span:] = sin_part
                held[m, im, :span] = -sin_part
                held[m, im, span:] = cos_part
    copy.wait()
    step = 16

    @pl.loop(0, number // step, unroll=2)
    def _(n):
        rows = pl.ds(pl.multiple_of(n * step, step), step)
        span = pl.ds(pl.multiple_of(n * step * 16, step * 16), step * 16)
        wide[span, :] = cells[span, :].astype(F32)
        re = [wide[pl.ds(n * step * 16 + 2 * k, step, stride=16), :] for k in range(8)]
        im = [wide[pl.ds(n * step * 16 + 2 * k + 1, step, stride=16), :] for k in range(8)]
        out_re, out_im = eight_point(re, im)
        for m in range(8):
            value = jnp.concatenate([out_re[m], out_im[m]], axis=1)
            top = value.astype(BF16)
            sums[m, rows, :256] = top
            sums[m, rows, 256:] = (value - top.astype(F32)).astype(BF16)

    for m in range(8):
        both = sums[m]
        left = jnp.concatenate([both, both[:, :256]], axis=1)
        right = jnp.concatenate([high[m], high[m], rest[m]], axis=0)
        image[m] = dot(left, right).astype(BF16)


def prepare_kernel(
    counts, assign, stations, time_slots, basis, freq, route, back, pick, weights, turns, *, slot_count
):
    number = route.shape[0]
    tiles, capacity = assign.shape
    scaled = freq[...] * (-1.0 / 32.0)
    turns[...] = jnp.concatenate([scaled] * (turns.shape[1] // freq.shape[1]), axis=1)

    per = 128 // capacity
    down = lax.broadcasted_iota(jnp.int32, (number, 128), 0)
    slot = lax.broadcasted_iota(jnp.int32, (1, capacity), 1)
    for n in range(tiles // per):
        chosen = [
            jnp.where(slot < counts[0, d], assign[d : d + 1, :], -1)
            for d in range(n * per, (n + 1) * per)
        ]
        hot = (jnp.concatenate(chosen, axis=1) == down).astype(F32)
        route[:, n * 128 : (n + 1) * 128] = hot.astype(BF16)
        back[n * 128 : (n + 1) * 128, :] = hot.T.astype(BF16)

    index = (stations[...] * slot_count + time_slots[...]).astype(F32)
    index = jnp.concatenate([index, jnp.zeros((6, number), F32)], axis=0).T
    index = index.astype(jnp.int32)
    across = lax.broadcasted_iota(jnp.int32, (number, pick.shape[1]), 1)
    for which in range(2):
        hot = (index[:, which : which + 1] == across).astype(F32)
        pick[which * number : (which + 1) * number, :] = hot.astype(BF16)

    terms = basis.shape[1]
    edge = math.isqrt(basis.shape[2])
    for m in range(8):
        starts = [(8 * n + m) * edge for n in range(edge // 8)]
        b_re = jnp.concatenate([basis[0, :, n : n + edge] for n in starts], axis=1)
        b_im = jnp.concatenate([basis[1, :, n : n + edge] for n in starts], axis=1)
        weights[m, :terms, :128] = b_re
        weights[m, :terms, 128:] = b_im
        weights[m, terms:, :128] = -b_im
        weights[m, terms:, 128:] = b_re


def unit_powers(turns):
    turns = turns - jnp.round(turns)
    angle = (0.5 * math.pi) * turns
    sq = angle * angle
    s = angle * (
        1.0 + sq * (-1.0 / 6 + sq * (1.0 / 120 + sq * (-1.0 / 5040 + sq * (1.0 / 362880))))
    )
    c = 1.0 + sq * (
        -0.5 + sq * (1.0 / 24 + sq * (-1.0 / 720 + sq * (1.0 / 40320 - sq * (1.0 / 3628800))))
    )
    for _ in range(2):
        c, s = 1.0 - 2.0 * (s * s), 2.0 * (s * c)
    return c, s


def cmul(ar, ai, br, bi):
    return ar * br - ai * bi, ar * bi + ai * br


def pack_kernel(me, coefs_hbm, tracks_hbm, *refs):
    out, (coefs, tracks, sems) = refs[:-3], refs[-3:]
    copies = [
        pltpu.make_async_copy(coefs_hbm, coefs, sems.at[0]),
        pltpu.make_async_copy(tracks_hbm, tracks, sems.at[1]),
    ]
    for copy in copies:
        copy.start()
    for copy in copies:
        copy.wait()
    capacity = tracks.shape[2]
    rows = coefs.shape[0]
    for r in range(len(out)):
        plane = (me[0] // 4) ^ r
        kept = []
        for k in (0, 2):
            tr = jnp.concatenate([tracks[plane * 4 + k], tracks[plane * 4 + k + 1]], axis=1)
            t_hi = tr.astype(BF16).astype(F32)
            t_mid = (tr - t_hi).astype(BF16).astype(F32)
            kept += [t_hi, t_mid, tr - t_hi - t_mid]
        pieces = jnp.concatenate(kept, axis=0)
        if 2 * capacity < 128:
            blank = jnp.zeros((pieces.shape[0], 128 - 2 * capacity), F32)
            pieces = jnp.concatenate([pieces, blank], axis=1)
        out[r][:rows, :] = coefs[:, :128]
        out[r][rows : 2 * rows, :] = coefs[:, 128:]
        out[r][2 * rows :, :] = pieces.astype(BF16)


def stack_kernel(*refs):
    blocks, out = refs[:-3], refs[-1]
    for r, block in enumerate(blocks):
        out[r] = block[...]


def predict_kernel(
    me,
    near,
    over_y,
    over_core,
    over_both,
    route,
    back,
    pick,
    weights,
    turns,
    image,
    *refs,
):
    table, lanes, coef, wre, wim, pure, puim, zrow, hre, him, zv, interleaved = refs[-12:]
    number = image.shape[1]
    tiles, kinds3, capacity = lanes.shape
    slots = tiles * capacity
    rows_own = table.shape[0] // tiles
    vis = turns.shape[1]
    kinds = kinds3 // 3
    steps = kinds // 2
    chan = vis // steps
    mine = me[0]

    for arrived, flip in ((near, 0), (over_y, 2), (over_core, 1), (over_both, 3)):
        for r in range(arrived.shape[0]):
            owner = mine ^ (4 * r + flip)
            at = pl.ds(pl.multiple_of(owner * rows_own, rows_own), rows_own)
            table[at, :128] = arrived[r, :rows_own, :]
            table[at, 128:] = arrived[r, rows_own : 2 * rows_own, :]
            piece = arrived[r, 2 * rows_own :, :].astype(F32)
            piece = jnp.where(mine & 2 == 0, piece[:kinds3, :], piece[kinds3:, :])
            moved = jnp.where(mine & 1 == 0, piece, pltpu.roll(piece, 128 - capacity, 1))
            lanes[owner] = moved[:, :capacity]
    per = 128 // capacity
    pieces = jnp.concatenate(
        [
            jnp.concatenate([lanes[d] for d in range(n * per, (n + 1) * per)], axis=1)
            for n in range(tiles // per)
        ],
        axis=1,
    )
    pieces = jnp.concatenate([pieces, jnp.zeros((kinds, slots), F32)], axis=0).astype(BF16)

    per_sub = dot(route[...], pieces, NT).astype(BF16)
    wide = 2 * steps * chan
    from_row = lax.broadcasted_iota(jnp.int32, (4 * kinds, wide), 0) % kinds
    to_lane = lax.broadcasted_iota(jnp.int32, (4 * kinds, wide), 1) // chan
    spread = (from_row == to_lane).astype(F32).astype(BF16)
    uv = dot(per_sub, spread)
    ur, ui = unit_powers(uv[:, :vis] * turns[...])
    vr, vi = unit_powers(uv[:, vis:] * turns[...])

    pure[pl.ds(0, number, stride=8), :] = jnp.ones_like(ur)
    puim[pl.ds(0, number, stride=8), :] = jnp.zeros_like(ur)
    pure[pl.ds(1, number, stride=8), :] = ur
    puim[pl.ds(1, number, stride=8), :] = ui
    cr, ci = ur, ui
    for k in range(2, 8):
        cr, ci = cmul(cr, ci, ur, ui)
        pure[pl.ds(k, number, stride=8), :] = cr
        puim[pl.ds(k, number, stride=8), :] = ci
    cr, ci = cmul(cr, ci, ur, ui)
    zrow[0] = cr
    zrow[1] = ci
    cr, ci = cmul(cr, ci, cr, ci)
    zrow[2] = cr
    zrow[3] = ci
    zv[0] = vr
    zv[1] = vi
    cr, ci = vr, vi
    for _ in range(3):
        cr, ci = cmul(cr, ci, cr, ci)
    zrow[4] = cr
    zrow[5] = ci

    coef[...] = dot(pick[...], table[...]).astype(BF16)

    block = 32
    for m in range(8):
        beams = dot(coef[...], weights[m])
        for n in range(0, number, block):
            first = beams[n : n + block, :]
            second = beams[number + n : number + n + block, :]
            f_re, f_im, s_re, s_im = first[:, :128], first[:, 128:], second[:, :128], second[:, 128:]
            g_re = f_re * s_re + f_im * s_im
            g_im = f_im * s_re - f_re * s_im
            i_re = image[m, n : n + block, :128].astype(F32)
            i_im = image[m, n : n + block, 128:].astype(F32)
            to = pl.ds(n * 8 + m, block, stride=8)
            wre[to, :] = i_re * g_re - i_im * g_im
            wim[to, :] = i_re * g_im + i_im * g_re

    unroll = 16

    def one(g):
        at = pl.ds(pl.multiple_of(g * 8, 8), 8)
        w_re, w_im = wre[at, :], wim[at, :]
        lhs = [
            jnp.concatenate([w_re[:, n : n + 32], w_im[:, n : n + 32]], axis=1)
            for n in range(0, 128, 32)
        ]
        lhs = jnp.concatenate(lhs, axis=0).astype(BF16)
        p_re, p_im = pure[at, :], puim[at, :]
        z = [jnp.broadcast_to(zrow[k, pl.ds(g, 1), :], (8, 128)) for k in range(6)]
        rr, ii, ri, ir = p_re * z[0], p_im * z[1], p_re * z[1], p_im * z[0]
        up_re, up_im = rr - ii, ri + ir
        dn_re, dn_im = rr + ii, ir - ri
        rr, ii, ri, ir = p_re * z[2], p_im * z[3], p_re * z[3], p_im * z[2]
        lo_re, lo_im = rr + ii, ir - ri
        c = jnp.concatenate([lo_re, dn_re, p_re, up_re], axis=0).astype(BF16)
        s = jnp.concatenate([lo_im, dn_im, p_im, up_im], axis=0).astype(BF16)
        top = jnp.concatenate([c, s], axis=1)
        low = jnp.concatenate([-s, c], axis=1)
        rhs = jnp.concatenate([top, low], axis=0)
        out = dot(lhs, rhs)
        h_re, h_im = out[24:32, :128], out[24:32, 128:]
        for j in (2, 1, 0):
            n_re = h_re * z[4] - h_im * z[5] + out[8 * j : 8 * j + 8, :128]
            h_im = h_re * z[5] + h_im * z[4] + out[8 * j : 8 * j + 8, 128:]
            h_re = n_re
        hre[at, :] = h_re
        him[at, :] = h_im

    @pl.loop(0, number // unroll)
    def _(n):
        for k in range(unroll):
            one(n * unroll + k)

    vr, vi = zv[0], zv[1]
    a_re = hre[pl.ds(7, number, stride=8), :]
    a_im = him[pl.ds(7, number, stride=8), :]
    for k in range(6, -1, -1):
        n_re = a_re * vr - a_im * vi + hre[pl.ds(k, number, stride=8), :]
        a_im = a_re * vi + a_im * vr + him[pl.ds(k, number, stride=8), :]
        a_re = n_re
    cr, ci = cmul(zrow[4], zrow[5], zrow[4], zrow[5])
    m_re, m_im = a_re * cr + a_im * ci, a_im * cr - a_re * ci
    models = jnp.concatenate([m_re, m_im], axis=1).astype(BF16)
    sent = dot(back[...], models)
    interleaved[pl.ds(0, slots, stride=2), :] = sent[:, :128]
    interleaved[pl.ds(1, slots, stride=2), :] = sent[:, 128:]
    along_z, in_plane = refs[: tiles // 4], refs[tiles // 4 : tiles // 4 + 4]
    for r in range(tiles // 4):
        for p in range(4):
            start = pl.multiple_of((mine ^ (4 * r + p)) * (2 * capacity), capacity)
            along_z[r][p] = interleaved[pl.ds(start, capacity), :].astype(BF16)
            in_plane[p][r] = interleaved[pl.ds(start + capacity, capacity), :].astype(BF16)


def turn_kernel(*refs):
    count = refs[0].shape[0]
    blocks, out = refs[:-count], refs[-count:]
    for i, block in enumerate(blocks):
        for j in range(count):
            out[j][i] = block[j]


def residual_kernel(me, observed, *refs):
    arrived, residual = refs[:-1], refs[-1]
    by_z, by_plane = arrived[:-4], arrived[-4:]
    rows = by_plane[0].shape[1]
    for r in range(len(by_z)):
        for p in range(4):
            source = me[0] ^ (4 * r + p)
            residual[source, :rows, :] = observed[source, :rows, :] - by_plane[p][r].astype(F32)
            residual[source, rows:, :] = observed[source, rows:, :] - by_z[r][p].astype(F32)


def exchange(value, step, tiles):
    return lax.ppermute(value, "tile", [(i, i ^ step) for i in range(tiles)])


def per_device(
    subgrids,
    stations,
    time_slots,
    assign,
    counts,
    beam_coefs,
    beam_basis,
    frequencies,
    uv_tracks,
    observed,
):
    tiles = lax.axis_size("tile")
    capacity = assign.shape[2]
    slots = tiles * capacity
    number = subgrids.shape[0]
    pixels = subgrids.shape[2]
    edge = math.isqrt(pixels)
    slot_count = beam_coefs.shape[1]
    terms2 = beam_coefs.shape[2]
    steps = uv_tracks.shape[4]
    chan = frequencies.shape[0]
    vis = steps * chan
    vmem = pl.BlockSpec(memory_space=pltpu.VMEM)
    own_tracks = jnp.transpose(uv_tracks[0], (0, 2, 3, 1)).reshape(tiles, 2 * steps, capacity)
    own_rows = beam_coefs.shape[0] * slot_count
    smem = pl.BlockSpec(memory_space=pltpu.SMEM)
    anywhere = pl.BlockSpec(memory_space=pl.ANY)
    hbm = pl.BlockSpec(memory_space=pltpu.HBM)
    outer = tiles // 4
    me = lax.axis_index("tile").astype(jnp.int32).reshape(1)
    block = jax.ShapeDtypeStruct((2 * own_rows + 12 * steps, 128), BF16)
    packed = pl.pallas_call(
        pack_kernel,
        out_shape=[block] * outer,
        in_specs=[smem, hbm, hbm],
        out_specs=[vmem] * outer,
        scratch_shapes=[
            pltpu.VMEM((own_rows, terms2), BF16),
            pltpu.VMEM((tiles, 2 * steps, capacity), F32),
            pltpu.SemaphoreType.DMA((2,)),
        ],
        compiler_params=pltpu.CompilerParams(vmem_limit_bytes=56 * MIB),
        name="pack",
    )(me, beam_coefs.reshape(own_rows, terms2), own_tracks)
    along = [packed[0]] + [exchange(packed[r], 4 * r, tiles) for r in range(1, outer)]

    cells = jnp.transpose(subgrids.reshape(number, 2, 8, 128), (0, 2, 1, 3))
    cells = cells.reshape(number * 16, 128)
    row_turns, cell_turns = transform_tables(edge)
    image = pl.pallas_call(
        transform_kernel,
        out_shape=jax.ShapeDtypeStruct((8, number, 256), BF16),
        in_specs=[hbm] + [vmem] * 2,
        out_specs=vmem,
        scratch_shapes=[
            pltpu.VMEM((number * 16, 128), BF16),
            pltpu.VMEM((8, 256, 256), BF16),
            pltpu.VMEM((8, 256, 256), BF16),
            pltpu.VMEM((number * 16, 128), F32),
            pltpu.VMEM((8, number, 512), BF16),
            pltpu.SemaphoreType.DMA,
        ],
        compiler_params=pltpu.CompilerParams(vmem_limit_bytes=14 * MIB),
        name="transform",
    )(cells, jnp.asarray(row_turns), jnp.asarray(cell_turns))

    route, back, pick, weights, turns = pl.pallas_call(
        functools.partial(prepare_kernel, slot_count=slot_count),
        out_shape=[
            jax.ShapeDtypeStruct((number, slots), BF16),
            jax.ShapeDtypeStruct((slots, number), BF16),
            jax.ShapeDtypeStruct((2 * number, tiles * own_rows), BF16),
            jax.ShapeDtypeStruct((8, terms2, 256), BF16),
            jax.ShapeDtypeStruct((1, vis), F32),
        ],
        in_specs=[smem] + [vmem] * 5,
        out_specs=[vmem] * 5,
        compiler_params=pltpu.CompilerParams(vmem_limit_bytes=8 * MIB * (1 + tiles // 64)),
        name="prepare",
    )(
        counts,
        assign[0],
        stations.T,
        time_slots.reshape(1, number),
        beam_basis,
        frequencies.reshape(1, chan),
    )

    near = pl.pallas_call(
        stack_kernel,
        out_shape=jax.ShapeDtypeStruct((outer,) + block.shape, BF16),
        in_specs=[vmem] * outer + [anywhere] * 2,
        out_specs=vmem,
        compiler_params=pltpu.CompilerParams(vmem_limit_bytes=2 * MIB * (tiles // 16)),
        name="stack",
    )(*along, image, weights)
    over_y = exchange(near, 2, tiles)
    over_core = exchange(near, 1, tiles)
    over_both = exchange(over_y, 1, tiles)

    for_z = jax.ShapeDtypeStruct((4, capacity, vis), BF16)
    for_plane = jax.ShapeDtypeStruct((outer, capacity, vis), BF16)
    models = pl.pallas_call(
        predict_kernel,
        out_shape=[for_z] * outer + [for_plane] * 4,
        in_specs=[smem] + [vmem] * 10,
        out_specs=[vmem] * (outer + 4),
        scratch_shapes=[
            pltpu.VMEM((tiles * own_rows, terms2), BF16),
            pltpu.VMEM((tiles, 6 * steps, capacity), F32),
            pltpu.VMEM((2 * number, terms2), BF16),
            pltpu.VMEM((number * 8, 128), F32),
            pltpu.VMEM((number * 8, 128), F32),
            pltpu.VMEM((number * 8, vis), F32),
            pltpu.VMEM((number * 8, vis), F32),
            pltpu.VMEM((6, number, vis), F32),
            pltpu.VMEM((number * 8, vis), F32),
            pltpu.VMEM((number * 8, vis), F32),
            pltpu.VMEM((2, number, vis), F32),
            pltpu.VMEM((2 * slots, vis), F32),
        ],
        compiler_params=pltpu.CompilerParams(vmem_limit_bytes=20 * MIB * (1 + tiles // 64)),
        name="predict",
    )(
        me,
        near,
        over_y,
        over_core,
        over_both,
        route,
        back,
        pick,
        weights,
        turns,
        image,
    )
    def turned(blocks, out_shape):
        return pl.pallas_call(
            turn_kernel,
            out_shape=out_shape,
            in_specs=[vmem] * len(blocks),
            out_specs=[vmem] * len(out_shape),
            compiler_params=pltpu.CompilerParams(vmem_limit_bytes=2 * MIB),
            name="turn",
        )(*blocks)

    first, second = models[:outer], models[outer:]
    second = [second[0]] + [exchange(second[p], p, tiles) for p in range(1, 4)]
    first = [first[0]] + [exchange(first[r], 4 * r, tiles) for r in range(1, outer)]
    second = turned(second, [for_z] * outer)
    second = [second[0]] + [exchange(second[r], 4 * r, tiles) for r in range(1, outer)]
    first = turned(first, [for_plane] * 4)
    first = [first[0]] + [exchange(first[p], p, tiles) for p in range(1, 4)]
    residual = pl.pallas_call(
        residual_kernel,
        out_shape=jax.ShapeDtypeStruct((tiles, 2 * capacity, vis), F32),
        in_specs=[smem] + [vmem] * (5 + outer),
        out_specs=vmem,
        compiler_params=pltpu.CompilerParams(vmem_limit_bytes=6 * MIB),
        name="residual",
    )(me, observed.reshape(tiles, 2 * capacity, vis), *second, *first)
    return residual.reshape(observed.shape)


def solution(mesh):
    return jax.shard_map(
        per_device,
        mesh=mesh,
        in_specs=(
            P(("grp", "tile"), None, None),
            P(("grp", "tile"), None),
            P(("grp", "tile")),
            P(("grp", "tile"), None, None),
            P(("grp", "tile"), None),
            P(("grp", "tile"), None, None),
            P(),
            P("grp"),
            P(("grp", "tile"), None, None, None, None),
            P(("grp", "tile"), None, None, None, None),
        ),
        out_specs=P(("grp", "tile"), None, None, None, None),
        check_vma=False,
    )
```

```python
import functools
import math

import jax
import jax.numpy as jnp
import numpy as np
from jax import lax
from jax.experimental import pallas as pl
from jax.experimental.pallas import tpu as pltpu
from jax.sharding import PartitionSpec as P

TWO_PI = 2.0 * math.pi
F32 = jnp.float32
BF16 = jnp.bfloat16
MIB = 1024 * 1024
NT = (((1,), (1,)), ((), ()))


def dot(a, b, dims=(((1,), (0,)), ((), ()))):
    return lax.dot_general(a, b, dims, preferred_element_type=F32)


def transform_tables(edge):
    low = edge // 8
    outer = np.arange(8)[:, None, None, None]
    b = np.arange(low)[None, :, None, None]
    inner = np.arange(low)[None, None, :, None]
    x = np.arange(edge)
    turns = np.broadcast_to(b * (outer + 8 * inner) % edge, (8, low, low, edge))
    rows = TWO_PI / edge * turns.reshape(8, low, low * edge)
    cells = TWO_PI / edge * np.tile(x[:, None] * x[None, :] % edge, (1, low))
    rows = np.stack([np.cos(rows), np.sin(rows)]).astype(np.float32)
    cells = (np.stack([np.cos(cells), np.sin(cells)]) / edge**2).astype(np.float32)
    return rows.reshape(2, 8 * low, low * edge), cells


def eight_point(re, im):
    half = math.sqrt(0.5)

    def four(r, i):
        s0r, s0i, d0r, d0i = r[0] + r[2], i[0] + i[2], r[0] - r[2], i[0] - i[2]
        s1r, s1i, d1r, d1i = r[1] + r[3], i[1] + i[3], r[1] - r[3], i[1] - i[3]
        return (
            [s0r + s1r, d0r - d1i, s0r - s1r, d0r + d1i],
            [s0i + s1i, d0i + d1r, s0i - s1i, d0i - d1r],
        )

    er, ei = four(re[0::2], im[0::2])
    orr, oi = four(re[1::2], im[1::2])
    tr = [orr[0], half * (orr[1] - oi[1]), -oi[2], -half * (orr[3] + oi[3])]
    ti = [oi[0], half * (orr[1] + oi[1]), orr[2], half * (orr[3] - oi[3])]
    out_re = [er[m] + tr[m] for m in range(4)] + [er[m] - tr[m] for m in range(4)]
    out_im = [ei[m] + ti[m] for m in range(4)] + [ei[m] - ti[m] for m in range(4)]
    return out_re, out_im


def transform_kernel(cells_hbm, row_turns, cell_turns, after, image, cells, high, rest, wide, sums, sem):
    copy = pltpu.make_async_copy(cells_hbm, cells, sem)
    copy.start()
    number = image.shape[1]
    edge, span = cell_turns.shape[1:]
    low = span // edge
    cell_c, cell_s = cell_turns[0], cell_turns[1]
    for m in range(8):
        for k in range(low):
            at = m * low + k
            row_c, row_s = row_turns[0, at : at + 1, :], row_turns[1, at : at + 1, :]
            c = row_c * cell_c - row_s * cell_s
            s = row_s * cell_c + row_c * cell_s
            c_top, s_top = c.astype(BF16), s.astype(BF16)
            c_left = (c - c_top.astype(F32)).astype(BF16)
            s_left = (s - s_top.astype(F32)).astype(BF16)
            re = slice(k * edge, (k + 1) * edge)
            im = slice(span + k * edge, span + (k + 1) * edge)
            for held, cos_part, sin_part in ((high, c_top, s_top), (rest, c_left, s_left)):
                held[m, re, :span] = cos_part
                held[m, re, span:] = sin_part
                held[m, im, :span] = -sin_part
                held[m, im, span:] = cos_part
    copy.wait()
    step = 16

    @pl.loop(0, number // step, unroll=2)
    def _(n):
        rows = pl.ds(pl.multiple_of(n * step, step), step)
        span = pl.ds(pl.multiple_of(n * step * 16, step * 16), step * 16)
        wide[span, :] = cells[span, :].astype(F32)
        re = [wide[pl.ds(n * step * 16 + 2 * k, step, stride=16), :] for k in range(8)]
        im = [wide[pl.ds(n * step * 16 + 2 * k + 1, step, stride=16), :] for k in range(8)]
        out_re, out_im = eight_point(re, im)
        for m in range(8):
            value = jnp.concatenate([out_re[m], out_im[m]], axis=1)
            top = value.astype(BF16)
            sums[m, rows, :256] = top
            sums[m, rows, 256:] = (value - top.astype(F32)).astype(BF16)

    for m in range(8):
        both = sums[m]
        left = jnp.concatenate([both, both[:, :256]], axis=1)
        right = jnp.concatenate([high[m], high[m], rest[m]], axis=0)
        image[m] = dot(left, right).astype(BF16)


def prepare_kernel(
    counts, assign, stations, time_slots, basis, freq, route, back, pick, weights, turns, *, slot_count
):
    number = route.shape[0]
    tiles, capacity = assign.shape
    scaled = freq[...] * (-1.0 / 32.0)
    turns[...] = jnp.concatenate([scaled] * (turns.shape[1] // freq.shape[1]), axis=1)

    per = 128 // capacity
    down = lax.broadcasted_iota(jnp.int32, (number, 128), 0)
    slot = lax.broadcasted_iota(jnp.int32, (1, capacity), 1)
    for n in range(tiles // per):
        chosen = [
            jnp.where(slot < counts[0, d], assign[d : d + 1, :], -1)
            for d in range(n * per, (n + 1) * per)
        ]
        hot = (jnp.concatenate(chosen, axis=1) == down).astype(F32)
        route[:, n * 128 : (n + 1) * 128] = hot.astype(BF16)
        back[n * 128 : (n + 1) * 128, :] = hot.T.astype(BF16)

    index = (stations[...] * slot_count + time_slots[...]).astype(F32)
    index = jnp.concatenate([index, jnp.zeros((6, number), F32)], axis=0).T
    index = index.astype(jnp.int32)
    across = lax.broadcasted_iota(jnp.int32, (number, pick.shape[1]), 1)
    for which in range(2):
        hot = (index[:, which : which + 1] == across).astype(F32)
        pick[which * number : (which + 1) * number, :] = hot.astype(BF16)

    terms = basis.shape[1]
    edge = math.isqrt(basis.shape[2])
    for m in range(8):
        starts = [(8 * n + m) * edge for n in range(edge // 8)]
        b_re = jnp.concatenate([basis[0, :, n : n + edge] for n in starts], axis=1)
        b_im = jnp.concatenate([basis[1, :, n : n + edge] for n in starts], axis=1)
        weights[m, :terms, :128] = b_re
        weights[m, :terms, 128:] = b_im
        weights[m, terms:, :128] = -b_im
        weights[m, terms:, 128:] = b_re


def unit_powers(turns):
    turns = turns - jnp.round(turns)
    angle = (0.5 * math.pi) * turns
    sq = angle * angle
    s = angle * (
        1.0 + sq * (-1.0 / 6 + sq * (1.0 / 120 + sq * (-1.0 / 5040 + sq * (1.0 / 362880))))
    )
    c = 1.0 + sq * (
        -0.5 + sq * (1.0 / 24 + sq * (-1.0 / 720 + sq * (1.0 / 40320 - sq * (1.0 / 3628800))))
    )
    for _ in range(2):
        c, s = 1.0 - 2.0 * (s * s), 2.0 * (s * c)
    return c, s


def cmul(ar, ai, br, bi):
    return ar * br - ai * bi, ar * bi + ai * br


def pack_kernel(me, coefs_hbm, tracks_hbm, *refs):
    out, (coefs, tracks, sems) = refs[:-3], refs[-3:]
    copies = [
        pltpu.make_async_copy(coefs_hbm, coefs, sems.at[0]),
        pltpu.make_async_copy(tracks_hbm, tracks, sems.at[1]),
    ]
    for copy in copies:
        copy.start()
    for copy in copies:
        copy.wait()
    capacity = tracks.shape[2]
    rows = coefs.shape[0]
    for r in range(len(out)):
        plane = (me[0] // 4) ^ r
        kept = []
        for k in (0, 2):
            tr = jnp.concatenate([tracks[plane * 4 + k], tracks[plane * 4 + k + 1]], axis=1)
            t_hi = tr.astype(BF16).astype(F32)
            t_mid = (tr - t_hi).astype(BF16).astype(F32)
            kept += [t_hi, t_mid, tr - t_hi - t_mid]
        pieces = jnp.concatenate(kept, axis=0)
        if 2 * capacity < 128:
            blank = jnp.zeros((pieces.shape[0], 128 - 2 * capacity), F32)
            pieces = jnp.concatenate([pieces, blank], axis=1)
        out[r][:rows, :] = coefs[:, :128]
        out[r][rows : 2 * rows, :] = coefs[:, 128:]
        out[r][2 * rows :, :] = pieces.astype(BF16)


def stack_kernel(*refs):
    blocks, out = refs[:-2], refs[-1]
    for r, block in enumerate(blocks[::-1]):
        out[r] = block[...]


def relay_kernel(block, after, out):
    out[...] = block[...]


def predict_kernel(
    me,
    near,
    over_y,
    over_core,
    over_both,
    route,
    back,
    pick,
    weights,
    turns,
    image,
    *refs,
):
    table, lanes, coef, wre, wim, pure, puim, zrow, hre, him, zv, interleaved = refs[-12:]
    number = image.shape[1]
    tiles, kinds3, capacity = lanes.shape
    slots = tiles * capacity
    rows_own = table.shape[0] // tiles
    vis = turns.shape[1]
    kinds = kinds3 // 3
    steps = kinds // 2
    chan = vis // steps
    mine = me[0]

    for arrived, flip in ((near, 0), (over_y, 2), (over_core, 1), (over_both, 3)):
        for r in range(arrived.shape[0]):
            owner = mine ^ (4 * r + flip)
            at = pl.ds(pl.multiple_of(owner * rows_own, rows_own), rows_own)
            table[at, :128] = arrived[r, :rows_own, :]
            table[at, 128:] = arrived[r, rows_own : 2 * rows_own, :]
            piece = arrived[r, 2 * rows_own :, :].astype(F32)
            piece = jnp.where(mine & 2 == 0, piece[:kinds3, :], piece[kinds3:, :])
            moved = jnp.where(mine & 1 == 0, piece, pltpu.roll(piece, 128 - capacity, 1))
            lanes[owner] = moved[:, :capacity]
    per = 128 // capacity
    pieces = jnp.concatenate(
        [
            jnp.concatenate([lanes[d] for d in range(n * per, (n + 1) * per)], axis=1)
            for n in range(tiles // per)
        ],
        axis=1,
    )
    pieces = jnp.concatenate([pieces, jnp.zeros((kinds, slots), F32)], axis=0).astype(BF16)

    per_sub = dot(route[...], pieces, NT).astype(BF16)
    wide = 2 * steps * chan
    from_row = lax.broadcasted_iota(jnp.int32, (4 * kinds, wide), 0) % kinds
    to_lane = lax.broadcasted_iota(jnp.int32, (4 * kinds, wide), 1) // chan
    spread = (from_row == to_lane).astype(F32).astype(BF16)
    uv = dot(per_sub, spread)
    ur, ui = unit_powers(uv[:, :vis] * turns[...])
    vr, vi = unit_powers(uv[:, vis:] * turns[...])

    pure[pl.ds(0, number, stride=8), :] = jnp.ones_like(ur)
    puim[pl.ds(0, number, stride=8), :] = jnp.zeros_like(ur)
    pure[pl.ds(1, number, stride=8), :] = ur
    puim[pl.ds(1, number, stride=8), :] = ui
    cr, ci = ur, ui
    for k in range(2, 8):
        cr, ci = cmul(cr, ci, ur, ui)
        pure[pl.ds(k, number, stride=8), :] = cr
        puim[pl.ds(k, number, stride=8), :] = ci
    cr, ci = cmul(cr, ci, ur, ui)
    zrow[0] = cr
    zrow[1] = ci
    cr, ci = cmul(cr, ci, cr, ci)
    zrow[2] = cr
    zrow[3] = ci
    zv[0] = vr
    zv[1] = vi
    cr, ci = vr, vi
    for _ in range(3):
        cr, ci = cmul(cr, ci, cr, ci)
    zrow[4] = cr
    zrow[5] = ci

    coef[...] = dot(pick[...], table[...]).astype(BF16)

    block = 32
    for m in range(8):
        beams = dot(coef[...], weights[m])
        for n in range(0, number, block):
            first = beams[n : n + block, :]
            second = beams[number + n : number + n + block, :]
            f_re, f_im, s_re, s_im = first[:, :128], first[:, 128:], second[:, :128], second[:, 128:]
            g_re = f_re * s_re + f_im * s_im
            g_im = f_im * s_re - f_re * s_im
            i_re = image[m, n : n + block, :128].astype(F32)
            i_im = image[m, n : n + block, 128:].astype(F32)
            to = pl.ds(n * 8 + m, block, stride=8)
            wre[to, :] = i_re * g_re - i_im * g_im
            wim[to, :] = i_re * g_im + i_im * g_re

    unroll = 32

    def one(g):
        at = pl.ds(pl.multiple_of(g * 8, 8), 8)
        w_re, w_im = wre[at, :], wim[at, :]
        lhs = [
            jnp.concatenate([w_re[:, n : n + 32], w_im[:, n : n + 32]], axis=1)
            for n in range(0, 128, 32)
        ]
        lhs = jnp.concatenate(lhs, axis=0).astype(BF16)
        p_re, p_im = pure[at, :], puim[at, :]
        z = [jnp.broadcast_to(zrow[k, pl.ds(g, 1), :], (8, 128)) for k in range(6)]
        rr, ii, ri, ir = p_re * z[0], p_im * z[1], p_re * z[1], p_im * z[0]
        up_re, up_im = rr - ii, ri + ir
        dn_re, dn_im = rr + ii, ir - ri
        rr, ii, ri, ir = p_re * z[2], p_im * z[3], p_re * z[3], p_im * z[2]
        lo_re, lo_im = rr + ii, ir - ri
        c = jnp.concatenate([lo_re, dn_re, p_re, up_re], axis=0).astype(BF16)
        s = jnp.concatenate([lo_im, dn_im, p_im, up_im], axis=0).astype(BF16)
        top = jnp.concatenate([c, s], axis=1)
        low = jnp.concatenate([-s, c], axis=1)
        rhs = jnp.concatenate([top, low], axis=0)
        out = dot(lhs, rhs)
        h_re, h_im = out[24:32, :128], out[24:32, 128:]
        for j in (2, 1, 0):
            n_re = h_re * z[4] - h_im * z[5] + out[8 * j : 8 * j + 8, :128]
            h_im = h_re * z[5] + h_im * z[4] + out[8 * j : 8 * j + 8, 128:]
            h_re = n_re
        hre[at, :] = h_re
        him[at, :] = h_im

    @pl.loop(0, number // unroll)
    def _(n):
        for k in range(unroll):
            one(n * unroll + k)

    vr, vi = zv[0], zv[1]
    a_re = hre[pl.ds(7, number, stride=8), :]
    a_im = him[pl.ds(7, number, stride=8), :]
    for k in range(6, -1, -1):
        n_re = a_re * vr - a_im * vi + hre[pl.ds(k, number, stride=8), :]
        a_im = a_re * vi + a_im * vr + him[pl.ds(k, number, stride=8), :]
        a_re = n_re
    cr, ci = cmul(zrow[4], zrow[5], zrow[4], zrow[5])
    m_re, m_im = a_re * cr + a_im * ci, a_im * cr - a_re * ci
    models = jnp.concatenate([m_re, m_im], axis=1).astype(BF16)
    sent = dot(back[...], models)
    interleaved[pl.ds(0, slots, stride=2), :] = sent[:, :128]
    interleaved[pl.ds(1, slots, stride=2), :] = sent[:, 128:]
    along_z, in_plane = refs[: tiles // 4], refs[tiles // 4 : tiles // 4 + 4]
    for r in range(tiles // 4):
        for p in range(4):
            start = pl.multiple_of((mine ^ (4 * r + p)) * (2 * capacity), capacity)
            along_z[r][p] = interleaved[pl.ds(start, capacity), :].astype(BF16)
            in_plane[p][r] = interleaved[pl.ds(start + capacity, capacity), :].astype(BF16)


def turn_kernel(*refs):
    count = refs[0].shape[0]
    blocks, out = refs[:-count], refs[-count:]
    for i, block in enumerate(blocks[::-1]):
        for j in range(count):
            out[j][i] = block[j]


def residual_kernel(me, observed, *refs):
    arrived, residual = refs[:-1], refs[-1]
    by_z, by_plane = arrived[:-4][::-1], arrived[-4:]
    rows = by_plane[0].shape[1]
    for r in range(len(by_z)):
        for p in range(4):
            source = me[0] ^ (4 * r + p)
            residual[source, :rows, :] = observed[source, :rows, :] - by_plane[p][r].astype(F32)
            residual[source, rows:, :] = observed[source, rows:, :] - by_z[r][p].astype(F32)


def exchange(value, step, tiles):
    return lax.ppermute(value, "tile", [(i, i ^ step) for i in range(tiles)])


def per_device(
    subgrids,
    stations,
    time_slots,
    assign,
    counts,
    beam_coefs,
    beam_basis,
    frequencies,
    uv_tracks,
    observed,
):
    tiles = lax.axis_size("tile")
    capacity = assign.shape[2]
    slots = tiles * capacity
    number = subgrids.shape[0]
    pixels = subgrids.shape[2]
    edge = math.isqrt(pixels)
    slot_count = beam_coefs.shape[1]
    terms2 = beam_coefs.shape[2]
    steps = uv_tracks.shape[4]
    chan = frequencies.shape[0]
    vis = steps * chan
    vmem = pl.BlockSpec(memory_space=pltpu.VMEM)
    own_tracks = jnp.transpose(uv_tracks[0], (0, 2, 3, 1)).reshape(tiles, 2 * steps, capacity)
    own_rows = beam_coefs.shape[0] * slot_count
    smem = pl.BlockSpec(memory_space=pltpu.SMEM)
    anywhere = pl.BlockSpec(memory_space=pl.ANY)
    hbm = pl.BlockSpec(memory_space=pltpu.HBM)
    outer = tiles // 4
    me = lax.axis_index("tile").astype(jnp.int32).reshape(1)
    block = jax.ShapeDtypeStruct((2 * own_rows + 12 * steps, 128), BF16)
    packed = pl.pallas_call(
        pack_kernel,
        out_shape=[block] * outer,
        in_specs=[smem, hbm, hbm],
        out_specs=[vmem] * outer,
        scratch_shapes=[
            pltpu.VMEM((own_rows, terms2), BF16),
            pltpu.VMEM((tiles, 2 * steps, capacity), F32),
            pltpu.SemaphoreType.DMA((2,)),
        ],
        compiler_params=pltpu.CompilerParams(vmem_limit_bytes=56 * MIB),
        name="pack",
    )(me, beam_coefs.reshape(own_rows, terms2), own_tracks)
    along = [packed[0]] + [exchange(packed[r], 4 * r, tiles) for r in range(1, outer)]

    route, back, pick, weights, turns = pl.pallas_call(
        functools.partial(prepare_kernel, slot_count=slot_count),
        out_shape=[
            jax.ShapeDtypeStruct((number, slots), BF16),
            jax.ShapeDtypeStruct((slots, number), BF16),
            jax.ShapeDtypeStruct((2 * number, tiles * own_rows), BF16),
            jax.ShapeDtypeStruct((8, terms2, 256), BF16),
            jax.ShapeDtypeStruct((1, vis), F32),
        ],
        in_specs=[smem] + [vmem] * 5,
        out_specs=[vmem] * 5,
        compiler_params=pltpu.CompilerParams(vmem_limit_bytes=8 * MIB * (1 + tiles // 64)),
        name="prepare",
    )(
        counts,
        assign[0],
        stations.T,
        time_slots.reshape(1, number),
        beam_basis,
        frequencies.reshape(1, chan),
    )

    near = pl.pallas_call(
        stack_kernel,
        out_shape=jax.ShapeDtypeStruct((outer,) + block.shape, BF16),
        in_specs=[vmem] * outer + [anywhere],
        out_specs=vmem,
        compiler_params=pltpu.CompilerParams(vmem_limit_bytes=2 * MIB * (tiles // 16)),
        name="stack",
    )(*along[::-1], weights)
    over_core = exchange(near, 1, tiles)
    over_y = exchange(near, 2, tiles)
    cells = jnp.transpose(subgrids.reshape(number, 2, 8, 128), (0, 2, 1, 3))
    cells = cells.reshape(number * 16, 128)
    row_turns, cell_turns = transform_tables(edge)
    image = pl.pallas_call(
        transform_kernel,
        out_shape=jax.ShapeDtypeStruct((8, number, 256), BF16),
        in_specs=[hbm] + [vmem] * 2 + [anywhere],
        out_specs=vmem,
        scratch_shapes=[
            pltpu.VMEM((number * 16, 128), BF16),
            pltpu.VMEM((8, 256, 256), BF16),
            pltpu.VMEM((8, 256, 256), BF16),
            pltpu.VMEM((number * 16, 128), F32),
            pltpu.VMEM((8, number, 512), BF16),
            pltpu.SemaphoreType.DMA,
        ],
        compiler_params=pltpu.CompilerParams(vmem_limit_bytes=14 * MIB),
        name="transform",
    )(cells, jnp.asarray(row_turns), jnp.asarray(cell_turns), near)

    over_both = pl.pallas_call(
        relay_kernel,
        out_shape=jax.ShapeDtypeStruct(over_y.shape, BF16),
        in_specs=[vmem, anywhere],
        out_specs=vmem,
        compiler_params=pltpu.CompilerParams(vmem_limit_bytes=2 * MIB * (tiles // 16)),
        name="relay",
    )(over_y, image)
    over_both = exchange(over_both, 1, tiles)

    for_z = jax.ShapeDtypeStruct((4, capacity, vis), BF16)
    for_plane = jax.ShapeDtypeStruct((outer, capacity, vis), BF16)
    models = pl.pallas_call(
        predict_kernel,
        out_shape=[for_z] * outer + [for_plane] * 4,
        in_specs=[smem] + [vmem] * 10,
        out_specs=[vmem] * (outer + 4),
        scratch_shapes=[
            pltpu.VMEM((tiles * own_rows, terms2), BF16),
            pltpu.VMEM((tiles, 6 * steps, capacity), F32),
            pltpu.VMEM((2 * number, terms2), BF16),
            pltpu.VMEM((number * 8, 128), F32),
            pltpu.VMEM((number * 8, 128), F32),
            pltpu.VMEM((number * 8, vis), F32),
            pltpu.VMEM((number * 8, vis), F32),
            pltpu.VMEM((6, number, vis), F32),
            pltpu.VMEM((number * 8, vis), F32),
            pltpu.VMEM((number * 8, vis), F32),
            pltpu.VMEM((2, number, vis), F32),
            pltpu.VMEM((2 * slots, vis), F32),
        ],
        compiler_params=pltpu.CompilerParams(vmem_limit_bytes=20 * MIB * (1 + tiles // 64)),
        name="predict",
    )(
        me,
        near,
        over_y,
        over_core,
        over_both,
        route,
        back,
        pick,
        weights,
        turns,
        image,
    )
    def turned(blocks, out_shape):
        return pl.pallas_call(
            turn_kernel,
            out_shape=out_shape,
            in_specs=[vmem] * len(blocks),
            out_specs=[vmem] * len(out_shape),
            compiler_params=pltpu.CompilerParams(vmem_limit_bytes=2 * MIB),
            name="turn",
        )(*blocks[::-1])

    first, second = models[:outer], models[outer:]
    second = [second[0]] + [exchange(second[p], p, tiles) for p in range(1, 4)]
    first = [first[0]] + [exchange(first[r], 4 * r, tiles) for r in range(1, outer)]
    second = turned(second, [for_z] * outer)
    second = [second[0]] + [exchange(second[r], 4 * r, tiles) for r in range(1, outer)]
    first = turned(first, [for_plane] * 4)
    first = [first[0]] + [exchange(first[p], p, tiles) for p in range(1, 4)]
    residual = pl.pallas_call(
        residual_kernel,
        out_shape=jax.ShapeDtypeStruct((tiles, 2 * capacity, vis), F32),
        in_specs=[smem] + [vmem] * (5 + outer),
        out_specs=vmem,
        compiler_params=pltpu.CompilerParams(vmem_limit_bytes=6 * MIB),
        name="residual",
    )(me, observed.reshape(tiles, 2 * capacity, vis), *second[::-1], *first)
    return residual.reshape(observed.shape)


def solution(mesh):
    return jax.shard_map(
        per_device,
        mesh=mesh,
        in_specs=(
            P(("grp", "tile"), None, None),
            P(("grp", "tile"), None),
            P(("grp", "tile")),
            P(("grp", "tile"), None, None),
            P(("grp", "tile"), None),
            P(("grp", "tile"), None, None),
            P(),
            P("grp"),
            P(("grp", "tile"), None, None, None, None),
            P(("grp", "tile"), None, None, None, None),
        ),
        out_specs=P(("grp", "tile"), None, None, None, None),
        check_vma=False,
    )
```

```python
import functools
import math

import jax
import jax.numpy as jnp
import numpy as np
from jax import lax
from jax.experimental import pallas as pl
from jax.experimental.pallas import tpu as pltpu
from jax.sharding import PartitionSpec as P

TWO_PI = 2.0 * math.pi
F32 = jnp.float32
BF16 = jnp.bfloat16
MIB = 1024 * 1024
NT = (((1,), (1,)), ((), ()))


def dot(a, b, dims=(((1,), (0,)), ((), ()))):
    return lax.dot_general(a, b, dims, preferred_element_type=F32)


def transform_tables(edge):
    low = edge // 8
    outer = np.arange(8)[:, None, None, None]
    b = np.arange(low)[None, :, None, None]
    inner = np.arange(low)[None, None, :, None]
    x = np.arange(edge)
    turns = np.broadcast_to(b * (outer + 8 * inner) % edge, (8, low, low, edge))
    rows = TWO_PI / edge * turns.reshape(8, low, low * edge)
    cells = TWO_PI / edge * np.tile(x[:, None] * x[None, :] % edge, (1, low))
    rows = np.stack([np.cos(rows), np.sin(rows)]).astype(np.float32)
    cells = (np.stack([np.cos(cells), np.sin(cells)]) / edge**2).astype(np.float32)
    return rows.reshape(2, 8 * low, low * edge), cells


def eight_point(re, im):
    half = math.sqrt(0.5)

    def four(r, i):
        s0r, s0i, d0r, d0i = r[0] + r[2], i[0] + i[2], r[0] - r[2], i[0] - i[2]
        s1r, s1i, d1r, d1i = r[1] + r[3], i[1] + i[3], r[1] - r[3], i[1] - i[3]
        return (
            [s0r + s1r, d0r - d1i, s0r - s1r, d0r + d1i],
            [s0i + s1i, d0i + d1r, s0i - s1i, d0i - d1r],
        )

    er, ei = four(re[0::2], im[0::2])
    orr, oi = four(re[1::2], im[1::2])
    tr = [orr[0], half * (orr[1] - oi[1]), -oi[2], -half * (orr[3] + oi[3])]
    ti = [oi[0], half * (orr[1] + oi[1]), orr[2], half * (orr[3] - oi[3])]
    out_re = [er[m] + tr[m] for m in range(4)] + [er[m] - tr[m] for m in range(4)]
    out_im = [ei[m] + ti[m] for m in range(4)] + [ei[m] - ti[m] for m in range(4)]
    return out_re, out_im


def transform_kernel(cells_hbm, row_turns, cell_turns, image, cells, high, rest, wide, sums, sem):
    copy = pltpu.make_async_copy(cells_hbm, cells, sem)
    copy.start()
    number = image.shape[1]
    edge, span = cell_turns.shape[1:]
    low = span // edge
    cell_c, cell_s = cell_turns[0], cell_turns[1]
    for m in range(8):
        for k in range(low):
            at = m * low + k
            row_c, row_s = row_turns[0, at : at + 1, :], row_turns[1, at : at + 1, :]
            c = row_c * cell_c - row_s * cell_s
            s = row_s * cell_c + row_c * cell_s
            c_top, s_top = c.astype(BF16), s.astype(BF16)
            c_left = (c - c_top.astype(F32)).astype(BF16)
            s_left = (s - s_top.astype(F32)).astype(BF16)
            re = slice(k * edge, (k + 1) * edge)
            im = slice(span + k * edge, span + (k + 1) * edge)
            for held, cos_part, sin_part in ((high, c_top, s_top), (rest, c_left, s_left)):
                held[m, re, :span] = cos_part
                held[m, re, span:] = sin_part
                held[m, im, :span] = -sin_part
                held[m, im, span:] = cos_part
    copy.wait()
    step = 16

    @pl.loop(0, number // step, unroll=8)
    def _(n):
        rows = pl.ds(pl.multiple_of(n * step, step), step)
        span = pl.ds(pl.multiple_of(n * step * 16, step * 16), step * 16)
        wide[span, :] = cells[span, :].astype(F32)
        re = [wide[pl.ds(n * step * 16 + 2 * k, step, stride=16), :] for k in range(8)]
        im = [wide[pl.ds(n * step * 16 + 2 * k + 1, step, stride=16), :] for k in range(8)]
        out_re, out_im = eight_point(re, im)
        for m in range(8):
            value = jnp.concatenate([out_re[m], out_im[m]], axis=1)
            top = value.astype(BF16)
            sums[m, rows, :256] = top
            sums[m, rows, 256:] = (value - top.astype(F32)).astype(BF16)

    for m in range(8):
        both = sums[m]
        left = jnp.concatenate([both, both[:, :256]], axis=1)
        right = jnp.concatenate([high[m], high[m], rest[m]], axis=0)
        image[m] = dot(left, right).astype(BF16)


def prepare_kernel(
    counts, assign, stations, time_slots, basis, freq, after, route, back, pick, weights, turns, *, slot_count
):
    number = route.shape[0]
    tiles, capacity = assign.shape
    scaled = freq[...] * (-1.0 / 32.0)
    turns[...] = jnp.concatenate([scaled] * (turns.shape[1] // freq.shape[1]), axis=1)

    per = 128 // capacity
    down = lax.broadcasted_iota(jnp.int32, (number, 128), 0)
    slot = lax.broadcasted_iota(jnp.int32, (1, capacity), 1)
    for n in range(tiles // per):
        chosen = [
            jnp.where(slot < counts[0, d], assign[d : d + 1, :], -1)
            for d in range(n * per, (n + 1) * per)
        ]
        hot = (jnp.concatenate(chosen, axis=1) == down).astype(F32)
        route[:, n * 128 : (n + 1) * 128] = hot.astype(BF16)
        back[n * 128 : (n + 1) * 128, :] = hot.T.astype(BF16)

    index = (stations[...] * slot_count + time_slots[...]).astype(F32)
    index = jnp.concatenate([index, jnp.zeros((6, number), F32)], axis=0).T
    index = index.astype(jnp.int32)
    across = lax.broadcasted_iota(jnp.int32, (number, pick.shape[1]), 1)
    for which in range(2):
        hot = (index[:, which : which + 1] == across).astype(F32)
        pick[which * number : (which + 1) * number, :] = hot.astype(BF16)

    terms = basis.shape[1]
    edge = math.isqrt(basis.shape[2])
    for m in range(8):
        starts = [(8 * n + m) * edge for n in range(edge // 8)]
        b_re = jnp.concatenate([basis[0, :, n : n + edge] for n in starts], axis=1)
        b_im = jnp.concatenate([basis[1, :, n : n + edge] for n in starts], axis=1)
        weights[m, :terms, :128] = b_re
        weights[m, :terms, 128:] = b_im
        weights[m, terms:, :128] = -b_im
        weights[m, terms:, 128:] = b_re


def unit_powers(turns):
    turns = turns - jnp.round(turns)
    angle = (0.5 * math.pi) * turns
    sq = angle * angle
    s = angle * (
        1.0 + sq * (-1.0 / 6 + sq * (1.0 / 120 + sq * (-1.0 / 5040 + sq * (1.0 / 362880))))
    )
    c = 1.0 + sq * (
        -0.5 + sq * (1.0 / 24 + sq * (-1.0 / 720 + sq * (1.0 / 40320 - sq * (1.0 / 3628800))))
    )
    for _ in range(2):
        c, s = 1.0 - 2.0 * (s * s), 2.0 * (s * c)
    return c, s


def cmul(ar, ai, br, bi):
    return ar * br - ai * bi, ar * bi + ai * br


def pack_kernel(me, coefs_hbm, tracks_hbm, *refs):
    out, (coefs, tracks, sems) = refs[:-3], refs[-3:]
    copies = [
        pltpu.make_async_copy(coefs_hbm, coefs, sems.at[0]),
        pltpu.make_async_copy(tracks_hbm, tracks, sems.at[1]),
    ]
    for copy in copies:
        copy.start()
    for copy in copies:
        copy.wait()
    capacity = tracks.shape[2]
    rows = coefs.shape[0]
    for r in range(len(out)):
        plane = (me[0] // 4) ^ r
        kept = []
        for k in (0, 2):
            tr = jnp.concatenate([tracks[plane * 4 + k], tracks[plane * 4 + k + 1]], axis=1)
            t_hi = tr.astype(BF16).astype(F32)
            t_mid = (tr - t_hi).astype(BF16).astype(F32)
            kept += [t_hi, t_mid, tr - t_hi - t_mid]
        pieces = jnp.concatenate(kept, axis=0)
        if 2 * capacity < 128:
            blank = jnp.zeros((pieces.shape[0], 128 - 2 * capacity), F32)
            pieces = jnp.concatenate([pieces, blank], axis=1)
        out[r][:rows, :] = coefs[:, :128]
        out[r][rows : 2 * rows, :] = coefs[:, 128:]
        out[r][2 * rows :, :] = pieces.astype(BF16)


def stack_kernel(me, *refs):
    blocks, near, for_y = refs[:-3], refs[-2], refs[-1]
    pair = near.shape[1] - for_y.shape[1]
    table = for_y.shape[1] - pair
    for r, block in enumerate(blocks[::-1]):
        near[r] = block[...]
        tracks = block[table:, :].astype(F32)
        tracks = jnp.where(me[0] & 2 == 0, tracks[pair:, :], tracks[:pair, :])
        for_y[r, :table, :] = block[:table, :]
        for_y[r, table:, :] = tracks.astype(BF16)


def relay_kernel(block, after, out):
    out[...] = block[...]


def predict_kernel(
    me,
    near,
    over_y,
    over_core,
    over_both,
    route,
    back,
    pick,
    weights,
    turns,
    image,
    *refs,
):
    table, lanes, coef, wre, wim, pure, puim, zrow, hre, him, zv, interleaved = refs[-12:]
    number = image.shape[1]
    tiles, kinds3, capacity = lanes.shape
    slots = tiles * capacity
    rows_own = table.shape[0] // tiles
    vis = turns.shape[1]
    kinds = kinds3 // 3
    steps = kinds // 2
    chan = vis // steps
    mine = me[0]

    for arrived, flip in ((near, 0), (over_y, 2), (over_core, 1), (over_both, 3)):
        for r in range(arrived.shape[0]):
            owner = mine ^ (4 * r + flip)
            at = pl.ds(pl.multiple_of(owner * rows_own, rows_own), rows_own)
            table[at, :128] = arrived[r, :rows_own, :]
            table[at, 128:] = arrived[r, rows_own : 2 * rows_own, :]
            piece = arrived[r, 2 * rows_own :, :].astype(F32)
            if piece.shape[0] > kinds3:
                piece = jnp.where(mine & 2 == 0, piece[:kinds3, :], piece[kinds3:, :])
            moved = jnp.where(mine & 1 == 0, piece, pltpu.roll(piece, 128 - capacity, 1))
            lanes[owner] = moved[:, :capacity]
    per = 128 // capacity
    pieces = jnp.concatenate(
        [
            jnp.concatenate([lanes[d] for d in range(n * per, (n + 1) * per)], axis=1)
            for n in range(tiles // per)
        ],
        axis=1,
    )
    pieces = jnp.concatenate([pieces, jnp.zeros((kinds, slots), F32)], axis=0).astype(BF16)

    per_sub = dot(route[...], pieces, NT).astype(BF16)
    wide = 2 * steps * chan
    from_row = lax.broadcasted_iota(jnp.int32, (4 * kinds, wide), 0) % kinds
    to_lane = lax.broadcasted_iota(jnp.int32, (4 * kinds, wide), 1) // chan
    spread = (from_row == to_lane).astype(F32).astype(BF16)
    uv = dot(per_sub, spread)
    ur, ui = unit_powers(uv[:, :vis] * turns[...])
    vr, vi = unit_powers(uv[:, vis:] * turns[...])

    pure[pl.ds(0, number, stride=8), :] = jnp.ones_like(ur)
    puim[pl.ds(0, number, stride=8), :] = jnp.zeros_like(ur)
    pure[pl.ds(1, number, stride=8), :] = ur
    puim[pl.ds(1, number, stride=8), :] = ui
    cr, ci = ur, ui
    for k in range(2, 8):
        cr, ci = cmul(cr, ci, ur, ui)
        pure[pl.ds(k, number, stride=8), :] = cr
        puim[pl.ds(k, number, stride=8), :] = ci
    cr, ci = cmul(cr, ci, ur, ui)
    zrow[0] = cr
    zrow[1] = ci
    cr, ci = cmul(cr, ci, cr, ci)
    zrow[2] = cr
    zrow[3] = ci
    zv[0] = vr
    zv[1] = vi
    cr, ci = vr, vi
    for _ in range(3):
        cr, ci = cmul(cr, ci, cr, ci)
    zrow[4] = cr
    zrow[5] = ci

    coef[...] = dot(pick[...], table[...]).astype(BF16)

    block = 32
    for m in range(8):
        beams = dot(coef[...], weights[m])
        for n in range(0, number, block):
            first = beams[n : n + block, :]
            second = beams[number + n : number + n + block, :]
            f_re, f_im, s_re, s_im = first[:, :128], first[:, 128:], second[:, :128], second[:, 128:]
            g_re = f_re * s_re + f_im * s_im
            g_im = f_im * s_re - f_re * s_im
            i_re = image[m, n : n + block, :128].astype(F32)
            i_im = image[m, n : n + block, 128:].astype(F32)
            to = pl.ds(n * 8 + m, block, stride=8)
            wre[to, :] = i_re * g_re - i_im * g_im
            wim[to, :] = i_re * g_im + i_im * g_re

    unroll = 64

    def one(g):
        at = pl.ds(pl.multiple_of(g * 8, 8), 8)
        w_re, w_im = wre[at, :], wim[at, :]
        lhs = [
            jnp.concatenate([w_re[:, n : n + 32], w_im[:, n : n + 32]], axis=1)
            for n in range(0, 128, 32)
        ]
        lhs = jnp.concatenate(lhs, axis=0).astype(BF16)
        p_re, p_im = pure[at, :], puim[at, :]
        z = [jnp.broadcast_to(zrow[k, pl.ds(g, 1), :], (8, 128)) for k in range(6)]
        rr, ii, ri, ir = p_re * z[0], p_im * z[1], p_re * z[1], p_im * z[0]
        up_re, up_im = rr - ii, ri + ir
        dn_re, dn_im = rr + ii, ir - ri
        rr, ii, ri, ir = p_re * z[2], p_im * z[3], p_re * z[3], p_im * z[2]
        lo_re, lo_im = rr + ii, ir - ri
        c = jnp.concatenate([lo_re, dn_re, p_re, up_re], axis=0).astype(BF16)
        s = jnp.concatenate([lo_im, dn_im, p_im, up_im], axis=0).astype(BF16)
        top = jnp.concatenate([c, s], axis=1)
        low = jnp.concatenate([-s, c], axis=1)
        rhs = jnp.concatenate([top, low], axis=0)
        out = dot(lhs, rhs)
        h_re, h_im = out[24:32, :128], out[24:32, 128:]
        for j in (2, 1, 0):
            n_re = h_re * z[4] - h_im * z[5] + out[8 * j : 8 * j + 8, :128]
            h_im = h_re * z[5] + h_im * z[4] + out[8 * j : 8 * j + 8, 128:]
            h_re = n_re
        hre[at, :] = h_re
        him[at, :] = h_im

    @pl.loop(0, number // unroll)
    def _(n):
        for k in range(unroll):
            one(n * unroll + k)

    vr, vi = zv[0], zv[1]
    a_re = hre[pl.ds(7, number, stride=8), :]
    a_im = him[pl.ds(7, number, stride=8), :]
    for k in range(6, -1, -1):
        n_re = a_re * vr - a_im * vi + hre[pl.ds(k, number, stride=8), :]
        a_im = a_re * vi + a_im * vr + him[pl.ds(k, number, stride=8), :]
        a_re = n_re
    cr, ci = cmul(zrow[4], zrow[5], zrow[4], zrow[5])
    m_re, m_im = a_re * cr + a_im * ci, a_im * cr - a_re * ci
    models = jnp.concatenate([m_re, m_im], axis=1).astype(BF16)
    sent = dot(back[...], models)
    interleaved[pl.ds(0, slots, stride=2), :] = sent[:, :128]
    interleaved[pl.ds(1, slots, stride=2), :] = sent[:, 128:]
    along_z, in_plane = refs[: tiles // 4], refs[tiles // 4 : tiles // 4 + 4]
    for r in range(tiles // 4):
        for p in range(4):
            start = pl.multiple_of((mine ^ (4 * r + p)) * (2 * capacity), capacity)
            along_z[r][p] = interleaved[pl.ds(start, capacity), :].astype(BF16)
            in_plane[p][r] = interleaved[pl.ds(start + capacity, capacity), :].astype(BF16)


def turn_kernel(*refs):
    count = refs[0].shape[0]
    blocks, out = refs[:-count], refs[-count:]
    for i, block in enumerate(blocks[::-1]):
        for j in range(count):
            out[j][i] = block[j]


def residual_kernel(me, observed, *refs):
    arrived, residual = refs[:-1], refs[-1]
    by_z, by_plane = arrived[:-4][::-1], arrived[-4:]
    rows = by_plane[0].shape[1]
    for r in range(len(by_z)):
        for p in range(4):
            source = me[0] ^ (4 * r + p)
            residual[source, :rows, :] = observed[source, :rows, :] - by_plane[p][r].astype(F32)
            residual[source, rows:, :] = observed[source, rows:, :] - by_z[r][p].astype(F32)


def exchange(value, step, tiles):
    return lax.ppermute(value, "tile", [(i, i ^ step) for i in range(tiles)])


def per_device(
    subgrids,
    stations,
    time_slots,
    assign,
    counts,
    beam_coefs,
    beam_basis,
    frequencies,
    uv_tracks,
    observed,
):
    tiles = lax.axis_size("tile")
    capacity = assign.shape[2]
    slots = tiles * capacity
    number = subgrids.shape[0]
    pixels = subgrids.shape[2]
    edge = math.isqrt(pixels)
    slot_count = beam_coefs.shape[1]
    terms2 = beam_coefs.shape[2]
    steps = uv_tracks.shape[4]
    chan = frequencies.shape[0]
    vis = steps * chan
    vmem = pl.BlockSpec(memory_space=pltpu.VMEM)
    own_tracks = jnp.transpose(uv_tracks[0], (0, 2, 3, 1)).reshape(tiles, 2 * steps, capacity)
    own_rows = beam_coefs.shape[0] * slot_count
    smem = pl.BlockSpec(memory_space=pltpu.SMEM)
    anywhere = pl.BlockSpec(memory_space=pl.ANY)
    hbm = pl.BlockSpec(memory_space=pltpu.HBM)
    outer = tiles // 4
    me = lax.axis_index("tile").astype(jnp.int32).reshape(1)
    block = jax.ShapeDtypeStruct((2 * own_rows + 12 * steps, 128), BF16)
    packed = pl.pallas_call(
        pack_kernel,
        out_shape=[block] * outer,
        in_specs=[smem, hbm, hbm],
        out_specs=[vmem] * outer,
        scratch_shapes=[
            pltpu.VMEM((own_rows, terms2), BF16),
            pltpu.VMEM((tiles, 2 * steps, capacity), F32),
            pltpu.SemaphoreType.DMA((2,)),
        ],
        compiler_params=pltpu.CompilerParams(vmem_limit_bytes=56 * MIB),
        name="pack",
    )(me, beam_coefs.reshape(own_rows, terms2), own_tracks)
    along = [packed[0]] + [exchange(packed[r], 4 * r, tiles) for r in range(1, outer)]

    cells = jnp.transpose(subgrids.reshape(number, 2, 8, 128), (0, 2, 1, 3))
    cells = cells.reshape(number * 16, 128)
    row_turns, cell_turns = transform_tables(edge)
    image = pl.pallas_call(
        transform_kernel,
        out_shape=jax.ShapeDtypeStruct((8, number, 256), BF16),
        in_specs=[hbm] + [vmem] * 2,
        out_specs=vmem,
        scratch_shapes=[
            pltpu.VMEM((number * 16, 128), BF16),
            pltpu.VMEM((8, 256, 256), BF16),
            pltpu.VMEM((8, 256, 256), BF16),
            pltpu.VMEM((number * 16, 128), F32),
            pltpu.VMEM((8, number, 512), BF16),
            pltpu.SemaphoreType.DMA,
        ],
        compiler_params=pltpu.CompilerParams(vmem_limit_bytes=14 * MIB),
        name="transform",
    )(cells, jnp.asarray(row_turns), jnp.asarray(cell_turns))

    near, for_y = pl.pallas_call(
        stack_kernel,
        out_shape=[
            jax.ShapeDtypeStruct((outer,) + block.shape, BF16),
            jax.ShapeDtypeStruct((outer, 2 * own_rows + 6 * steps, 128), BF16),
        ],
        in_specs=[smem] + [vmem] * outer + [anywhere],
        out_specs=[vmem] * 2,
        compiler_params=pltpu.CompilerParams(vmem_limit_bytes=3 * MIB * (tiles // 16)),
        name="stack",
    )(me, *along[::-1], image)
    over_core = exchange(near, 1, tiles)
    over_y = exchange(for_y, 2, tiles)
    route, back, pick, weights, turns = pl.pallas_call(
        functools.partial(prepare_kernel, slot_count=slot_count),
        out_shape=[
            jax.ShapeDtypeStruct((number, slots), BF16),
            jax.ShapeDtypeStruct((slots, number), BF16),
            jax.ShapeDtypeStruct((2 * number, tiles * own_rows), BF16),
            jax.ShapeDtypeStruct((8, terms2, 256), BF16),
            jax.ShapeDtypeStruct((1, vis), F32),
        ],
        in_specs=[smem] + [vmem] * 5 + [anywhere],
        out_specs=[vmem] * 5,
        compiler_params=pltpu.CompilerParams(vmem_limit_bytes=8 * MIB * (1 + tiles // 64)),
        name="prepare",
    )(
        counts,
        assign[0],
        stations.T,
        time_slots.reshape(1, number),
        beam_basis,
        frequencies.reshape(1, chan),
        near,
    )

    over_both = pl.pallas_call(
        relay_kernel,
        out_shape=jax.ShapeDtypeStruct(over_y.shape, BF16),
        in_specs=[vmem, anywhere],
        out_specs=vmem,
        compiler_params=pltpu.CompilerParams(vmem_limit_bytes=2 * MIB * (tiles // 16)),
        name="relay",
    )(over_y, weights)
    over_both = exchange(over_both, 1, tiles)

    for_z = jax.ShapeDtypeStruct((4, capacity, vis), BF16)
    for_plane = jax.ShapeDtypeStruct((outer, capacity, vis), BF16)
    models = pl.pallas_call(
        predict_kernel,
        out_shape=[for_z] * outer + [for_plane] * 4,
        in_specs=[smem] + [vmem] * 10,
        out_specs=[vmem] * (outer + 4),
        scratch_shapes=[
            pltpu.VMEM((tiles * own_rows, terms2), BF16),
            pltpu.VMEM((tiles, 6 * steps, capacity), F32),
            pltpu.VMEM((2 * number, terms2), BF16),
            pltpu.VMEM((number * 8, 128), F32),
            pltpu.VMEM((number * 8, 128), F32),
            pltpu.VMEM((number * 8, vis), F32),
            pltpu.VMEM((number * 8, vis), F32),
            pltpu.VMEM((6, number, vis), F32),
            pltpu.VMEM((number * 8, vis), F32),
            pltpu.VMEM((number * 8, vis), F32),
            pltpu.VMEM((2, number, vis), F32),
            pltpu.VMEM((2 * slots, vis), F32),
        ],
        compiler_params=pltpu.CompilerParams(vmem_limit_bytes=20 * MIB * (1 + tiles // 64)),
        name="predict",
    )(
        me,
        near,
        over_y,
        over_core,
        over_both,
        route,
        back,
        pick,
        weights,
        turns,
        image,
    )
    def turned(blocks, out_shape):
        return pl.pallas_call(
            turn_kernel,
            out_shape=out_shape,
            in_specs=[vmem] * len(blocks),
            out_specs=[vmem] * len(out_shape),
            compiler_params=pltpu.CompilerParams(vmem_limit_bytes=2 * MIB),
            name="turn",
        )(*blocks[::-1])

    first, second = models[:outer], models[outer:]
    second = [second[0]] + [exchange(second[p], p, tiles) for p in range(1, 4)]
    first = [first[0]] + [exchange(first[r], 4 * r, tiles) for r in range(1, outer)]
    second = turned(second, [for_z] * outer)
    second = [second[0]] + [exchange(second[r], 4 * r, tiles) for r in range(1, outer)]
    first = turned(first, [for_plane] * 4)
    first = [first[0]] + [exchange(first[p], p, tiles) for p in range(1, 4)]
    residual = pl.pallas_call(
        residual_kernel,
        out_shape=jax.ShapeDtypeStruct((tiles, 2 * capacity, vis), F32),
        in_specs=[smem] + [vmem] * (5 + outer),
        out_specs=vmem,
        compiler_params=pltpu.CompilerParams(vmem_limit_bytes=6 * MIB),
        name="residual",
    )(me, observed.reshape(tiles, 2 * capacity, vis), *second[::-1], *first)
    return residual.reshape(observed.shape)


def solution(mesh):
    return jax.shard_map(
        per_device,
        mesh=mesh,
        in_specs=(
            P(("grp", "tile"), None, None),
            P(("grp", "tile"), None),
            P(("grp", "tile")),
            P(("grp", "tile"), None, None),
            P(("grp", "tile"), None),
            P(("grp", "tile"), None, None),
            P(),
            P("grp"),
            P(("grp", "tile"), None, None, None, None),
            P(("grp", "tile"), None, None, None, None),
        ),
        out_specs=P(("grp", "tile"), None, None, None, None),
        check_vma=False,
    )
```

```python
import functools
import math

import jax
import jax.numpy as jnp
import numpy as np
from jax import lax
from jax.experimental import pallas as pl
from jax.experimental.pallas import tpu as pltpu
from jax.sharding import PartitionSpec as P

TWO_PI = 2.0 * math.pi
F32 = jnp.float32
BF16 = jnp.bfloat16
MIB = 1024 * 1024
NT = (((1,), (1,)), ((), ()))


def dot(a, b, dims=(((1,), (0,)), ((), ()))):
    return lax.dot_general(a, b, dims, preferred_element_type=F32)


def transform_tables(edge):
    low = edge // 8
    outer = np.arange(8)[:, None, None, None]
    b = np.arange(low)[None, :, None, None]
    inner = np.arange(low)[None, None, :, None]
    x = np.arange(edge)
    turns = np.broadcast_to(b * (outer + 8 * inner) % edge, (8, low, low, edge))
    rows = TWO_PI / edge * turns.reshape(8, low, low * edge)
    cells = TWO_PI / edge * np.tile(x[:, None] * x[None, :] % edge, (1, low))
    rows = np.stack([np.cos(rows), np.sin(rows)]).astype(np.float32)
    cells = (np.stack([np.cos(cells), np.sin(cells)]) / edge**2).astype(np.float32)
    return rows.reshape(2, 8 * low, low * edge), cells


def eight_point(re, im):
    half = math.sqrt(0.5)

    def four(r, i):
        s0r, s0i, d0r, d0i = r[0] + r[2], i[0] + i[2], r[0] - r[2], i[0] - i[2]
        s1r, s1i, d1r, d1i = r[1] + r[3], i[1] + i[3], r[1] - r[3], i[1] - i[3]
        return (
            [s0r + s1r, d0r - d1i, s0r - s1r, d0r + d1i],
            [s0i + s1i, d0i + d1r, s0i - s1i, d0i - d1r],
        )

    er, ei = four(re[0::2], im[0::2])
    orr, oi = four(re[1::2], im[1::2])
    tr = [orr[0], half * (orr[1] - oi[1]), -oi[2], -half * (orr[3] + oi[3])]
    ti = [oi[0], half * (orr[1] + oi[1]), orr[2], half * (orr[3] - oi[3])]
    out_re = [er[m] + tr[m] for m in range(4)] + [er[m] - tr[m] for m in range(4)]
    out_im = [ei[m] + ti[m] for m in range(4)] + [ei[m] - ti[m] for m in range(4)]
    return out_re, out_im


def transform_kernel(cells_hbm, row_turns, cell_turns, image, cells, high, rest, wide, sums, sem):
    copy = pltpu.make_async_copy(cells_hbm, cells, sem)
    copy.start()
    number = image.shape[1]
    edge, span = cell_turns.shape[1:]
    low = span // edge
    cell_c, cell_s = cell_turns[0], cell_turns[1]
    for m in range(8):
        for k in range(low):
            at = m * low + k
            row_c, row_s = row_turns[0, at : at + 1, :], row_turns[1, at : at + 1, :]
            c = row_c * cell_c - row_s * cell_s
            s = row_s * cell_c + row_c * cell_s
            c_top, s_top = c.astype(BF16), s.astype(BF16)
            c_left = (c - c_top.astype(F32)).astype(BF16)
            s_left = (s - s_top.astype(F32)).astype(BF16)
            re = slice(k * edge, (k + 1) * edge)
            im = slice(span + k * edge, span + (k + 1) * edge)
            for held, cos_part, sin_part in ((high, c_top, s_top), (rest, c_left, s_left)):
                held[m, re, :span] = cos_part
                held[m, re, span:] = sin_part
                held[m, im, :span] = -sin_part
                held[m, im, span:] = cos_part
    copy.wait()
    step = 16

    @pl.loop(0, number // step, unroll=8)
    def _(n):
        rows = pl.ds(pl.multiple_of(n * step, step), step)
        span = pl.ds(pl.multiple_of(n * step * 16, step * 16), step * 16)
        wide[span, :] = cells[span, :].astype(F32)
        re = [wide[pl.ds(n * step * 16 + 2 * k, step, stride=16), :] for k in range(8)]
        im = [wide[pl.ds(n * step * 16 + 2 * k + 1, step, stride=16), :] for k in range(8)]
        out_re, out_im = eight_point(re, im)
        for m in range(8):
            value = jnp.concatenate([out_re[m], out_im[m]], axis=1)
            top = value.astype(BF16)
            sums[m, rows, :256] = top
            sums[m, rows, 256:] = (value - top.astype(F32)).astype(BF16)

    for m in range(8):
        both = sums[m]
        left = jnp.concatenate([both, both[:, :256]], axis=1)
        right = jnp.concatenate([high[m], high[m], rest[m]], axis=0)
        image[m] = dot(left, right).astype(BF16)


def relative(mine, place, tiles):
    outer = tiles // 4
    return mine ^ (4 * (place % outer) + place // outer)


def prepare_kernel(
    me, counts, assign, stations, time_slots, basis, freq, after, route, back, pick, weights, turns, *, slot_count
):
    number = route.shape[0]
    tiles, capacity = assign.shape
    outer = tiles // 4
    mine = me[0]
    scaled = freq[...] * (-1.0 / 32.0)
    turns[...] = jnp.concatenate([scaled] * (turns.shape[1] // freq.shape[1]), axis=1)

    per = 128 // capacity
    down = lax.broadcasted_iota(jnp.int32, (number, 128), 0)
    slot = lax.broadcasted_iota(jnp.int32, (1, capacity), 1)
    for n in range(tiles // per):
        chosen = []
        for place in range(n * per, (n + 1) * per):
            d = relative(mine, place, tiles)
            chosen.append(jnp.where(slot < counts[0, d], assign[pl.ds(d, 1), :], -1))
        hot = (jnp.concatenate(chosen, axis=1) == down).astype(F32)
        route[:, n * 128 : (n + 1) * 128] = hot.astype(BF16)
        back[n * 128 : (n + 1) * 128, :] = hot.T.astype(BF16)

    rows_own = pick.shape[1] // tiles
    each = rows_own // slot_count
    away = (stations[...] // each) ^ mine
    place = away % 4 * outer + away // 4
    index = place * rows_own + stations[...] % each * slot_count + time_slots[...]
    index = jnp.concatenate([index.astype(F32), jnp.zeros((6, number), F32)], axis=0).T
    index = index.astype(jnp.int32)
    across = lax.broadcasted_iota(jnp.int32, (number, pick.shape[1]), 1)
    for which in range(2):
        hot = (index[:, which : which + 1] == across).astype(F32)
        pick[which * number : (which + 1) * number, :] = hot.astype(BF16)

    terms = basis.shape[1]
    edge = math.isqrt(basis.shape[2])
    for m in range(8):
        starts = [(8 * n + m) * edge for n in range(edge // 8)]
        b_re = jnp.concatenate([basis[0, :, n : n + edge] for n in starts], axis=1)
        b_im = jnp.concatenate([basis[1, :, n : n + edge] for n in starts], axis=1)
        weights[m, :terms, :128] = b_re
        weights[m, :terms, 128:] = b_im
        weights[m, terms:, :128] = -b_im
        weights[m, terms:, 128:] = b_re


def unit_powers(turns):
    turns = turns - jnp.round(turns)
    angle = (0.5 * math.pi) * turns
    sq = angle * angle
    s = angle * (
        1.0 + sq * (-1.0 / 6 + sq * (1.0 / 120 + sq * (-1.0 / 5040 + sq * (1.0 / 362880))))
    )
    c = 1.0 + sq * (
        -0.5 + sq * (1.0 / 24 + sq * (-1.0 / 720 + sq * (1.0 / 40320 - sq * (1.0 / 3628800))))
    )
    for _ in range(2):
        c, s = 1.0 - 2.0 * (s * s), 2.0 * (s * c)
    return c, s


def cmul(ar, ai, br, bi):
    return ar * br - ai * bi, ar * bi + ai * br


def pack_kernel(me, coefs_hbm, tracks_hbm, *refs):
    out, for_y, coefs, tracks, sems = refs[:-4], *refs[-4:]
    copies = [
        pltpu.make_async_copy(coefs_hbm, coefs, sems.at[0]),
        pltpu.make_async_copy(tracks_hbm, tracks, sems.at[1]),
    ]
    for copy in copies:
        copy.start()
    for copy in copies:
        copy.wait()
    capacity = tracks.shape[2]
    rows = coefs.shape[0]
    for r in range(len(out)):
        plane = (me[0] // 4) ^ r
        kept = []
        for k in (0, 2):
            tr = jnp.concatenate([tracks[plane * 4 + k], tracks[plane * 4 + k + 1]], axis=1)
            top = tr.astype(BF16).astype(F32)
            kept += [top, tr - top]
        pieces = jnp.concatenate(kept, axis=0)
        if 2 * capacity < 128:
            blank = jnp.zeros((pieces.shape[0], 128 - 2 * capacity), F32)
            pieces = jnp.concatenate([pieces, blank], axis=1)
        out[r][:rows, :] = coefs[:, :128]
        out[r][rows : 2 * rows, :] = coefs[:, 128:]
        out[r][2 * rows :, :] = pieces.astype(BF16)
        if r == 0:
            for_y[:rows, :] = coefs[:, :128]
            for_y[rows : 2 * rows, :] = coefs[:, 128:]
            for_y[2 * rows :, :] = own_pair(pieces, me[0] ^ 2).astype(BF16)


def own_pair(pieces, device):
    half = pieces.shape[0] // 2
    return jnp.where(device & 2 == 0, pieces[:half, :], pieces[half:, :])


def stack_kernel(me, *refs):
    blocks, near, for_y = refs[:-4], refs[-2], refs[-1]
    table = 2 * for_y.shape[1] - near.shape[1]
    for r, block in enumerate(blocks[::-1]):
        near[r] = block[...]
        if r > 0:
            for_y[r - 1, :table, :] = block[:table, :]
            tracks = own_pair(block[table:, :].astype(F32), me[0] ^ 2)
            for_y[r - 1, table:, :] = tracks.astype(BF16)


def relay_kernel(own, others, after, out):
    out[0] = own[...]
    for r in range(others.shape[0]):
        out[r + 1] = others[r]


def unpacked(mine, groups, table, rows_own, capacity):
    kept = []
    for arrived in groups:
        for r in range(arrived.shape[0]):
            at = slice(len(kept) * rows_own, (len(kept) + 1) * rows_own)
            table[at, :128] = arrived[r, :rows_own, :]
            table[at, 128:] = arrived[r, rows_own : 2 * rows_own, :]
            piece = arrived[r, 2 * rows_own :, :].astype(F32)
            if arrived.shape[1] == groups[0].shape[1] and len(groups) > 1:
                piece = own_pair(piece, mine)
            moved = jnp.where(mine & 1 == 0, piece, pltpu.roll(piece, 128 - capacity, 1))
            kept.append(moved[:, :capacity])
    per = 128 // capacity
    tiles = [jnp.concatenate(kept[n : n + per], axis=1) for n in range(0, len(kept), per)]
    return jnp.concatenate(tiles, axis=1).astype(BF16)


def early_kernel(me, near, over_core, over_y, route, pick, coef, per_sub, table, *, capacity):
    places = 3 * near.shape[0]
    rows = table.shape[0]
    pieces = unpacked(me[0], (near, over_core, over_y), table, rows // places, capacity)
    coef[...] = dot(pick[:, :rows], table[...]).astype(BF16)
    per_sub[...] = dot(route[:, : places * capacity], pieces, NT)


def predict_kernel(
    me,
    over_both,
    route,
    back,
    pick,
    weights,
    turns,
    image,
    coef_early,
    per_sub_early,
    *refs,
):
    table, coef, wre, wim, pure, puim, zrow, hre, him, zv, interleaved = refs[-11:]
    number = image.shape[1]
    slots = back.shape[0]
    outer = over_both.shape[0]
    capacity = slots // (4 * outer)
    rows = table.shape[0]
    vis = turns.shape[1]
    kinds = per_sub_early.shape[1] // 2
    steps = kinds // 2
    chan = vis // steps
    pieces = unpacked(me[0], (over_both,), table, rows // outer, capacity)

    per_sub = per_sub_early[...] + dot(route[:, slots - outer * capacity :], pieces, NT)
    per_sub = per_sub.astype(BF16)
    wide = 2 * steps * chan
    from_row = lax.broadcasted_iota(jnp.int32, (2 * kinds, wide), 0) % kinds
    to_lane = lax.broadcasted_iota(jnp.int32, (2 * kinds, wide), 1) // chan
    spread = (from_row == to_lane).astype(F32).astype(BF16)
    uv = dot(per_sub, spread)
    ur, ui = unit_powers(uv[:, :vis] * turns[...])
    vr, vi = unit_powers(uv[:, vis:] * turns[...])

    pure[pl.ds(0, number, stride=8), :] = jnp.ones_like(ur)
    puim[pl.ds(0, number, stride=8), :] = jnp.zeros_like(ur)
    pure[pl.ds(1, number, stride=8), :] = ur
    puim[pl.ds(1, number, stride=8), :] = ui
    cr, ci = ur, ui
    for k in range(2, 8):
        cr, ci = cmul(cr, ci, ur, ui)
        pure[pl.ds(k, number, stride=8), :] = cr
        puim[pl.ds(k, number, stride=8), :] = ci
    cr, ci = cmul(cr, ci, ur, ui)
    zrow[0] = cr
    zrow[1] = ci
    cr, ci = cmul(cr, ci, cr, ci)
    zrow[2] = cr
    zrow[3] = ci
    zv[0] = vr
    zv[1] = vi
    cr, ci = vr, vi
    for _ in range(3):
        cr, ci = cmul(cr, ci, cr, ci)
    zrow[4] = cr
    zrow[5] = ci

    last = dot(pick[:, pick.shape[1] - rows :], table[...])
    coef[...] = (coef_early[...].astype(F32) + last).astype(BF16)

    block = 32
    for m in range(8):
        beams = dot(coef[...], weights[m])
        for n in range(0, number, block):
            first = beams[n : n + block, :]
            second = beams[number + n : number + n + block, :]
            f_re, f_im, s_re, s_im = first[:, :128], first[:, 128:], second[:, :128], second[:, 128:]
            g_re = f_re * s_re + f_im * s_im
            g_im = f_im * s_re - f_re * s_im
            i_re = image[m, n : n + block, :128].astype(F32)
            i_im = image[m, n : n + block, 128:].astype(F32)
            to = pl.ds(n * 8 + m, block, stride=8)
            wre[to, :] = i_re * g_re - i_im * g_im
            wim[to, :] = i_re * g_im + i_im * g_re

    unroll = 128

    def one(g):
        at = pl.ds(pl.multiple_of(g * 8, 8), 8)
        w_re, w_im = wre[at, :], wim[at, :]
        lhs = [
            jnp.concatenate([w_re[:, n : n + 32], w_im[:, n : n + 32]], axis=1)
            for n in range(0, 128, 32)
        ]
        lhs = jnp.concatenate(lhs, axis=0).astype(BF16)
        p_re, p_im = pure[at, :], puim[at, :]
        z = [jnp.broadcast_to(zrow[k, pl.ds(g, 1), :], (8, 128)) for k in range(6)]
        rr, ii, ri, ir = p_re * z[0], p_im * z[1], p_re * z[1], p_im * z[0]
        up_re, up_im = rr - ii, ri + ir
        dn_re, dn_im = rr + ii, ir - ri
        rr, ii, ri, ir = p_re * z[2], p_im * z[3], p_re * z[3], p_im * z[2]
        lo_re, lo_im = rr + ii, ir - ri
        c = jnp.concatenate([lo_re, dn_re, p_re, up_re], axis=0).astype(BF16)
        s = jnp.concatenate([lo_im, dn_im, p_im, up_im], axis=0).astype(BF16)
        top = jnp.concatenate([c, s], axis=1)
        low = jnp.concatenate([-s, c], axis=1)
        rhs = jnp.concatenate([top, low], axis=0)
        out = dot(lhs, rhs)
        h_re, h_im = out[24:32, :128], out[24:32, 128:]
        for j in (2, 1, 0):
            n_re = h_re * z[4] - h_im * z[5] + out[8 * j : 8 * j + 8, :128]
            h_im = h_re * z[5] + h_im * z[4] + out[8 * j : 8 * j + 8, 128:]
            h_re = n_re
        hre[at, :] = h_re
        him[at, :] = h_im

    @pl.loop(0, number // unroll)
    def _(n):
        for k in range(unroll):
            one(n * unroll + k)

    vr, vi = zv[0], zv[1]
    a_re = hre[pl.ds(7, number, stride=8), :]
    a_im = him[pl.ds(7, number, stride=8), :]
    for k in range(6, -1, -1):
        n_re = a_re * vr - a_im * vi + hre[pl.ds(k, number, stride=8), :]
        a_im = a_re * vi + a_im * vr + him[pl.ds(k, number, stride=8), :]
        a_re = n_re
    cr, ci = cmul(zrow[4], zrow[5], zrow[4], zrow[5])
    m_re, m_im = a_re * cr + a_im * ci, a_im * cr - a_re * ci
    models = jnp.concatenate([m_re, m_im], axis=1).astype(BF16)
    sent = dot(back[...], models)
    interleaved[pl.ds(0, slots, stride=2), :] = sent[:, :128]
    interleaved[pl.ds(1, slots, stride=2), :] = sent[:, 128:]
    along_z, in_plane = refs[:outer], refs[outer : outer + 4]
    for r in range(outer):
        for p in range(4):
            start = (p * outer + r) * (2 * capacity)
            along_z[r][p] = interleaved[start : start + capacity, :].astype(BF16)
            in_plane[p][r] = interleaved[start + capacity : start + 2 * capacity, :].astype(BF16)


def turn_kernel(*refs):
    count = refs[0].shape[0]
    blocks, out = refs[:-count], refs[-count:]
    for i, block in enumerate(blocks[::-1]):
        for j in range(count):
            out[j][i] = block[j]


def residual_second(me, observed, *refs):
    by_z, (out, kept, sem) = refs[:-3][::-1], refs[-3:]
    rows = kept.shape[1]
    for r in range(len(by_z)):
        for p in range(4):
            source = me[0] ^ (4 * r + p)
            kept[source] = observed[source, rows:, :] - by_z[r][p].astype(F32)
    copy = pltpu.make_async_copy(kept, out.at[:, rows:, :], sem)
    copy.start()
    copy.wait()


def residual_first(me, observed, second, *refs):
    by_plane, (out, kept, sem) = refs[:-3], refs[-3:]
    rows = kept.shape[1]
    for p in range(4):
        for r in range(by_plane[p].shape[0]):
            source = me[0] ^ (4 * r + p)
            kept[source] = observed[source, :rows, :] - by_plane[p][r].astype(F32)
    copy = pltpu.make_async_copy(kept, out.at[:, :rows, :], sem)
    copy.start()
    copy.wait()


def exchange(value, step, tiles):
    return lax.ppermute(value, "tile", [(i, i ^ step) for i in range(tiles)])


def per_device(
    subgrids,
    stations,
    time_slots,
    assign,
    counts,
    beam_coefs,
    beam_basis,
    frequencies,
    uv_tracks,
    observed,
):
    tiles = lax.axis_size("tile")
    capacity = assign.shape[2]
    slots = tiles * capacity
    number = subgrids.shape[0]
    pixels = subgrids.shape[2]
    edge = math.isqrt(pixels)
    slot_count = beam_coefs.shape[1]
    terms2 = beam_coefs.shape[2]
    steps = uv_tracks.shape[4]
    chan = frequencies.shape[0]
    vis = steps * chan
    vmem = pl.BlockSpec(memory_space=pltpu.VMEM)
    own_tracks = jnp.transpose(uv_tracks[0], (0, 2, 3, 1)).reshape(tiles, 2 * steps, capacity)
    own_rows = beam_coefs.shape[0] * slot_count
    smem = pl.BlockSpec(memory_space=pltpu.SMEM)
    anywhere = pl.BlockSpec(memory_space=pl.ANY)
    hbm = pl.BlockSpec(memory_space=pltpu.HBM)
    outer = tiles // 4
    me = lax.axis_index("tile").astype(jnp.int32).reshape(1)
    block = jax.ShapeDtypeStruct((2 * own_rows + 8 * steps, 128), BF16)
    block_y = jax.ShapeDtypeStruct((2 * own_rows + 4 * steps, 128), BF16)
    *packed, own_y = pl.pallas_call(
        pack_kernel,
        out_shape=[block] * outer + [block_y],
        in_specs=[smem, hbm, hbm],
        out_specs=[vmem] * (outer + 1),
        scratch_shapes=[
            pltpu.VMEM((own_rows, terms2), BF16),
            pltpu.VMEM((tiles, 2 * steps, capacity), F32),
            pltpu.SemaphoreType.DMA((2,)),
        ],
        compiler_params=pltpu.CompilerParams(vmem_limit_bytes=56 * MIB),
        name="pack",
    )(me, beam_coefs.reshape(own_rows, terms2), own_tracks)
    along = [packed[0]] + [exchange(packed[r], 4 * r, tiles) for r in range(1, outer)]
    own_over_y = exchange(own_y, 2, tiles)

    cells = jnp.transpose(subgrids.reshape(number, 2, 8, 128), (0, 2, 1, 3))
    cells = cells.reshape(number * 16, 128)
    row_turns, cell_turns = transform_tables(edge)
    image = pl.pallas_call(
        transform_kernel,
        out_shape=jax.ShapeDtypeStruct((8, number, 256), BF16),
        in_specs=[hbm] + [vmem] * 2,
        out_specs=vmem,
        scratch_shapes=[
            pltpu.VMEM((number * 16, 128), BF16),
            pltpu.VMEM((8, 256, 256), BF16),
            pltpu.VMEM((8, 256, 256), BF16),
            pltpu.VMEM((number * 16, 128), F32),
            pltpu.VMEM((8, number, 512), BF16),
            pltpu.SemaphoreType.DMA,
        ],
        compiler_params=pltpu.CompilerParams(vmem_limit_bytes=14 * MIB),
        name="transform",
    )(cells, jnp.asarray(row_turns), jnp.asarray(cell_turns))

    near, for_y = pl.pallas_call(
        stack_kernel,
        out_shape=[
            jax.ShapeDtypeStruct((outer,) + block.shape, BF16),
            jax.ShapeDtypeStruct((outer - 1,) + block_y.shape, BF16),
        ],
        in_specs=[smem] + [vmem] * outer + [anywhere] * 2,
        out_specs=[vmem] * 2,
        compiler_params=pltpu.CompilerParams(vmem_limit_bytes=3 * MIB * (tiles // 16)),
        name="stack",
    )(me, *along[::-1], own_over_y, image)
    over_core = exchange(near, 1, tiles)
    over_y = exchange(for_y, 2, tiles)
    route, back, pick, weights, turns = pl.pallas_call(
        functools.partial(prepare_kernel, slot_count=slot_count),
        out_shape=[
            jax.ShapeDtypeStruct((number, slots), BF16),
            jax.ShapeDtypeStruct((slots, number), BF16),
            jax.ShapeDtypeStruct((2 * number, tiles * own_rows), BF16),
            jax.ShapeDtypeStruct((8, terms2, 256), BF16),
            jax.ShapeDtypeStruct((1, vis), F32),
        ],
        in_specs=[smem] * 2 + [vmem] * 5 + [anywhere],
        out_specs=[vmem] * 5,
        compiler_params=pltpu.CompilerParams(vmem_limit_bytes=8 * MIB * (1 + tiles // 64)),
        name="prepare",
    )(
        me,
        counts,
        assign[0],
        stations.T,
        time_slots.reshape(1, number),
        beam_basis,
        frequencies.reshape(1, chan),
        near,
    )

    over_y = pl.pallas_call(
        relay_kernel,
        out_shape=jax.ShapeDtypeStruct((outer,) + block_y.shape, BF16),
        in_specs=[vmem, vmem, anywhere],
        out_specs=vmem,
        compiler_params=pltpu.CompilerParams(vmem_limit_bytes=2 * MIB * (tiles // 16)),
        name="relay",
    )(own_over_y, over_y, weights)
    over_both = exchange(over_y, 1, tiles)
    coef_early, per_sub_early = pl.pallas_call(
        functools.partial(early_kernel, capacity=capacity),
        out_shape=[
            jax.ShapeDtypeStruct((2 * number, terms2), BF16),
            jax.ShapeDtypeStruct((number, 4 * steps), F32),
        ],
        in_specs=[smem] + [vmem] * 5,
        out_specs=[vmem] * 2,
        scratch_shapes=[pltpu.VMEM((3 * outer * own_rows, terms2), BF16)],
        compiler_params=pltpu.CompilerParams(vmem_limit_bytes=8 * MIB * (1 + tiles // 64)),
        name="early",
    )(me, near, over_core, over_y, route, pick)

    for_z = jax.ShapeDtypeStruct((4, capacity, vis), BF16)
    for_plane = jax.ShapeDtypeStruct((outer, capacity, vis), BF16)
    models = pl.pallas_call(
        predict_kernel,
        out_shape=[for_z] * outer + [for_plane] * 4,
        in_specs=[smem] + [vmem] * 9,
        out_specs=[vmem] * (outer + 4),
        scratch_shapes=[
            pltpu.VMEM((outer * own_rows, terms2), BF16),
            pltpu.VMEM((2 * number, terms2), BF16),
            pltpu.VMEM((number * 8, 128), F32),
            pltpu.VMEM((number * 8, 128), F32),
            pltpu.VMEM((number * 8, vis), F32),
            pltpu.VMEM((number * 8, vis), F32),
            pltpu.VMEM((6, number, vis), F32),
            pltpu.VMEM((number * 8, vis), F32),
            pltpu.VMEM((number * 8, vis), F32),
            pltpu.VMEM((2, number, vis), F32),
            pltpu.VMEM((2 * slots, vis), F32),
        ],
        compiler_params=pltpu.CompilerParams(vmem_limit_bytes=20 * MIB * (1 + tiles // 64)),
        name="predict",
    )(
        me,
        over_both,
        route,
        back,
        pick,
        weights,
        turns,
        image,
        coef_early,
        per_sub_early,
    )
    def turned(blocks, out_shape):
        return pl.pallas_call(
            turn_kernel,
            out_shape=out_shape,
            in_specs=[vmem] * len(blocks),
            out_specs=[vmem] * len(out_shape),
            compiler_params=pltpu.CompilerParams(vmem_limit_bytes=2 * MIB),
            name="turn",
        )(*blocks[::-1])

    first, second = models[:outer], models[outer:]
    second = [second[0]] + [exchange(second[p], p, tiles) for p in range(1, 4)]
    first = [first[0]] + [exchange(first[r], 4 * r, tiles) for r in range(1, outer)]
    second = turned(second, [for_z] * outer)
    second = [second[0]] + [exchange(second[r], 4 * r, tiles) for r in range(1, outer)]
    first = turned(first, [for_plane] * 4)
    first = [first[0]] + [exchange(first[p], p, tiles) for p in range(1, 4)]
    ours = observed.reshape(tiles, 2 * capacity, vis)
    finish = functools.partial(
        pl.pallas_call,
        out_shape=jax.ShapeDtypeStruct(ours.shape, F32),
        out_specs=anywhere,
        scratch_shapes=[pltpu.VMEM((tiles, capacity, vis), F32), pltpu.SemaphoreType.DMA],
        compiler_params=pltpu.CompilerParams(vmem_limit_bytes=6 * MIB),
    )
    residual = finish(
        residual_second, in_specs=[smem] + [vmem] * (1 + outer), name="residual_second"
    )(me, ours, *second[::-1])
    residual = finish(
        residual_first,
        in_specs=[smem, vmem, anywhere] + [vmem] * 4,
        input_output_aliases={2: 0},
        name="residual_first",
    )(me, ours, residual, *first)
    return residual.reshape(observed.shape)


def solution(mesh):
    return jax.shard_map(
        per_device,
        mesh=mesh,
        in_specs=(
            P(("grp", "tile"), None, None),
            P(("grp", "tile"), None),
            P(("grp", "tile")),
            P(("grp", "tile"), None, None),
            P(("grp", "tile"), None),
            P(("grp", "tile"), None, None),
            P(),
            P("grp"),
            P(("grp", "tile"), None, None, None, None),
            P(("grp", "tile"), None, None, None, None),
        ),
        out_specs=P(("grp", "tile"), None, None, None, None),
        check_vma=False,
    )
```

```python
import functools
import math

import jax
import jax.numpy as jnp
import numpy as np
from jax import lax
from jax.experimental import pallas as pl
from jax.experimental.pallas import tpu as pltpu
from jax.sharding import PartitionSpec as P

TWO_PI = 2.0 * math.pi
F32 = jnp.float32
BF16 = jnp.bfloat16
MIB = 1024 * 1024
NT = (((1,), (1,)), ((), ()))


def dot(a, b, dims=(((1,), (0,)), ((), ()))):
    return lax.dot_general(a, b, dims, preferred_element_type=F32)


def transform_tables(edge):
    low = edge // 8
    outer = np.arange(8)[:, None, None, None]
    b = np.arange(low)[None, :, None, None]
    inner = np.arange(low)[None, None, :, None]
    x = np.arange(edge)
    turns = np.broadcast_to(b * (outer + 8 * inner) % edge, (8, low, low, edge))
    rows = TWO_PI / edge * turns.reshape(8, low, low * edge)
    cells = TWO_PI / edge * np.tile(x[:, None] * x[None, :] % edge, (1, low))
    rows = np.stack([np.cos(rows), np.sin(rows)]).astype(np.float32)
    cells = (np.stack([np.cos(cells), np.sin(cells)]) / edge**2).astype(np.float32)
    return rows.reshape(2, 8 * low, low * edge), cells


def eight_point(re, im):
    half = math.sqrt(0.5)

    def four(r, i):
        s0r, s0i, d0r, d0i = r[0] + r[2], i[0] + i[2], r[0] - r[2], i[0] - i[2]
        s1r, s1i, d1r, d1i = r[1] + r[3], i[1] + i[3], r[1] - r[3], i[1] - i[3]
        return (
            [s0r + s1r, d0r - d1i, s0r - s1r, d0r + d1i],
            [s0i + s1i, d0i + d1r, s0i - s1i, d0i - d1r],
        )

    er, ei = four(re[0::2], im[0::2])
    orr, oi = four(re[1::2], im[1::2])
    tr = [orr[0], half * (orr[1] - oi[1]), -oi[2], -half * (orr[3] + oi[3])]
    ti = [oi[0], half * (orr[1] + oi[1]), orr[2], half * (orr[3] - oi[3])]
    out_re = [er[m] + tr[m] for m in range(4)] + [er[m] - tr[m] for m in range(4)]
    out_im = [ei[m] + ti[m] for m in range(4)] + [ei[m] - ti[m] for m in range(4)]
    return out_re, out_im


def transform_kernel(cells, row_turns, cell_turns, image, high, rest, wide, sums):
    number = image.shape[1]
    edge, span = cell_turns.shape[1:]
    low = span // edge
    cell_c, cell_s = cell_turns[0], cell_turns[1]
    for m in range(8):
        for k in range(low):
            at = m * low + k
            row_c, row_s = row_turns[0, at : at + 1, :], row_turns[1, at : at + 1, :]
            c = row_c * cell_c - row_s * cell_s
            s = row_s * cell_c + row_c * cell_s
            c_top, s_top = c.astype(BF16), s.astype(BF16)
            c_left = (c - c_top.astype(F32)).astype(BF16)
            s_left = (s - s_top.astype(F32)).astype(BF16)
            re = slice(k * edge, (k + 1) * edge)
            im = slice(span + k * edge, span + (k + 1) * edge)
            for held, cos_part, sin_part in ((high, c_top, s_top), (rest, c_left, s_left)):
                held[m, re, :span] = cos_part
                held[m, re, span:] = sin_part
                held[m, im, :span] = -sin_part
                held[m, im, span:] = cos_part
    step = 16

    @pl.loop(0, number // step, unroll=8)
    def _(n):
        rows = pl.ds(pl.multiple_of(n * step, step), step)
        span = pl.ds(pl.multiple_of(n * step * 16, step * 16), step * 16)
        wide[span, :] = cells[span, :].astype(F32)
        re = [wide[pl.ds(n * step * 16 + 2 * k, step, stride=16), :] for k in range(8)]
        im = [wide[pl.ds(n * step * 16 + 2 * k + 1, step, stride=16), :] for k in range(8)]
        out_re, out_im = eight_point(re, im)
        for m in range(8):
            value = jnp.concatenate([out_re[m], out_im[m]], axis=1)
            top = value.astype(BF16)
            sums[m, rows, :256] = top
            sums[m, rows, 256:] = (value - top.astype(F32)).astype(BF16)

    for m in range(8):
        both = sums[m]
        left = jnp.concatenate([both, both[:, :256]], axis=1)
        right = jnp.concatenate([high[m], high[m], rest[m]], axis=0)
        image[m] = dot(left, right).astype(BF16)


def relative(mine, place, tiles):
    outer = tiles // 4
    return mine ^ (4 * (place % outer) + place // outer)


def prepare_kernel(
    me, counts, assign, stations, time_slots, basis, freq, after, route, back, pick, weights, turns, *, slot_count
):
    number = route.shape[0]
    tiles, capacity = assign.shape
    outer = tiles // 4
    mine = me[0]
    scaled = freq[...] * (-1.0 / 32.0)
    turns[...] = jnp.concatenate([scaled] * (turns.shape[1] // freq.shape[1]), axis=1)

    per = 128 // capacity
    down = lax.broadcasted_iota(jnp.int32, (number, 128), 0)
    slot = lax.broadcasted_iota(jnp.int32, (1, capacity), 1)
    for n in range(tiles // per):
        chosen = []
        for place in range(n * per, (n + 1) * per):
            d = relative(mine, place, tiles)
            chosen.append(jnp.where(slot < counts[0, d], assign[pl.ds(d, 1), :], -1))
        hot = (jnp.concatenate(chosen, axis=1) == down).astype(F32)
        route[:, n * 128 : (n + 1) * 128] = hot.astype(BF16)
        back[n * 128 : (n + 1) * 128, :] = hot.T.astype(BF16)

    rows_own = pick.shape[1] // tiles
    each = rows_own // slot_count
    away = (stations[...] // each) ^ mine
    place = away % 4 * outer + away // 4
    index = place * rows_own + stations[...] % each * slot_count + time_slots[...]
    index = jnp.concatenate([index.astype(F32), jnp.zeros((6, number), F32)], axis=0).T
    index = index.astype(jnp.int32)
    across = lax.broadcasted_iota(jnp.int32, (number, pick.shape[1]), 1)
    for which in range(2):
        hot = (index[:, which : which + 1] == across).astype(F32)
        pick[which * number : (which + 1) * number, :] = hot.astype(BF16)

    terms = basis.shape[1]
    edge = math.isqrt(basis.shape[2])
    for m in range(8):
        starts = [(8 * n + m) * edge for n in range(edge // 8)]
        b_re = jnp.concatenate([basis[0, :, n : n + edge] for n in starts], axis=1)
        b_im = jnp.concatenate([basis[1, :, n : n + edge] for n in starts], axis=1)
        weights[m, :terms, :128] = b_re
        weights[m, :terms, 128:] = b_im
        weights[m, terms:, :128] = -b_im
        weights[m, terms:, 128:] = b_re


def unit_powers(turns):
    turns = turns - jnp.round(turns)
    angle = (0.5 * math.pi) * turns
    sq = angle * angle
    s = angle * (
        1.0 + sq * (-1.0 / 6 + sq * (1.0 / 120 + sq * (-1.0 / 5040 + sq * (1.0 / 362880))))
    )
    c = 1.0 + sq * (
        -0.5 + sq * (1.0 / 24 + sq * (-1.0 / 720 + sq * (1.0 / 40320 - sq * (1.0 / 3628800))))
    )
    for _ in range(2):
        c, s = 1.0 - 2.0 * (s * s), 2.0 * (s * c)
    return c, s


def cmul(ar, ai, br, bi):
    return ar * br - ai * bi, ar * bi + ai * br


def pack_kernel(me, coefs_hbm, tracks_hbm, *refs):
    out, (coefs, tracks, sems) = refs[:-3], refs[-3:]
    copies = [
        pltpu.make_async_copy(coefs_hbm, coefs, sems.at[0]),
        pltpu.make_async_copy(tracks_hbm, tracks, sems.at[1]),
    ]
    for copy in copies:
        copy.start()
    for copy in copies:
        copy.wait()
    capacity = tracks.shape[2]
    rows = coefs.shape[0]
    for r in range(len(out)):
        plane = (me[0] // 4) ^ r
        kept = []
        for k in (0, 2):
            tr = jnp.concatenate([tracks[plane * 4 + k], tracks[plane * 4 + k + 1]], axis=1)
            top = tr.astype(BF16).astype(F32)
            kept += [top, tr - top]
        pieces = jnp.concatenate(kept, axis=0)
        if 2 * capacity < 128:
            blank = jnp.zeros((pieces.shape[0], 128 - 2 * capacity), F32)
            pieces = jnp.concatenate([pieces, blank], axis=1)
        out[r][:rows, :] = coefs[:, :128]
        out[r][rows : 2 * rows, :] = coefs[:, 128:]
        out[r][2 * rows :, :] = pieces.astype(BF16)


def own_pair(pieces, device):
    half = pieces.shape[0] // 2
    return jnp.where(device & 2 == 0, pieces[:half, :], pieces[half:, :])


def stack_kernel(me, *refs):
    blocks, near, for_y = refs[:-3], refs[-2], refs[-1]
    table = 2 * for_y.shape[1] - near.shape[1]
    for r, block in enumerate(blocks[::-1]):
        near[r] = block[...]
        for_y[r, :table, :] = block[:table, :]
        tracks = own_pair(block[table:, :].astype(F32), me[0] ^ 2)
        for_y[r, table:, :] = tracks.astype(BF16)


def relay_kernel(block, after, out):
    out[...] = block[...]


def unpacked(mine, groups, table, rows_own, capacity):
    kept = []
    for arrived in groups:
        for r in range(arrived.shape[0]):
            at = slice(len(kept) * rows_own, (len(kept) + 1) * rows_own)
            table[at, :128] = arrived[r, :rows_own, :]
            table[at, 128:] = arrived[r, rows_own : 2 * rows_own, :]
            piece = arrived[r, 2 * rows_own :, :].astype(F32)
            if arrived.shape[1] == groups[0].shape[1] and len(groups) > 1:
                piece = own_pair(piece, mine)
            moved = jnp.where(mine & 1 == 0, piece, pltpu.roll(piece, 128 - capacity, 1))
            kept.append(moved[:, :capacity])
    per = 128 // capacity
    tiles = [jnp.concatenate(kept[n : n + per], axis=1) for n in range(0, len(kept), per)]
    return jnp.concatenate(tiles, axis=1).astype(BF16)


def early_kernel(me, near, over_core, over_y, route, pick, coef, per_sub, table, *, capacity):
    places = 3 * near.shape[0]
    rows = table.shape[0]
    pieces = unpacked(me[0], (near, over_core, over_y), table, rows // places, capacity)
    coef[...] = dot(pick[:, :rows], table[...]).astype(BF16)
    per_sub[...] = dot(route[:, : places * capacity], pieces, NT)


def predict_kernel(
    me,
    over_both,
    route,
    back,
    pick,
    weights,
    turns,
    image,
    coef_early,
    per_sub_early,
    *refs,
):
    table, coef, wre, wim, pure, puim, zrow, hre, him, zv, interleaved = refs[-11:]
    number = image.shape[1]
    slots = back.shape[0]
    outer = over_both.shape[0]
    capacity = slots // (4 * outer)
    rows = table.shape[0]
    vis = turns.shape[1]
    kinds = per_sub_early.shape[1] // 2
    steps = kinds // 2
    chan = vis // steps
    pieces = unpacked(me[0], (over_both,), table, rows // outer, capacity)

    per_sub = per_sub_early[...] + dot(route[:, slots - outer * capacity :], pieces, NT)
    per_sub = per_sub.astype(BF16)
    wide = 2 * steps * chan
    from_row = lax.broadcasted_iota(jnp.int32, (2 * kinds, wide), 0) % kinds
    to_lane = lax.broadcasted_iota(jnp.int32, (2 * kinds, wide), 1) // chan
    spread = (from_row == to_lane).astype(F32).astype(BF16)
    uv = dot(per_sub, spread)
    ur, ui = unit_powers(uv[:, :vis] * turns[...])
    vr, vi = unit_powers(uv[:, vis:] * turns[...])

    pure[pl.ds(0, number, stride=8), :] = jnp.ones_like(ur)
    puim[pl.ds(0, number, stride=8), :] = jnp.zeros_like(ur)
    pure[pl.ds(1, number, stride=8), :] = ur
    puim[pl.ds(1, number, stride=8), :] = ui
    cr, ci = ur, ui
    for k in range(2, 8):
        cr, ci = cmul(cr, ci, ur, ui)
        pure[pl.ds(k, number, stride=8), :] = cr
        puim[pl.ds(k, number, stride=8), :] = ci
    cr, ci = cmul(cr, ci, ur, ui)
    zrow[0] = cr
    zrow[1] = ci
    cr, ci = cmul(cr, ci, cr, ci)
    zrow[2] = cr
    zrow[3] = ci
    zv[0] = vr
    zv[1] = vi
    cr, ci = vr, vi
    for _ in range(3):
        cr, ci = cmul(cr, ci, cr, ci)
    zrow[4] = cr
    zrow[5] = ci

    last = dot(pick[:, pick.shape[1] - rows :], table[...])
    coef[...] = (coef_early[...].astype(F32) + last).astype(BF16)

    block = 32
    for m in range(8):
        beams = dot(coef[...], weights[m])
        for n in range(0, number, block):
            first = beams[n : n + block, :]
            second = beams[number + n : number + n + block, :]
            f_re, f_im, s_re, s_im = first[:, :128], first[:, 128:], second[:, :128], second[:, 128:]
            g_re = f_re * s_re + f_im * s_im
            g_im = f_im * s_re - f_re * s_im
            i_re = image[m, n : n + block, :128].astype(F32)
            i_im = image[m, n : n + block, 128:].astype(F32)
            to = pl.ds(n * 8 + m, block, stride=8)
            wre[to, :] = i_re * g_re - i_im * g_im
            wim[to, :] = i_re * g_im + i_im * g_re

    unroll = 256

    def one(g):
        at = pl.ds(pl.multiple_of(g * 8, 8), 8)
        w_re, w_im = wre[at, :], wim[at, :]
        lhs = [
            jnp.concatenate([w_re[:, n : n + 32], w_im[:, n : n + 32]], axis=1)
            for n in range(0, 128, 32)
        ]
        lhs = jnp.concatenate(lhs, axis=0).astype(BF16)
        p_re, p_im = pure[at, :], puim[at, :]
        z = [jnp.broadcast_to(zrow[k, pl.ds(g, 1), :], (8, 128)) for k in range(6)]
        rr, ii, ri, ir = p_re * z[0], p_im * z[1], p_re * z[1], p_im * z[0]
        up_re, up_im = rr - ii, ri + ir
        dn_re, dn_im = rr + ii, ir - ri
        rr, ii, ri, ir = p_re * z[2], p_im * z[3], p_re * z[3], p_im * z[2]
        lo_re, lo_im = rr + ii, ir - ri
        c = jnp.concatenate([lo_re, dn_re, p_re, up_re], axis=0).astype(BF16)
        s = jnp.concatenate([lo_im, dn_im, p_im, up_im], axis=0).astype(BF16)
        top = jnp.concatenate([c, s], axis=1)
        low = jnp.concatenate([-s, c], axis=1)
        rhs = jnp.concatenate([top, low], axis=0)
        out = dot(lhs, rhs)
        h_re, h_im = out[24:32, :128], out[24:32, 128:]
        for j in (2, 1, 0):
            n_re = h_re * z[4] - h_im * z[5] + out[8 * j : 8 * j + 8, :128]
            h_im = h_re * z[5] + h_im * z[4] + out[8 * j : 8 * j + 8, 128:]
            h_re = n_re
        hre[at, :] = h_re
        him[at, :] = h_im

    @pl.loop(0, number // unroll)
    def _(n):
        for k in range(unroll):
            one(n * unroll + k)

    vr, vi = zv[0], zv[1]
    a_re = hre[pl.ds(7, number, stride=8), :]
    a_im = him[pl.ds(7, number, stride=8), :]
    for k in range(6, -1, -1):
        n_re = a_re * vr - a_im * vi + hre[pl.ds(k, number, stride=8), :]
        a_im = a_re * vi + a_im * vr + him[pl.ds(k, number, stride=8), :]
        a_re = n_re
    cr, ci = cmul(zrow[4], zrow[5], zrow[4], zrow[5])
    m_re, m_im = a_re * cr + a_im * ci, a_im * cr - a_re * ci
    models = jnp.concatenate([m_re, m_im], axis=1).astype(BF16)
    sent = dot(back[...], models)
    interleaved[pl.ds(0, slots, stride=2), :] = sent[:, :128]
    interleaved[pl.ds(1, slots, stride=2), :] = sent[:, 128:]
    along_z, in_plane = refs[:outer], refs[outer : outer + 4]
    for r in range(outer):
        for p in range(4):
            start = (p * outer + r) * (2 * capacity)
            along_z[r][p] = interleaved[start : start + capacity, :].astype(BF16)
            in_plane[p][r] = interleaved[start + capacity : start + 2 * capacity, :].astype(BF16)


def turn_kernel(*refs, order):
    blocks, out = refs[: len(order)], refs[len(order) :]
    for i, block in zip(order, blocks):
        for j in range(len(out)):
            out[j][i] = block[j]


def residual_kernel(me, observed, *refs, along_z, in_plane, outer):
    arrived, (out, kept, sems) = refs[: len(along_z) + len(in_plane)], refs[-3:]
    rows = kept.shape[1]
    pieces = [(r, p, rows, arrived[n].at[p]) for n, r in enumerate(along_z) for p in range(4)]
    pieces += [
        (r, p, 0, arrived[len(along_z) + n].at[r]) for n, p in enumerate(in_plane) for r in range(outer)
    ]
    copies = []
    for n, (r, p, start, values) in enumerate(pieces):
        source = me[0] ^ (4 * r + p)
        kept[n] = observed[source, start : start + rows, :] - values[...].astype(F32)
        copy = pltpu.make_async_copy(kept.at[n], out.at[source, pl.ds(start, rows), :], sems.at[n])
        copy.start()
        copies.append(copy)
    for copy in copies:
        copy.wait()


def exchange(value, step, tiles):
    return lax.ppermute(value, "tile", [(i, i ^ step) for i in range(tiles)])


def per_device(
    subgrids,
    stations,
    time_slots,
    assign,
    counts,
    beam_coefs,
    beam_basis,
    frequencies,
    uv_tracks,
    observed,
):
    tiles = lax.axis_size("tile")
    capacity = assign.shape[2]
    slots = tiles * capacity
    number = subgrids.shape[0]
    pixels = subgrids.shape[2]
    edge = math.isqrt(pixels)
    slot_count = beam_coefs.shape[1]
    terms2 = beam_coefs.shape[2]
    steps = uv_tracks.shape[4]
    chan = frequencies.shape[0]
    vis = steps * chan
    vmem = pl.BlockSpec(memory_space=pltpu.VMEM)
    own_tracks = jnp.transpose(uv_tracks[0], (0, 2, 3, 1)).reshape(tiles, 2 * steps, capacity)
    own_rows = beam_coefs.shape[0] * slot_count
    smem = pl.BlockSpec(memory_space=pltpu.SMEM)
    anywhere = pl.BlockSpec(memory_space=pl.ANY)
    hbm = pl.BlockSpec(memory_space=pltpu.HBM)
    outer = tiles // 4
    me = lax.axis_index("tile").astype(jnp.int32).reshape(1)
    block = jax.ShapeDtypeStruct((2 * own_rows + 8 * steps, 128), BF16)
    block_y = jax.ShapeDtypeStruct((2 * own_rows + 4 * steps, 128), BF16)
    packed = pl.pallas_call(
        pack_kernel,
        out_shape=[block] * outer,
        in_specs=[smem, hbm, hbm],
        out_specs=[vmem] * outer,
        scratch_shapes=[
            pltpu.VMEM((own_rows, terms2), BF16),
            pltpu.VMEM((tiles, 2 * steps, capacity), F32),
            pltpu.SemaphoreType.DMA((2,)),
        ],
        compiler_params=pltpu.CompilerParams(vmem_limit_bytes=56 * MIB),
        name="pack",
    )(me, beam_coefs.reshape(own_rows, terms2), own_tracks)
    along = [packed[0]] + [exchange(packed[r], 4 * r, tiles) for r in range(1, outer)]

    cells = jnp.transpose(subgrids.reshape(number, 2, 8, 128), (0, 2, 1, 3))
    cells = cells.reshape(number * 16, 128)
    row_turns, cell_turns = transform_tables(edge)
    image = pl.pallas_call(
        transform_kernel,
        out_shape=jax.ShapeDtypeStruct((8, number, 256), BF16),
        in_specs=[vmem] * 3,
        out_specs=vmem,
        scratch_shapes=[
            pltpu.VMEM((8, 256, 256), BF16),
            pltpu.VMEM((8, 256, 256), BF16),
            pltpu.VMEM((number * 16, 128), F32),
            pltpu.VMEM((8, number, 512), BF16),
        ],
        compiler_params=pltpu.CompilerParams(vmem_limit_bytes=14 * MIB),
        name="transform",
    )(cells, jnp.asarray(row_turns), jnp.asarray(cell_turns))

    near, for_y = pl.pallas_call(
        stack_kernel,
        out_shape=[
            jax.ShapeDtypeStruct((outer,) + block.shape, BF16),
            jax.ShapeDtypeStruct((outer,) + block_y.shape, BF16),
        ],
        in_specs=[smem] + [vmem] * outer + [anywhere],
        out_specs=[vmem] * 2,
        compiler_params=pltpu.CompilerParams(vmem_limit_bytes=3 * MIB * (tiles // 16)),
        name="stack",
    )(me, *along[::-1], image)
    over_core = exchange(near, 1, tiles)
    over_y = exchange(for_y, 2, tiles)
    route, back, pick, weights, turns = pl.pallas_call(
        functools.partial(prepare_kernel, slot_count=slot_count),
        out_shape=[
            jax.ShapeDtypeStruct((number, slots), BF16),
            jax.ShapeDtypeStruct((slots, number), BF16),
            jax.ShapeDtypeStruct((2 * number, tiles * own_rows), BF16),
            jax.ShapeDtypeStruct((8, terms2, 256), BF16),
            jax.ShapeDtypeStruct((1, vis), F32),
        ],
        in_specs=[smem] * 2 + [vmem] * 5 + [anywhere],
        out_specs=[vmem] * 5,
        compiler_params=pltpu.CompilerParams(vmem_limit_bytes=8 * MIB * (1 + tiles // 64)),
        name="prepare",
    )(
        me,
        counts,
        assign[0],
        stations.T,
        time_slots.reshape(1, number),
        beam_basis,
        frequencies.reshape(1, chan),
        near,
    )

    over_y = pl.pallas_call(
        relay_kernel,
        out_shape=jax.ShapeDtypeStruct((outer,) + block_y.shape, BF16),
        in_specs=[vmem, anywhere],
        out_specs=vmem,
        compiler_params=pltpu.CompilerParams(vmem_limit_bytes=2 * MIB * (tiles // 16)),
        name="relay",
    )(over_y, weights)
    over_both = exchange(over_y, 1, tiles)
    coef_early, per_sub_early = pl.pallas_call(
        functools.partial(early_kernel, capacity=capacity),
        out_shape=[
            jax.ShapeDtypeStruct((2 * number, terms2), BF16),
            jax.ShapeDtypeStruct((number, 4 * steps), F32),
        ],
        in_specs=[smem] + [vmem] * 5,
        out_specs=[vmem] * 2,
        scratch_shapes=[pltpu.VMEM((3 * outer * own_rows, terms2), BF16)],
        compiler_params=pltpu.CompilerParams(vmem_limit_bytes=8 * MIB * (1 + tiles // 64)),
        name="early",
    )(me, near, over_core, over_y, route, pick)

    for_z = jax.ShapeDtypeStruct((4, capacity, vis), BF16)
    for_plane = jax.ShapeDtypeStruct((outer, capacity, vis), BF16)
    models = pl.pallas_call(
        predict_kernel,
        out_shape=[for_z] * outer + [for_plane] * 4,
        in_specs=[smem] + [vmem] * 9,
        out_specs=[vmem] * (outer + 4),
        scratch_shapes=[
            pltpu.VMEM((outer * own_rows, terms2), BF16),
            pltpu.VMEM((2 * number, terms2), BF16),
            pltpu.VMEM((number * 8, 128), F32),
            pltpu.VMEM((number * 8, 128), F32),
            pltpu.VMEM((number * 8, vis), F32),
            pltpu.VMEM((number * 8, vis), F32),
            pltpu.VMEM((6, number, vis), F32),
            pltpu.VMEM((number * 8, vis), F32),
            pltpu.VMEM((number * 8, vis), F32),
            pltpu.VMEM((2, number, vis), F32),
            pltpu.VMEM((2 * slots, vis), F32),
        ],
        compiler_params=pltpu.CompilerParams(vmem_limit_bytes=20 * MIB * (1 + tiles // 64)),
        name="predict",
    )(
        me,
        over_both,
        route,
        back,
        pick,
        weights,
        turns,
        image,
        coef_early,
        per_sub_early,
    )
    def turned(blocks, order, out_shape):
        return pl.pallas_call(
            functools.partial(turn_kernel, order=order),
            out_shape=out_shape,
            in_specs=[vmem] * len(blocks),
            out_specs=[vmem] * len(out_shape),
            compiler_params=pltpu.CompilerParams(vmem_limit_bytes=2 * MIB),
            name="turn",
        )(*[blocks[i] for i in order])

    first, second = models[:outer], models[outer:]
    second = [second[0]] + [exchange(second[p], p, tiles) for p in range(1, 4)]
    first = [first[0]] + [exchange(first[r], 4 * r, tiles) for r in range(1, outer)]
    second = turned(second, (1, 2, 3, 0), [for_z] * outer)
    second = [second[0]] + [exchange(second[r], 4 * r, tiles) for r in range(1, outer)]
    first = turned(first, tuple(range(outer))[::-1], [for_plane] * 4)
    first = [first[0]] + [exchange(first[p], p, tiles) for p in range(1, 4)]
    ours = observed.reshape(tiles, 2 * capacity, vis)

    def finish(name, along_z, in_plane, held):
        count = 4 * len(along_z) + outer * len(in_plane)
        arrived = [second[r] for r in along_z] + [first[p] for p in in_plane]
        return pl.pallas_call(
            functools.partial(residual_kernel, along_z=along_z, in_plane=in_plane, outer=outer),
            out_shape=jax.ShapeDtypeStruct(ours.shape, F32),
            in_specs=[smem] + [vmem] * (1 + len(arrived)) + [anywhere] * len(held),
            out_specs=anywhere,
            scratch_shapes=[
                pltpu.VMEM((count, capacity, vis), F32),
                pltpu.SemaphoreType.DMA((count,)),
            ],
            input_output_aliases={2 + len(arrived): 0} if held else {},
            compiler_params=pltpu.CompilerParams(vmem_limit_bytes=6 * MIB),
            name=name,
        )(me, ours, *arrived, *held)

    residual = finish("residual_early", (0, outer - 1), (0,), ())
    residual = finish("residual_last", tuple(range(1, outer - 1))[::-1], (1, 2, 3), (residual,))
    return residual.reshape(observed.shape)


def solution(mesh):
    return jax.shard_map(
        per_device,
        mesh=mesh,
        in_specs=(
            P(("grp", "tile"), None, None),
            P(("grp", "tile"), None),
            P(("grp", "tile")),
            P(("grp", "tile"), None, None),
            P(("grp", "tile"), None),
            P(("grp", "tile"), None, None),
            P(),
            P("grp"),
            P(("grp", "tile"), None, None, None, None),
            P(("grp", "tile"), None, None, None, None),
        ),
        out_specs=P(("grp", "tile"), None, None, None, None),
        check_vma=False,
    )
```

```python
import functools
import math

import jax
import jax.numpy as jnp
import numpy as np
from jax import lax
from jax.experimental import pallas as pl
from jax.experimental.pallas import tpu as pltpu
from jax.sharding import PartitionSpec as P

TWO_PI = 2.0 * math.pi
F32 = jnp.float32
BF16 = jnp.bfloat16
MIB = 1024 * 1024
NT = (((1,), (1,)), ((), ()))


def dot(a, b, dims=(((1,), (0,)), ((), ()))):
    return lax.dot_general(a, b, dims, preferred_element_type=F32)


def transform_tables(edge):
    low = edge // 8
    outer = np.arange(8)[:, None, None, None]
    b = np.arange(low)[None, :, None, None]
    inner = np.arange(low)[None, None, :, None]
    x = np.arange(edge)
    turns = np.broadcast_to(b * (outer + 8 * inner) % edge, (8, low, low, edge))
    rows = TWO_PI / edge * turns.reshape(8, low, low * edge)
    cells = TWO_PI / edge * np.tile(x[:, None] * x[None, :] % edge, (1, low))
    rows = np.stack([np.cos(rows), np.sin(rows)]).astype(np.float32)
    cells = (np.stack([np.cos(cells), np.sin(cells)]) / edge**2).astype(np.float32)
    return rows.reshape(2, 8 * low, low * edge), cells


def eight_point(re, im):
    half = math.sqrt(0.5)

    def four(r, i):
        s0r, s0i, d0r, d0i = r[0] + r[2], i[0] + i[2], r[0] - r[2], i[0] - i[2]
        s1r, s1i, d1r, d1i = r[1] + r[3], i[1] + i[3], r[1] - r[3], i[1] - i[3]
        return (
            [s0r + s1r, d0r - d1i, s0r - s1r, d0r + d1i],
            [s0i + s1i, d0i + d1r, s0i - s1i, d0i - d1r],
        )

    er, ei = four(re[0::2], im[0::2])
    orr, oi = four(re[1::2], im[1::2])
    tr = [orr[0], half * (orr[1] - oi[1]), -oi[2], -half * (orr[3] + oi[3])]
    ti = [oi[0], half * (orr[1] + oi[1]), orr[2], half * (orr[3] - oi[3])]
    out_re = [er[m] + tr[m] for m in range(4)] + [er[m] - tr[m] for m in range(4)]
    out_im = [ei[m] + ti[m] for m in range(4)] + [ei[m] - ti[m] for m in range(4)]
    return out_re, out_im


def transform_kernel(cells, row_turns, cell_turns, image, high, rest, wide, sums):
    number = image.shape[1]
    edge, span = cell_turns.shape[1:]
    low = span // edge
    cell_c, cell_s = cell_turns[0], cell_turns[1]
    for m in range(8):
        for k in range(low):
            at = m * low + k
            row_c, row_s = row_turns[0, at : at + 1, :], row_turns[1, at : at + 1, :]
            c = row_c * cell_c - row_s * cell_s
            s = row_s * cell_c + row_c * cell_s
            c_top, s_top = c.astype(BF16), s.astype(BF16)
            c_left = (c - c_top.astype(F32)).astype(BF16)
            s_left = (s - s_top.astype(F32)).astype(BF16)
            re = slice(k * edge, (k + 1) * edge)
            im = slice(span + k * edge, span + (k + 1) * edge)
            for held, cos_part, sin_part in ((high, c_top, s_top), (rest, c_left, s_left)):
                held[m, re, :span] = cos_part
                held[m, re, span:] = sin_part
                held[m, im, :span] = -sin_part
                held[m, im, span:] = cos_part
    step = 16

    @pl.loop(0, number // step, unroll=8)
    def _(n):
        rows = pl.ds(pl.multiple_of(n * step, step), step)
        span = pl.ds(pl.multiple_of(n * step * 16, step * 16), step * 16)
        wide[span, :] = cells[span, :].astype(F32)
        re = [wide[pl.ds(n * step * 16 + 2 * k, step, stride=16), :] for k in range(8)]
        im = [wide[pl.ds(n * step * 16 + 2 * k + 1, step, stride=16), :] for k in range(8)]
        out_re, out_im = eight_point(re, im)
        for m in range(8):
            value = jnp.concatenate([out_re[m], out_im[m]], axis=1)
            top = value.astype(BF16)
            sums[m, rows, :256] = top
            sums[m, rows, 256:] = (value - top.astype(F32)).astype(BF16)

    for m in range(8):
        both = sums[m]
        left = jnp.concatenate([both, both[:, :256]], axis=1)
        right = jnp.concatenate([high[m], high[m], rest[m]], axis=0)
        image[m] = dot(left, right).astype(BF16)


def relative(mine, place, tiles):
    outer = tiles // 4
    return mine ^ (4 * (place % outer) + place // outer)


def prepare_kernel(
    me, counts, assign, stations, time_slots, basis, freq, after, route, back, pick, weights, turns, *, slot_count
):
    number = route.shape[0]
    tiles, capacity = assign.shape
    outer = tiles // 4
    mine = me[0]
    scaled = freq[...] * (-1.0 / 32.0)
    turns[...] = jnp.concatenate([scaled] * (turns.shape[1] // freq.shape[1]), axis=1)

    per = 128 // capacity
    down = lax.broadcasted_iota(jnp.int32, (number, 128), 0)
    slot = lax.broadcasted_iota(jnp.int32, (1, capacity), 1)
    for n in range(tiles // per):
        chosen = []
        for place in range(n * per, (n + 1) * per):
            d = relative(mine, place, tiles)
            chosen.append(jnp.where(slot < counts[0, d], assign[pl.ds(d, 1), :], -1))
        hot = (jnp.concatenate(chosen, axis=1) == down).astype(F32)
        route[:, n * 128 : (n + 1) * 128] = hot.astype(BF16)
        back[n * 128 : (n + 1) * 128, :] = hot.T.astype(BF16)

    rows_own = pick.shape[1] // tiles
    each = rows_own // slot_count
    away = (stations[...] // each) ^ mine
    place = away % 4 * outer + away // 4
    index = place * rows_own + stations[...] % each * slot_count + time_slots[...]
    index = jnp.concatenate([index.astype(F32), jnp.zeros((6, number), F32)], axis=0).T
    index = index.astype(jnp.int32)
    across = lax.broadcasted_iota(jnp.int32, (number, pick.shape[1]), 1)
    for which in range(2):
        hot = (index[:, which : which + 1] == across).astype(F32)
        pick[which * number : (which + 1) * number, :] = hot.astype(BF16)

    terms = basis.shape[1]
    edge = math.isqrt(basis.shape[2])
    for m in range(8):
        starts = [(8 * n + m) * edge for n in range(edge // 8)]
        b_re = jnp.concatenate([basis[0, :, n : n + edge] for n in starts], axis=1)
        b_im = jnp.concatenate([basis[1, :, n : n + edge] for n in starts], axis=1)
        weights[m, :terms, :128] = b_re
        weights[m, :terms, 128:] = b_im
        weights[m, terms:, :128] = -b_im
        weights[m, terms:, 128:] = b_re


def unit_powers(turns):
    turns = turns - jnp.round(turns)
    angle = (0.5 * math.pi) * turns
    sq = angle * angle
    s = angle * (
        1.0 + sq * (-1.0 / 6 + sq * (1.0 / 120 + sq * (-1.0 / 5040 + sq * (1.0 / 362880))))
    )
    c = 1.0 + sq * (
        -0.5 + sq * (1.0 / 24 + sq * (-1.0 / 720 + sq * (1.0 / 40320 - sq * (1.0 / 3628800))))
    )
    for _ in range(2):
        c, s = 1.0 - 2.0 * (s * s), 2.0 * (s * c)
    return c, s


def cmul(ar, ai, br, bi):
    return ar * br - ai * bi, ar * bi + ai * br


def pack_kernel(me, coefs_hbm, tracks_hbm, *refs):
    out, (coefs, tracks, sems) = refs[:-3], refs[-3:]
    copies = [
        pltpu.make_async_copy(coefs_hbm, coefs, sems.at[0]),
        pltpu.make_async_copy(tracks_hbm, tracks, sems.at[1]),
    ]
    for copy in copies:
        copy.start()
    for copy in copies:
        copy.wait()
    capacity = tracks.shape[2]
    rows = coefs.shape[0]
    for r in range(len(out)):
        plane = (me[0] // 4) ^ r
        kept = []
        for k in (0, 2):
            tr = jnp.concatenate([tracks[plane * 4 + k], tracks[plane * 4 + k + 1]], axis=1)
            top = tr.astype(BF16).astype(F32)
            kept += [top, tr - top]
        pieces = jnp.concatenate(kept, axis=0)
        if 2 * capacity < 128:
            blank = jnp.zeros((pieces.shape[0], 128 - 2 * capacity), F32)
            pieces = jnp.concatenate([pieces, blank], axis=1)
        out[r][:rows, :] = coefs[:, :128]
        out[r][rows : 2 * rows, :] = coefs[:, 128:]
        out[r][2 * rows :, :] = pieces.astype(BF16)


def own_pair(pieces, device):
    half = pieces.shape[0] // 2
    return jnp.where(device & 2 == 0, pieces[:half, :], pieces[half:, :])


def stack_kernel(me, *refs):
    blocks, near, for_y = refs[:-3], refs[-2], refs[-1]
    table = 2 * for_y.shape[1] - near.shape[1]
    for r, block in enumerate(blocks[::-1]):
        near[r] = block[...]
        for_y[r, :table, :] = block[:table, :]
        tracks = own_pair(block[table:, :].astype(F32), me[0] ^ 2)
        for_y[r, table:, :] = tracks.astype(BF16)


def relay_kernel(block, after, out):
    out[...] = block[...]


def unpacked(mine, groups, table, rows_own, capacity):
    kept = []
    for arrived in groups:
        for r in range(arrived.shape[0]):
            at = slice(len(kept) * rows_own, (len(kept) + 1) * rows_own)
            table[at, :128] = arrived[r, :rows_own, :]
            table[at, 128:] = arrived[r, rows_own : 2 * rows_own, :]
            piece = arrived[r, 2 * rows_own :, :].astype(F32)
            if arrived.shape[1] == groups[0].shape[1] and len(groups) > 1:
                piece = own_pair(piece, mine)
            moved = jnp.where(mine & 1 == 0, piece, pltpu.roll(piece, 128 - capacity, 1))
            kept.append(moved[:, :capacity])
    per = 128 // capacity
    tiles = [jnp.concatenate(kept[n : n + per], axis=1) for n in range(0, len(kept), per)]
    return jnp.concatenate(tiles, axis=1).astype(BF16)


def early_kernel(me, near, over_core, over_y, route, pick, coef, per_sub, table, *, capacity):
    places = 3 * near.shape[0]
    rows = table.shape[0]
    pieces = unpacked(me[0], (near, over_core, over_y), table, rows // places, capacity)
    coef[...] = dot(pick[:, :rows], table[...]).astype(BF16)
    per_sub[...] = dot(route[:, : places * capacity], pieces, NT)


def predict_kernel(
    me,
    over_both,
    route,
    back,
    pick,
    weights,
    turns,
    image,
    coef_early,
    per_sub_early,
    *refs,
):
    table, coef, wre, wim, pure, puim, zrow, hre, him, zv, interleaved = refs[-11:]
    number = image.shape[1]
    slots = back.shape[0]
    outer = over_both.shape[0]
    capacity = slots // (4 * outer)
    rows = table.shape[0]
    vis = turns.shape[1]
    kinds = per_sub_early.shape[1] // 2
    steps = kinds // 2
    chan = vis // steps
    pieces = unpacked(me[0], (over_both,), table, rows // outer, capacity)

    per_sub = per_sub_early[...] + dot(route[:, slots - outer * capacity :], pieces, NT)
    per_sub = per_sub.astype(BF16)
    wide = 2 * steps * chan
    from_row = lax.broadcasted_iota(jnp.int32, (2 * kinds, wide), 0) % kinds
    to_lane = lax.broadcasted_iota(jnp.int32, (2 * kinds, wide), 1) // chan
    spread = (from_row == to_lane).astype(F32).astype(BF16)
    uv = dot(per_sub, spread)
    ur, ui = unit_powers(uv[:, :vis] * turns[...])
    vr, vi = unit_powers(uv[:, vis:] * turns[...])

    pure[pl.ds(0, number, stride=8), :] = jnp.ones_like(ur)
    puim[pl.ds(0, number, stride=8), :] = jnp.zeros_like(ur)
    pure[pl.ds(1, number, stride=8), :] = ur
    puim[pl.ds(1, number, stride=8), :] = ui
    cr, ci = ur, ui
    for k in range(2, 8):
        cr, ci = cmul(cr, ci, ur, ui)
        pure[pl.ds(k, number, stride=8), :] = cr
        puim[pl.ds(k, number, stride=8), :] = ci
    cr, ci = cmul(cr, ci, ur, ui)
    zrow[0] = cr
    zrow[1] = ci
    cr, ci = cmul(cr, ci, cr, ci)
    zrow[2] = cr
    zrow[3] = ci
    zv[0] = vr
    zv[1] = vi
    cr, ci = vr, vi
    for _ in range(3):
        cr, ci = cmul(cr, ci, cr, ci)
    zrow[4] = cr
    zrow[5] = ci

    last = dot(pick[:, pick.shape[1] - rows :], table[...])
    coef[...] = (coef_early[...].astype(F32) + last).astype(BF16)

    block = 32
    for m in range(8):
        beams = dot(coef[...], weights[m])
        for n in range(0, number, block):
            first = beams[n : n + block, :]
            second = beams[number + n : number + n + block, :]
            f_re, f_im, s_re, s_im = first[:, :128], first[:, 128:], second[:, :128], second[:, 128:]
            g_re = f_re * s_re + f_im * s_im
            g_im = f_im * s_re - f_re * s_im
            i_re = image[m, n : n + block, :128].astype(F32)
            i_im = image[m, n : n + block, 128:].astype(F32)
            to = pl.ds(n * 8 + m, block, stride=8)
            wre[to, :] = i_re * g_re - i_im * g_im
            wim[to, :] = i_re * g_im + i_im * g_re

    unroll = 128

    def one(g):
        at = pl.ds(pl.multiple_of(g * 8, 8), 8)
        w_re, w_im = wre[at, :], wim[at, :]
        lhs = [
            jnp.concatenate([w_re[:, n : n + 32], w_im[:, n : n + 32]], axis=1)
            for n in range(0, 128, 32)
        ]
        lhs = jnp.concatenate(lhs, axis=0).astype(BF16)
        p_re, p_im = pure[at, :], puim[at, :]
        z = [jnp.broadcast_to(zrow[k, pl.ds(g, 1), :], (8, 128)) for k in range(6)]
        rr, ii, ri, ir = p_re * z[0], p_im * z[1], p_re * z[1], p_im * z[0]
        up_re, up_im = rr - ii, ri + ir
        dn_re, dn_im = rr + ii, ir - ri
        rr, ii, ri, ir = p_re * z[2], p_im * z[3], p_re * z[3], p_im * z[2]
        lo_re, lo_im = rr + ii, ir - ri
        c = jnp.concatenate([lo_re, dn_re, p_re, up_re], axis=0).astype(BF16)
        s = jnp.concatenate([lo_im, dn_im, p_im, up_im], axis=0).astype(BF16)
        top = jnp.concatenate([c, s], axis=1)
        low = jnp.concatenate([-s, c], axis=1)
        rhs = jnp.concatenate([top, low], axis=0)
        out = dot(lhs, rhs)
        h_re, h_im = out[24:32, :128], out[24:32, 128:]
        for j in (2, 1, 0):
            n_re = h_re * z[4] - h_im * z[5] + out[8 * j : 8 * j + 8, :128]
            h_im = h_re * z[5] + h_im * z[4] + out[8 * j : 8 * j + 8, 128:]
            h_re = n_re
        hre[at, :] = h_re
        him[at, :] = h_im

    @pl.loop(0, number // unroll)
    def _(n):
        for k in range(unroll):
            one(n * unroll + k)

    vr, vi = zv[0], zv[1]
    a_re = hre[pl.ds(7, number, stride=8), :]
    a_im = him[pl.ds(7, number, stride=8), :]
    for k in range(6, -1, -1):
        n_re = a_re * vr - a_im * vi + hre[pl.ds(k, number, stride=8), :]
        a_im = a_re * vi + a_im * vr + him[pl.ds(k, number, stride=8), :]
        a_re = n_re
    cr, ci = cmul(zrow[4], zrow[5], zrow[4], zrow[5])
    m_re, m_im = a_re * cr + a_im * ci, a_im * cr - a_re * ci
    models = jnp.concatenate([m_re, m_im], axis=1).astype(BF16)
    sent = dot(back[...], models)
    interleaved[pl.ds(0, slots, stride=2), :] = sent[:, :128]
    interleaved[pl.ds(1, slots, stride=2), :] = sent[:, 128:]
    along_z, in_plane = refs[:outer], refs[outer : outer + 4]
    for r in range(outer):
        for p in range(4):
            start = (p * outer + r) * (2 * capacity)
            along_z[r][p] = interleaved[start : start + capacity, :].astype(BF16)
            in_plane[p][r] = interleaved[start + capacity : start + 2 * capacity, :].astype(BF16)


def turn_kernel(*refs, order):
    blocks, out = refs[: len(order)], refs[len(order) :]
    for i, block in zip(order, blocks):
        for j in range(len(out)):
            out[j][i] = block[j]


def residual_kernel(me, observed, *refs, along_z, in_plane, outer):
    arrived, (out, kept, sems) = refs[: len(along_z) + len(in_plane)], refs[-3:]
    rows = kept.shape[1]
    pieces = [(r, p, rows, arrived[n].at[p]) for n, r in enumerate(along_z) for p in range(4)]
    pieces += [
        (r, p, 0, arrived[len(along_z) + n].at[r]) for n, p in enumerate(in_plane) for r in range(outer)
    ]
    copies = []
    for n, (r, p, start, values) in enumerate(pieces):
        source = me[0] ^ (4 * r + p)
        kept[n] = observed[source, start : start + rows, :] - values[...].astype(F32)
        copy = pltpu.make_async_copy(kept.at[n], out.at[source, pl.ds(start, rows), :], sems.at[n])
        copy.start()
        copies.append(copy)
    for copy in copies:
        copy.wait()


def exchange(value, step, tiles):
    return lax.ppermute(value, "tile", [(i, i ^ step) for i in range(tiles)])


def per_device(
    subgrids,
    stations,
    time_slots,
    assign,
    counts,
    beam_coefs,
    beam_basis,
    frequencies,
    uv_tracks,
    observed,
):
    tiles = lax.axis_size("tile")
    capacity = assign.shape[2]
    slots = tiles * capacity
    number = subgrids.shape[0]
    pixels = subgrids.shape[2]
    edge = math.isqrt(pixels)
    slot_count = beam_coefs.shape[1]
    terms2 = beam_coefs.shape[2]
    steps = uv_tracks.shape[4]
    chan = frequencies.shape[0]
    vis = steps * chan
    vmem = pl.BlockSpec(memory_space=pltpu.VMEM)
    own_tracks = jnp.transpose(uv_tracks[0], (0, 2, 3, 1)).reshape(tiles, 2 * steps, capacity)
    own_rows = beam_coefs.shape[0] * slot_count
    smem = pl.BlockSpec(memory_space=pltpu.SMEM)
    anywhere = pl.BlockSpec(memory_space=pl.ANY)
    hbm = pl.BlockSpec(memory_space=pltpu.HBM)
    outer = tiles // 4
    me = lax.axis_index("tile").astype(jnp.int32).reshape(1)
    block = jax.ShapeDtypeStruct((2 * own_rows + 8 * steps, 128), BF16)
    block_y = jax.ShapeDtypeStruct((2 * own_rows + 4 * steps, 128), BF16)
    packed = pl.pallas_call(
        pack_kernel,
        out_shape=[block] * outer,
        in_specs=[smem, hbm, hbm],
        out_specs=[vmem] * outer,
        scratch_shapes=[
            pltpu.VMEM((own_rows, terms2), BF16),
            pltpu.VMEM((tiles, 2 * steps, capacity), F32),
            pltpu.SemaphoreType.DMA((2,)),
        ],
        compiler_params=pltpu.CompilerParams(vmem_limit_bytes=56 * MIB),
        name="pack",
    )(me, beam_coefs.reshape(own_rows, terms2), own_tracks)
    along = [packed[0]] + [exchange(packed[r], 4 * r, tiles) for r in range(1, outer)]

    cells = jnp.transpose(subgrids.reshape(number, 2, 8, 128), (0, 2, 1, 3))
    cells = cells.reshape(number * 16, 128)
    row_turns, cell_turns = transform_tables(edge)
    image = pl.pallas_call(
        transform_kernel,
        out_shape=jax.ShapeDtypeStruct((8, number, 256), BF16),
        in_specs=[vmem] * 3,
        out_specs=vmem,
        scratch_shapes=[
            pltpu.VMEM((8, 256, 256), BF16),
            pltpu.VMEM((8, 256, 256), BF16),
            pltpu.VMEM((number * 16, 128), F32),
            pltpu.VMEM((8, number, 512), BF16),
        ],
        compiler_params=pltpu.CompilerParams(vmem_limit_bytes=14 * MIB),
        name="transform",
    )(cells, jnp.asarray(row_turns), jnp.asarray(cell_turns))

    near, for_y = pl.pallas_call(
        stack_kernel,
        out_shape=[
            jax.ShapeDtypeStruct((outer,) + block.shape, BF16),
            jax.ShapeDtypeStruct((outer,) + block_y.shape, BF16),
        ],
        in_specs=[smem] + [vmem] * outer + [anywhere],
        out_specs=[vmem] * 2,
        compiler_params=pltpu.CompilerParams(vmem_limit_bytes=3 * MIB * (tiles // 16)),
        name="stack",
    )(me, *along[::-1], image)
    over_core = exchange(near, 1, tiles)
    over_y = exchange(for_y, 2, tiles)
    route, back, pick, weights, turns = pl.pallas_call(
        functools.partial(prepare_kernel, slot_count=slot_count),
        out_shape=[
            jax.ShapeDtypeStruct((number, slots), BF16),
            jax.ShapeDtypeStruct((slots, number), BF16),
            jax.ShapeDtypeStruct((2 * number, tiles * own_rows), BF16),
            jax.ShapeDtypeStruct((8, terms2, 256), BF16),
            jax.ShapeDtypeStruct((1, vis), F32),
        ],
        in_specs=[smem] * 2 + [vmem] * 5 + [anywhere],
        out_specs=[vmem] * 5,
        compiler_params=pltpu.CompilerParams(vmem_limit_bytes=8 * MIB * (1 + tiles // 64)),
        name="prepare",
    )(
        me,
        counts,
        assign[0],
        stations.T,
        time_slots.reshape(1, number),
        beam_basis,
        frequencies.reshape(1, chan),
        near,
    )

    over_y = pl.pallas_call(
        relay_kernel,
        out_shape=jax.ShapeDtypeStruct((outer,) + block_y.shape, BF16),
        in_specs=[vmem, anywhere],
        out_specs=vmem,
        compiler_params=pltpu.CompilerParams(vmem_limit_bytes=2 * MIB * (tiles // 16)),
        name="relay",
    )(over_y, weights)
    over_both = exchange(over_y, 1, tiles)
    coef_early, per_sub_early = pl.pallas_call(
        functools.partial(early_kernel, capacity=capacity),
        out_shape=[
            jax.ShapeDtypeStruct((2 * number, terms2), BF16),
            jax.ShapeDtypeStruct((number, 4 * steps), F32),
        ],
        in_specs=[smem] + [vmem] * 5,
        out_specs=[vmem] * 2,
        scratch_shapes=[pltpu.VMEM((3 * outer * own_rows, terms2), BF16)],
        compiler_params=pltpu.CompilerParams(vmem_limit_bytes=8 * MIB * (1 + tiles // 64)),
        name="early",
    )(me, near, over_core, over_y, route, pick)

    for_z = jax.ShapeDtypeStruct((4, capacity, vis), BF16)
    for_plane = jax.ShapeDtypeStruct((outer, capacity, vis), BF16)
    models = pl.pallas_call(
        predict_kernel,
        out_shape=[for_z] * outer + [for_plane] * 4,
        in_specs=[smem] + [vmem] * 9,
        out_specs=[vmem] * (outer + 4),
        scratch_shapes=[
            pltpu.VMEM((outer * own_rows, terms2), BF16),
            pltpu.VMEM((2 * number, terms2), BF16),
            pltpu.VMEM((number * 8, 128), F32),
            pltpu.VMEM((number * 8, 128), F32),
            pltpu.VMEM((number * 8, vis), F32),
            pltpu.VMEM((number * 8, vis), F32),
            pltpu.VMEM((6, number, vis), F32),
            pltpu.VMEM((number * 8, vis), F32),
            pltpu.VMEM((number * 8, vis), F32),
            pltpu.VMEM((2, number, vis), F32),
            pltpu.VMEM((2 * slots, vis), F32),
        ],
        compiler_params=pltpu.CompilerParams(vmem_limit_bytes=20 * MIB * (1 + tiles // 64)),
        name="predict",
    )(
        me,
        over_both,
        route,
        back,
        pick,
        weights,
        turns,
        image,
        coef_early,
        per_sub_early,
    )
    def turned(blocks, order, out_shape):
        return pl.pallas_call(
            functools.partial(turn_kernel, order=order),
            out_shape=out_shape,
            in_specs=[vmem] * len(blocks),
            out_specs=[vmem] * len(out_shape),
            compiler_params=pltpu.CompilerParams(vmem_limit_bytes=2 * MIB),
            name="turn",
        )(*[blocks[i] for i in order])

    first, second = models[:outer], models[outer:]
    second = [second[0]] + [exchange(second[p], p, tiles) for p in range(1, 4)]
    first = [first[0]] + [exchange(first[r], 4 * r, tiles) for r in range(1, outer)]
    second = turned(second, (1, 2, 3, 0), [for_z] * outer)
    second = [second[0]] + [exchange(second[r], 4 * r, tiles) for r in range(1, outer)]
    first = turned(first, tuple(range(outer))[::-1], [for_plane] * 4)
    first = [first[0]] + [exchange(first[p], p, tiles) for p in range(1, 4)]
    ours = observed.reshape(tiles, 2 * capacity, vis)

    def finish(name, along_z, in_plane, held):
        count = 4 * len(along_z) + outer * len(in_plane)
        arrived = [second[r] for r in along_z] + [first[p] for p in in_plane]
        return pl.pallas_call(
            functools.partial(residual_kernel, along_z=along_z, in_plane=in_plane, outer=outer),
            out_shape=jax.ShapeDtypeStruct(ours.shape, F32),
            in_specs=[smem] + [vmem] * (1 + len(arrived)) + [anywhere] * len(held),
            out_specs=anywhere,
            scratch_shapes=[
                pltpu.VMEM((count, capacity, vis), F32),
                pltpu.SemaphoreType.DMA((count,)),
            ],
            input_output_aliases={2 + len(arrived): 0} if held else {},
            compiler_params=pltpu.CompilerParams(vmem_limit_bytes=6 * MIB),
            name=name,
        )(me, ours, *arrived, *held)

    residual = finish("residual_early", (0, outer - 1), (0,), ())
    residual = finish("residual_last", tuple(range(1, outer - 1))[::-1], (3, 2, 1), (residual,))
    return residual.reshape(observed.shape)


def solution(mesh):
    return jax.shard_map(
        per_device,
        mesh=mesh,
        in_specs=(
            P(("grp", "tile"), None, None),
            P(("grp", "tile"), None),
            P(("grp", "tile")),
            P(("grp", "tile"), None, None),
            P(("grp", "tile"), None),
            P(("grp", "tile"), None, None),
            P(),
            P("grp"),
            P(("grp", "tile"), None, None, None, None),
            P(("grp", "tile"), None, None, None, None),
        ),
        out_specs=P(("grp", "tile"), None, None, None, None),
        check_vma=False,
    )
```

```python
import functools
import math

import jax
import jax.numpy as jnp
import numpy as np
from jax import lax
from jax.experimental import pallas as pl
from jax.experimental.pallas import tpu as pltpu
from jax.sharding import PartitionSpec as P

TWO_PI = 2.0 * math.pi
F32 = jnp.float32
BF16 = jnp.bfloat16
MIB = 1024 * 1024
NT = (((1,), (1,)), ((), ()))


def dot(a, b, dims=(((1,), (0,)), ((), ()))):
    return lax.dot_general(a, b, dims, preferred_element_type=F32)


def transform_tables(edge):
    low = edge // 8
    outer = np.arange(8)[:, None, None, None]
    b = np.arange(low)[None, :, None, None]
    inner = np.arange(low)[None, None, :, None]
    x = np.arange(edge)
    turns = np.broadcast_to(b * (outer + 8 * inner) % edge, (8, low, low, edge))
    rows = TWO_PI / edge * turns.reshape(8, low, low * edge)
    cells = TWO_PI / edge * np.tile(x[:, None] * x[None, :] % edge, (1, low))
    rows = np.stack([np.cos(rows), np.sin(rows)]).astype(np.float32)
    cells = (np.stack([np.cos(cells), np.sin(cells)]) / edge**2).astype(np.float32)
    return rows.reshape(2, 8 * low, low * edge), cells


def eight_point(re, im):
    half = math.sqrt(0.5)

    def four(r, i):
        s0r, s0i, d0r, d0i = r[0] + r[2], i[0] + i[2], r[0] - r[2], i[0] - i[2]
        s1r, s1i, d1r, d1i = r[1] + r[3], i[1] + i[3], r[1] - r[3], i[1] - i[3]
        return (
            [s0r + s1r, d0r - d1i, s0r - s1r, d0r + d1i],
            [s0i + s1i, d0i + d1r, s0i - s1i, d0i - d1r],
        )

    er, ei = four(re[0::2], im[0::2])
    orr, oi = four(re[1::2], im[1::2])
    tr = [orr[0], half * (orr[1] - oi[1]), -oi[2], -half * (orr[3] + oi[3])]
    ti = [oi[0], half * (orr[1] + oi[1]), orr[2], half * (orr[3] - oi[3])]
    out_re = [er[m] + tr[m] for m in range(4)] + [er[m] - tr[m] for m in range(4)]
    out_im = [ei[m] + ti[m] for m in range(4)] + [ei[m] - ti[m] for m in range(4)]
    return out_re, out_im


def transform_kernel(cells, row_turns, cell_turns, image, high, rest, wide, sums):
    number = image.shape[1]
    edge, span = cell_turns.shape[1:]
    low = span // edge
    cell_c, cell_s = cell_turns[0], cell_turns[1]
    for m in range(8):
        for k in range(low):
            at = m * low + k
            row_c, row_s = row_turns[0, at : at + 1, :], row_turns[1, at : at + 1, :]
            c = row_c * cell_c - row_s * cell_s
            s = row_s * cell_c + row_c * cell_s
            c_top, s_top = c.astype(BF16), s.astype(BF16)
            c_left = (c - c_top.astype(F32)).astype(BF16)
            s_left = (s - s_top.astype(F32)).astype(BF16)
            re = slice(k * edge, (k + 1) * edge)
            im = slice(span + k * edge, span + (k + 1) * edge)
            for held, cos_part, sin_part in ((high, c_top, s_top), (rest, c_left, s_left)):
                held[m, re, :span] = cos_part
                held[m, re, span:] = sin_part
                held[m, im, :span] = -sin_part
                held[m, im, span:] = cos_part
    step = 16

    @pl.loop(0, number // step, unroll=8)
    def _(n):
        rows = pl.ds(pl.multiple_of(n * step, step), step)
        span = pl.ds(pl.multiple_of(n * step * 16, step * 16), step * 16)
        wide[span, :] = cells[span, :].astype(F32)
        re = [wide[pl.ds(n * step * 16 + 2 * k, step, stride=16), :] for k in range(8)]
        im = [wide[pl.ds(n * step * 16 + 2 * k + 1, step, stride=16), :] for k in range(8)]
        out_re, out_im = eight_point(re, im)
        for m in range(8):
            value = jnp.concatenate([out_re[m], out_im[m]], axis=1)
            top = value.astype(BF16)
            sums[m, rows, :256] = top
            sums[m, rows, 256:] = (value - top.astype(F32)).astype(BF16)

    for m in range(8):
        both = sums[m]
        left = jnp.concatenate([both, both[:, :256]], axis=1)
        right = jnp.concatenate([high[m], high[m], rest[m]], axis=0)
        image[m] = dot(left, right).astype(BF16)


def relative(mine, place, tiles):
    outer = tiles // 4
    return mine ^ (4 * (place % outer) + place // outer)


def prepare_kernel(
    me, counts, assign, stations, time_slots, basis, freq, after, route, back, pick, weights, turns, *, slot_count
):
    number = route.shape[0]
    tiles, capacity = assign.shape
    outer = tiles // 4
    mine = me[0]
    scaled = freq[...] * (-1.0 / 32.0)
    turns[...] = jnp.concatenate([scaled] * (turns.shape[1] // freq.shape[1]), axis=1)

    per = 128 // capacity
    down = lax.broadcasted_iota(jnp.int32, (number, 128), 0)
    slot = lax.broadcasted_iota(jnp.int32, (1, capacity), 1)
    for n in range(tiles // per):
        chosen = []
        for place in range(n * per, (n + 1) * per):
            d = relative(mine, place, tiles)
            chosen.append(jnp.where(slot < counts[0, d], assign[pl.ds(d, 1), :], -1))
        hot = (jnp.concatenate(chosen, axis=1) == down).astype(F32)
        route[:, n * 128 : (n + 1) * 128] = hot.astype(BF16)
        back[n * 128 : (n + 1) * 128, :] = hot.T.astype(BF16)

    rows_own = pick.shape[1] // tiles
    each = rows_own // slot_count
    away = (stations[...] // each) ^ mine
    place = away % 4 * outer + away // 4
    index = place * rows_own + stations[...] % each * slot_count + time_slots[...]
    index = jnp.concatenate([index.astype(F32), jnp.zeros((6, number), F32)], axis=0).T
    index = index.astype(jnp.int32)
    across = lax.broadcasted_iota(jnp.int32, (number, pick.shape[1]), 1)
    for which in range(2):
        hot = (index[:, which : which + 1] == across).astype(F32)
        pick[which * number : (which + 1) * number, :] = hot.astype(BF16)

    terms = basis.shape[1]
    edge = math.isqrt(basis.shape[2])
    for m in range(8):
        starts = [(8 * n + m) * edge for n in range(edge // 8)]
        b_re = jnp.concatenate([basis[0, :, n : n + edge] for n in starts], axis=1)
        b_im = jnp.concatenate([basis[1, :, n : n + edge] for n in starts], axis=1)
        weights[m, :terms, :128] = b_re
        weights[m, :terms, 128:] = b_im
        weights[m, terms:, :128] = -b_im
        weights[m, terms:, 128:] = b_re


def unit_powers(turns):
    turns = turns - jnp.round(turns)
    angle = (0.5 * math.pi) * turns
    sq = angle * angle
    s = angle * (
        1.0 + sq * (-1.0 / 6 + sq * (1.0 / 120 + sq * (-1.0 / 5040 + sq * (1.0 / 362880))))
    )
    c = 1.0 + sq * (
        -0.5 + sq * (1.0 / 24 + sq * (-1.0 / 720 + sq * (1.0 / 40320 - sq * (1.0 / 3628800))))
    )
    for _ in range(2):
        c, s = 1.0 - 2.0 * (s * s), 2.0 * (s * c)
    return c, s


def cmul(ar, ai, br, bi):
    return ar * br - ai * bi, ar * bi + ai * br


def pack_kernel(me, coefs_hbm, tracks_hbm, *refs):
    out, (coefs, tracks, sems) = refs[:-3], refs[-3:]
    copies = [
        pltpu.make_async_copy(coefs_hbm, coefs, sems.at[0]),
        pltpu.make_async_copy(tracks_hbm, tracks, sems.at[1]),
    ]
    for copy in copies:
        copy.start()
    for copy in copies:
        copy.wait()
    capacity = tracks.shape[2]
    rows = coefs.shape[0]
    for r in range(len(out)):
        plane = (me[0] // 4) ^ r
        kept = []
        for k in (0, 2):
            tr = jnp.concatenate([tracks[plane * 4 + k], tracks[plane * 4 + k + 1]], axis=1)
            top = tr.astype(BF16).astype(F32)
            kept += [top, tr - top]
        pieces = jnp.concatenate(kept, axis=0)
        if 2 * capacity < 128:
            blank = jnp.zeros((pieces.shape[0], 128 - 2 * capacity), F32)
            pieces = jnp.concatenate([pieces, blank], axis=1)
        out[r][:rows, :] = coefs[:, :128]
        out[r][rows : 2 * rows, :] = coefs[:, 128:]
        out[r][2 * rows :, :] = pieces.astype(BF16)


def own_pair(pieces, device):
    half = pieces.shape[0] // 2
    return jnp.where(device & 2 == 0, pieces[:half, :], pieces[half:, :])


def stack_kernel(me, *refs):
    blocks, near, for_y = refs[:-3], refs[-2], refs[-1]
    table = 2 * for_y.shape[1] - near.shape[1]
    for r, block in enumerate(blocks[::-1]):
        near[r] = block[...]
        for_y[r, :table, :] = block[:table, :]
        tracks = own_pair(block[table:, :].astype(F32), me[0] ^ 2)
        for_y[r, table:, :] = tracks.astype(BF16)


def relay_kernel(block, after, out):
    out[...] = block[...]


def unpacked(mine, groups, table, rows_own, capacity):
    kept = []
    for arrived in groups:
        for r in range(arrived.shape[0]):
            at = slice(len(kept) * rows_own, (len(kept) + 1) * rows_own)
            table[at, :128] = arrived[r, :rows_own, :]
            table[at, 128:] = arrived[r, rows_own : 2 * rows_own, :]
            piece = arrived[r, 2 * rows_own :, :].astype(F32)
            if arrived.shape[1] == groups[0].shape[1] and len(groups) > 1:
                piece = own_pair(piece, mine)
            moved = jnp.where(mine & 1 == 0, piece, pltpu.roll(piece, 128 - capacity, 1))
            kept.append(moved[:, :capacity])
    per = 128 // capacity
    tiles = [jnp.concatenate(kept[n : n + per], axis=1) for n in range(0, len(kept), per)]
    return jnp.concatenate(tiles, axis=1).astype(BF16)


def early_kernel(me, near, over_core, over_y, route, pick, coef, per_sub, table, *, capacity):
    places = 3 * near.shape[0]
    rows = table.shape[0]
    pieces = unpacked(me[0], (near, over_core, over_y), table, rows // places, capacity)
    coef[...] = dot(pick[:, :rows], table[...]).astype(BF16)
    per_sub[...] = dot(route[:, : places * capacity], pieces, NT)


def predict_kernel(
    me,
    over_both,
    route,
    back,
    pick,
    weights,
    turns,
    image,
    coef_early,
    per_sub_early,
    *refs,
):
    table, coef, wre, wim, pure, puim, zrow, hre, him, zv, interleaved = refs[-11:]
    number = image.shape[1]
    slots = back.shape[0]
    outer = over_both.shape[0]
    capacity = slots // (4 * outer)
    rows = table.shape[0]
    vis = turns.shape[1]
    kinds = per_sub_early.shape[1] // 2
    steps = kinds // 2
    chan = vis // steps
    pieces = unpacked(me[0], (over_both,), table, rows // outer, capacity)

    per_sub = per_sub_early[...] + dot(route[:, slots - outer * capacity :], pieces, NT)
    per_sub = per_sub.astype(BF16)
    wide = 2 * steps * chan
    from_row = lax.broadcasted_iota(jnp.int32, (2 * kinds, wide), 0) % kinds
    to_lane = lax.broadcasted_iota(jnp.int32, (2 * kinds, wide), 1) // chan
    spread = (from_row == to_lane).astype(F32).astype(BF16)
    uv = dot(per_sub, spread)
    ur, ui = unit_powers(uv[:, :vis] * turns[...])
    vr, vi = unit_powers(uv[:, vis:] * turns[...])

    pure[pl.ds(0, number, stride=8), :] = jnp.ones_like(ur)
    puim[pl.ds(0, number, stride=8), :] = jnp.zeros_like(ur)
    pure[pl.ds(1, number, stride=8), :] = ur
    puim[pl.ds(1, number, stride=8), :] = ui
    cr, ci = ur, ui
    for k in range(2, 8):
        cr, ci = cmul(cr, ci, ur, ui)
        pure[pl.ds(k, number, stride=8), :] = cr
        puim[pl.ds(k, number, stride=8), :] = ci
    cr, ci = cmul(cr, ci, ur, ui)
    zrow[0] = cr
    zrow[1] = ci
    cr, ci = cmul(cr, ci, cr, ci)
    zrow[2] = cr
    zrow[3] = ci
    zv[0] = vr
    zv[1] = vi
    cr, ci = vr, vi
    for _ in range(3):
        cr, ci = cmul(cr, ci, cr, ci)
    zrow[4] = cr
    zrow[5] = ci

    last = dot(pick[:, pick.shape[1] - rows :], table[...])
    coef[...] = (coef_early[...].astype(F32) + last).astype(BF16)

    block = 32
    for m in range(8):
        beams = dot(coef[...], weights[m])
        for n in range(0, number, block):
            first = beams[n : n + block, :]
            second = beams[number + n : number + n + block, :]
            f_re, f_im, s_re, s_im = first[:, :128], first[:, 128:], second[:, :128], second[:, 128:]
            g_re = f_re * s_re + f_im * s_im
            g_im = f_im * s_re - f_re * s_im
            i_re = image[m, n : n + block, :128].astype(F32)
            i_im = image[m, n : n + block, 128:].astype(F32)
            to = pl.ds(n * 8 + m, block, stride=8)
            wre[to, :] = i_re * g_re - i_im * g_im
            wim[to, :] = i_re * g_im + i_im * g_re

    unroll = 128

    def one(g):
        at = pl.ds(pl.multiple_of(g * 8, 8), 8)
        w_re, w_im = wre[at, :], wim[at, :]
        lhs = [
            jnp.concatenate([w_re[:, n : n + 32], w_im[:, n : n + 32]], axis=1)
            for n in range(0, 128, 32)
        ]
        lhs = jnp.concatenate(lhs, axis=0).astype(BF16)
        p_re, p_im = pure[at, :], puim[at, :]
        z = [jnp.broadcast_to(zrow[k, pl.ds(g, 1), :], (8, 128)) for k in range(6)]
        rr, ii, ri, ir = p_re * z[0], p_im * z[1], p_re * z[1], p_im * z[0]
        up_re, up_im = rr - ii, ri + ir
        dn_re, dn_im = rr + ii, ir - ri
        rr, ii, ri, ir = p_re * z[2], p_im * z[3], p_re * z[3], p_im * z[2]
        lo_re, lo_im = rr + ii, ir - ri
        c = jnp.concatenate([lo_re, dn_re, p_re, up_re], axis=0).astype(BF16)
        s = jnp.concatenate([lo_im, dn_im, p_im, up_im], axis=0).astype(BF16)
        top = jnp.concatenate([c, s], axis=1)
        low = jnp.concatenate([-s, c], axis=1)
        rhs = jnp.concatenate([top, low], axis=0)
        out = dot(lhs, rhs)
        h_re, h_im = out[24:32, :128], out[24:32, 128:]
        for j in (2, 1, 0):
            n_re = h_re * z[4] - h_im * z[5] + out[8 * j : 8 * j + 8, :128]
            h_im = h_re * z[5] + h_im * z[4] + out[8 * j : 8 * j + 8, 128:]
            h_re = n_re
        hre[at, :] = h_re
        him[at, :] = h_im

    @pl.loop(0, number // unroll)
    def _(n):
        for k in range(unroll):
            one(n * unroll + k)

    vr, vi = zv[0], zv[1]
    a_re = hre[pl.ds(7, number, stride=8), :]
    a_im = him[pl.ds(7, number, stride=8), :]
    for k in range(6, -1, -1):
        n_re = a_re * vr - a_im * vi + hre[pl.ds(k, number, stride=8), :]
        a_im = a_re * vi + a_im * vr + him[pl.ds(k, number, stride=8), :]
        a_re = n_re
    cr, ci = cmul(zrow[4], zrow[5], zrow[4], zrow[5])
    m_re, m_im = a_re * cr + a_im * ci, a_im * cr - a_re * ci
    models = jnp.concatenate([m_re, m_im], axis=1).astype(BF16)
    sent = dot(back[...], models)
    interleaved[pl.ds(0, slots, stride=2), :] = sent[:, :128]
    interleaved[pl.ds(1, slots, stride=2), :] = sent[:, 128:]
    along_z, in_plane = refs[:outer], refs[outer : outer + 4]
    rows = along_z[0].shape[1]
    for r in range(outer):
        for p in range(4):
            start = (p * outer + r) * (2 * capacity)
            along_z[r][p] = interleaved[start : start + rows, :].astype(BF16)
            in_plane[p][r] = interleaved[start + rows : start + 2 * capacity, :].astype(BF16)


def turn_kernel(*refs, order):
    blocks, out = refs[: len(order)], refs[len(order) :]
    for i, block in zip(order, blocks):
        for j in range(len(out)):
            out[j][i] = block[j]


def residual_kernel(me, observed, *refs, along_z, in_plane, outer):
    arrived, (out, kept, sems) = refs[: len(along_z) + len(in_plane)], refs[-3:]
    rows = arrived[-1].shape[1]
    pieces = [(r, p, rows, arrived[n].at[p]) for n, r in enumerate(along_z) for p in range(4)]
    pieces += [
        (r, p, 0, arrived[len(along_z) + n].at[r]) for n, p in enumerate(in_plane) for r in range(outer)
    ]
    copies = []
    for n, (r, p, start, values) in enumerate(pieces):
        source = me[0] ^ (4 * r + p)
        count = values.shape[0]
        kept[n, :count, :] = observed[source, start : start + count, :] - values[...].astype(F32)
        copy = pltpu.make_async_copy(
            kept.at[n, pl.ds(0, count), :], out.at[source, pl.ds(start, count), :], sems.at[n]
        )
        copy.start()
        copies.append(copy)
    for copy in copies:
        copy.wait()


def exchange(value, step, tiles):
    return lax.ppermute(value, "tile", [(i, i ^ step) for i in range(tiles)])


def per_device(
    subgrids,
    stations,
    time_slots,
    assign,
    counts,
    beam_coefs,
    beam_basis,
    frequencies,
    uv_tracks,
    observed,
):
    tiles = lax.axis_size("tile")
    capacity = assign.shape[2]
    slots = tiles * capacity
    number = subgrids.shape[0]
    pixels = subgrids.shape[2]
    edge = math.isqrt(pixels)
    slot_count = beam_coefs.shape[1]
    terms2 = beam_coefs.shape[2]
    steps = uv_tracks.shape[4]
    chan = frequencies.shape[0]
    vis = steps * chan
    vmem = pl.BlockSpec(memory_space=pltpu.VMEM)
    own_tracks = jnp.transpose(uv_tracks[0], (0, 2, 3, 1)).reshape(tiles, 2 * steps, capacity)
    own_rows = beam_coefs.shape[0] * slot_count
    smem = pl.BlockSpec(memory_space=pltpu.SMEM)
    anywhere = pl.BlockSpec(memory_space=pl.ANY)
    hbm = pl.BlockSpec(memory_space=pltpu.HBM)
    outer = tiles // 4
    me = lax.axis_index("tile").astype(jnp.int32).reshape(1)
    block = jax.ShapeDtypeStruct((2 * own_rows + 8 * steps, 128), BF16)
    block_y = jax.ShapeDtypeStruct((2 * own_rows + 4 * steps, 128), BF16)
    packed = pl.pallas_call(
        pack_kernel,
        out_shape=[block] * outer,
        in_specs=[smem, hbm, hbm],
        out_specs=[vmem] * outer,
        scratch_shapes=[
            pltpu.VMEM((own_rows, terms2), BF16),
            pltpu.VMEM((tiles, 2 * steps, capacity), F32),
            pltpu.SemaphoreType.DMA((2,)),
        ],
        compiler_params=pltpu.CompilerParams(vmem_limit_bytes=56 * MIB),
        name="pack",
    )(me, beam_coefs.reshape(own_rows, terms2), own_tracks)
    along = [packed[0]] + [exchange(packed[r], 4 * r, tiles) for r in range(1, outer)]

    cells = jnp.transpose(subgrids.reshape(number, 2, 8, 128), (0, 2, 1, 3))
    cells = cells.reshape(number * 16, 128)
    row_turns, cell_turns = transform_tables(edge)
    image = pl.pallas_call(
        transform_kernel,
        out_shape=jax.ShapeDtypeStruct((8, number, 256), BF16),
        in_specs=[vmem] * 3,
        out_specs=vmem,
        scratch_shapes=[
            pltpu.VMEM((8, 256, 256), BF16),
            pltpu.VMEM((8, 256, 256), BF16),
            pltpu.VMEM((number * 16, 128), F32),
            pltpu.VMEM((8, number, 512), BF16),
        ],
        compiler_params=pltpu.CompilerParams(vmem_limit_bytes=14 * MIB),
        name="transform",
    )(cells, jnp.asarray(row_turns), jnp.asarray(cell_turns))

    near, for_y = pl.pallas_call(
        stack_kernel,
        out_shape=[
            jax.ShapeDtypeStruct((outer,) + block.shape, BF16),
            jax.ShapeDtypeStruct((outer,) + block_y.shape, BF16),
        ],
        in_specs=[smem] + [vmem] * outer + [anywhere],
        out_specs=[vmem] * 2,
        compiler_params=pltpu.CompilerParams(vmem_limit_bytes=3 * MIB * (tiles // 16)),
        name="stack",
    )(me, *along[::-1], image)
    over_core = exchange(near, 1, tiles)
    over_y = exchange(for_y, 2, tiles)
    route, back, pick, weights, turns = pl.pallas_call(
        functools.partial(prepare_kernel, slot_count=slot_count),
        out_shape=[
            jax.ShapeDtypeStruct((number, slots), BF16),
            jax.ShapeDtypeStruct((slots, number), BF16),
            jax.ShapeDtypeStruct((2 * number, tiles * own_rows), BF16),
            jax.ShapeDtypeStruct((8, terms2, 256), BF16),
            jax.ShapeDtypeStruct((1, vis), F32),
        ],
        in_specs=[smem] * 2 + [vmem] * 5 + [anywhere],
        out_specs=[vmem] * 5,
        compiler_params=pltpu.CompilerParams(vmem_limit_bytes=8 * MIB * (1 + tiles // 64)),
        name="prepare",
    )(
        me,
        counts,
        assign[0],
        stations.T,
        time_slots.reshape(1, number),
        beam_basis,
        frequencies.reshape(1, chan),
        near,
    )

    over_y = pl.pallas_call(
        relay_kernel,
        out_shape=jax.ShapeDtypeStruct((outer,) + block_y.shape, BF16),
        in_specs=[vmem, anywhere],
        out_specs=vmem,
        compiler_params=pltpu.CompilerParams(vmem_limit_bytes=2 * MIB * (tiles // 16)),
        name="relay",
    )(over_y, weights)
    over_both = exchange(over_y, 1, tiles)
    coef_early, per_sub_early = pl.pallas_call(
        functools.partial(early_kernel, capacity=capacity),
        out_shape=[
            jax.ShapeDtypeStruct((2 * number, terms2), BF16),
            jax.ShapeDtypeStruct((number, 4 * steps), F32),
        ],
        in_specs=[smem] + [vmem] * 5,
        out_specs=[vmem] * 2,
        scratch_shapes=[pltpu.VMEM((3 * outer * own_rows, terms2), BF16)],
        compiler_params=pltpu.CompilerParams(vmem_limit_bytes=8 * MIB * (1 + tiles // 64)),
        name="early",
    )(me, near, over_core, over_y, route, pick)

    rows_first = max(16, 2 * capacity * 3 // 8 // 16 * 16)
    rows_second = 2 * capacity - rows_first
    for_z = jax.ShapeDtypeStruct((4, rows_first, vis), BF16)
    for_plane = jax.ShapeDtypeStruct((outer, rows_second, vis), BF16)
    models = pl.pallas_call(
        predict_kernel,
        out_shape=[for_z] * outer + [for_plane] * 4,
        in_specs=[smem] + [vmem] * 9,
        out_specs=[vmem] * (outer + 4),
        scratch_shapes=[
            pltpu.VMEM((outer * own_rows, terms2), BF16),
            pltpu.VMEM((2 * number, terms2), BF16),
            pltpu.VMEM((number * 8, 128), F32),
            pltpu.VMEM((number * 8, 128), F32),
            pltpu.VMEM((number * 8, vis), F32),
            pltpu.VMEM((number * 8, vis), F32),
            pltpu.VMEM((6, number, vis), F32),
            pltpu.VMEM((number * 8, vis), F32),
            pltpu.VMEM((number * 8, vis), F32),
            pltpu.VMEM((2, number, vis), F32),
            pltpu.VMEM((2 * slots, vis), F32),
        ],
        compiler_params=pltpu.CompilerParams(vmem_limit_bytes=20 * MIB * (1 + tiles // 64)),
        name="predict",
    )(
        me,
        over_both,
        route,
        back,
        pick,
        weights,
        turns,
        image,
        coef_early,
        per_sub_early,
    )
    def turned(blocks, order, out_shape):
        return pl.pallas_call(
            functools.partial(turn_kernel, order=order),
            out_shape=out_shape,
            in_specs=[vmem] * len(blocks),
            out_specs=[vmem] * len(out_shape),
            compiler_params=pltpu.CompilerParams(vmem_limit_bytes=2 * MIB),
            name="turn",
        )(*[blocks[i] for i in order])

    first, second = models[:outer], models[outer:]
    second = [second[0]] + [exchange(second[p], p, tiles) for p in range(1, 4)]
    first = [first[0]] + [exchange(first[r], 4 * r, tiles) for r in range(1, outer)]
    second = turned(
        second, (1, 2, 3, 0), [jax.ShapeDtypeStruct((4, rows_second, vis), BF16)] * outer
    )
    second = [second[0]] + [exchange(second[r], 4 * r, tiles) for r in range(1, outer)]
    first = turned(
        first,
        tuple(range(outer))[::-1],
        [jax.ShapeDtypeStruct((outer, rows_first, vis), BF16)] * 4,
    )
    first = [first[0]] + [exchange(first[p], p, tiles) for p in range(1, 4)]
    ours = observed.reshape(tiles, 2 * capacity, vis)

    def finish(name, along_z, in_plane, held):
        count = 4 * len(along_z) + outer * len(in_plane)
        arrived = [second[r] for r in along_z] + [first[p] for p in in_plane]
        return pl.pallas_call(
            functools.partial(residual_kernel, along_z=along_z, in_plane=in_plane, outer=outer),
            out_shape=jax.ShapeDtypeStruct(ours.shape, F32),
            in_specs=[smem] + [vmem] * (1 + len(arrived)) + [anywhere] * len(held),
            out_specs=anywhere,
            scratch_shapes=[
                pltpu.VMEM((count, max(rows_first, rows_second), vis), F32),
                pltpu.SemaphoreType.DMA((count,)),
            ],
            input_output_aliases={2 + len(arrived): 0} if held else {},
            compiler_params=pltpu.CompilerParams(vmem_limit_bytes=6 * MIB),
            name=name,
        )(me, ours, *arrived, *held)

    residual = finish("residual_early", (0, outer - 1), (0,), ())
    residual = finish("residual_last", tuple(range(1, outer - 1))[::-1], (3, 2, 1), (residual,))
    return residual.reshape(observed.shape)


def solution(mesh):
    return jax.shard_map(
        per_device,
        mesh=mesh,
        in_specs=(
            P(("grp", "tile"), None, None),
            P(("grp", "tile"), None),
            P(("grp", "tile")),
            P(("grp", "tile"), None, None),
            P(("grp", "tile"), None),
            P(("grp", "tile"), None, None),
            P(),
            P("grp"),
            P(("grp", "tile"), None, None, None, None),
            P(("grp", "tile"), None, None, None, None),
        ),
        out_specs=P(("grp", "tile"), None, None, None, None),
        check_vma=False,
    )
```

```python
import functools
import math

import jax
import jax.numpy as jnp
import numpy as np
from jax import lax
from jax.experimental import pallas as pl
from jax.experimental.pallas import tpu as pltpu
from jax.sharding import PartitionSpec as P

TWO_PI = 2.0 * math.pi
F32 = jnp.float32
BF16 = jnp.bfloat16
MIB = 1024 * 1024
NT = (((1,), (1,)), ((), ()))


def dot(a, b, dims=(((1,), (0,)), ((), ()))):
    return lax.dot_general(a, b, dims, preferred_element_type=F32)


def transform_tables(edge):
    low = edge // 8
    outer = np.arange(8)[:, None, None, None]
    b = np.arange(low)[None, :, None, None]
    inner = np.arange(low)[None, None, :, None]
    x = np.arange(edge)
    turns = np.broadcast_to(b * (outer + 8 * inner) % edge, (8, low, low, edge))
    rows = TWO_PI / edge * turns.reshape(8, low, low * edge)
    cells = TWO_PI / edge * np.tile(x[:, None] * x[None, :] % edge, (1, low))
    rows = np.stack([np.cos(rows), np.sin(rows)]).astype(np.float32)
    cells = (np.stack([np.cos(cells), np.sin(cells)]) / edge**2).astype(np.float32)
    return rows.reshape(2, 8 * low, low * edge), cells


def eight_point(re, im):
    half = math.sqrt(0.5)

    def four(r, i):
        s0r, s0i, d0r, d0i = r[0] + r[2], i[0] + i[2], r[0] - r[2], i[0] - i[2]
        s1r, s1i, d1r, d1i = r[1] + r[3], i[1] + i[3], r[1] - r[3], i[1] - i[3]
        return (
            [s0r + s1r, d0r - d1i, s0r - s1r, d0r + d1i],
            [s0i + s1i, d0i + d1r, s0i - s1i, d0i - d1r],
        )

    er, ei = four(re[0::2], im[0::2])
    orr, oi = four(re[1::2], im[1::2])
    tr = [orr[0], half * (orr[1] - oi[1]), -oi[2], -half * (orr[3] + oi[3])]
    ti = [oi[0], half * (orr[1] + oi[1]), orr[2], half * (orr[3] - oi[3])]
    out_re = [er[m] + tr[m] for m in range(4)] + [er[m] - tr[m] for m in range(4)]
    out_im = [ei[m] + ti[m] for m in range(4)] + [ei[m] - ti[m] for m in range(4)]
    return out_re, out_im


def transform_kernel(cells, row_turns, cell_turns, image, high, rest, wide, sums):
    number = image.shape[1]
    edge, span = cell_turns.shape[1:]
    low = span // edge
    cell_c, cell_s = cell_turns[0], cell_turns[1]
    for m in range(8):
        for k in range(low):
            at = m * low + k
            row_c, row_s = row_turns[0, at : at + 1, :], row_turns[1, at : at + 1, :]
            c = row_c * cell_c - row_s * cell_s
            s = row_s * cell_c + row_c * cell_s
            c_top, s_top = c.astype(BF16), s.astype(BF16)
            c_left = (c - c_top.astype(F32)).astype(BF16)
            s_left = (s - s_top.astype(F32)).astype(BF16)
            re = slice(k * edge, (k + 1) * edge)
            im = slice(span + k * edge, span + (k + 1) * edge)
            for held, cos_part, sin_part in ((high, c_top, s_top), (rest, c_left, s_left)):
                held[m, re, :span] = cos_part
                held[m, re, span:] = sin_part
                held[m, im, :span] = -sin_part
                held[m, im, span:] = cos_part
    step = 16

    @pl.loop(0, number // step, unroll=8)
    def _(n):
        rows = pl.ds(pl.multiple_of(n * step, step), step)
        span = pl.ds(pl.multiple_of(n * step * 16, step * 16), step * 16)
        wide[span, :] = cells[span, :].astype(F32)
        re = [wide[pl.ds(n * step * 16 + 2 * k, step, stride=16), :] for k in range(8)]
        im = [wide[pl.ds(n * step * 16 + 2 * k + 1, step, stride=16), :] for k in range(8)]
        out_re, out_im = eight_point(re, im)
        for m in range(8):
            value = jnp.concatenate([out_re[m], out_im[m]], axis=1)
            top = value.astype(BF16)
            sums[m, rows, :256] = top
            sums[m, rows, 256:] = (value - top.astype(F32)).astype(BF16)

    for m in range(8):
        both = sums[m]
        left = jnp.concatenate([both, both[:, :256]], axis=1)
        right = jnp.concatenate([high[m], high[m], rest[m]], axis=0)
        image[m] = dot(left, right).astype(BF16)


def relative(mine, place, tiles):
    outer = tiles // 4
    return mine ^ (4 * (place % outer) + place // outer)


def prepare_kernel(
    me, counts, assign, stations, time_slots, basis, freq, after, route, back, pick, weights, turns, *, slot_count
):
    number = route.shape[0]
    tiles, capacity = assign.shape
    outer = tiles // 4
    mine = me[0]
    scaled = freq[...] * (-1.0 / 32.0)
    turns[...] = jnp.concatenate([scaled] * (turns.shape[1] // freq.shape[1]), axis=1)

    per = 128 // capacity
    down = lax.broadcasted_iota(jnp.int32, (number, 128), 0)
    slot = lax.broadcasted_iota(jnp.int32, (1, capacity), 1)
    for n in range(tiles // per):
        chosen = []
        for place in range(n * per, (n + 1) * per):
            d = relative(mine, place, tiles)
            chosen.append(jnp.where(slot < counts[0, d], assign[pl.ds(d, 1), :], -1))
        hot = (jnp.concatenate(chosen, axis=1) == down).astype(F32)
        route[:, n * 128 : (n + 1) * 128] = hot.astype(BF16)
        back[n * 128 : (n + 1) * 128, :] = hot.T.astype(BF16)

    rows_own = pick.shape[1] // tiles
    each = rows_own // slot_count
    away = (stations[...] // each) ^ mine
    place = away % 4 * outer + away // 4
    index = place * rows_own + stations[...] % each * slot_count + time_slots[...]
    index = jnp.concatenate([index.astype(F32), jnp.zeros((6, number), F32)], axis=0).T
    index = index.astype(jnp.int32)
    across = lax.broadcasted_iota(jnp.int32, (number, pick.shape[1]), 1)
    for which in range(2):
        hot = (index[:, which : which + 1] == across).astype(F32)
        pick[which * number : (which + 1) * number, :] = hot.astype(BF16)

    terms = basis.shape[1]
    edge = math.isqrt(basis.shape[2])
    for m in range(8):
        starts = [(8 * n + m) * edge for n in range(edge // 8)]
        b_re = jnp.concatenate([basis[0, :, n : n + edge] for n in starts], axis=1)
        b_im = jnp.concatenate([basis[1, :, n : n + edge] for n in starts], axis=1)
        weights[m, :terms, :128] = b_re
        weights[m, :terms, 128:] = b_im
        weights[m, terms:, :128] = -b_im
        weights[m, terms:, 128:] = b_re


def unit_powers(turns):
    turns = turns - jnp.round(turns)
    angle = (0.5 * math.pi) * turns
    sq = angle * angle
    s = angle * (
        1.0 + sq * (-1.0 / 6 + sq * (1.0 / 120 + sq * (-1.0 / 5040 + sq * (1.0 / 362880))))
    )
    c = 1.0 + sq * (
        -0.5 + sq * (1.0 / 24 + sq * (-1.0 / 720 + sq * (1.0 / 40320 - sq * (1.0 / 3628800))))
    )
    for _ in range(2):
        c, s = 1.0 - 2.0 * (s * s), 2.0 * (s * c)
    return c, s


def cmul(ar, ai, br, bi):
    return ar * br - ai * bi, ar * bi + ai * br


def pack_kernel(me, coefs_hbm, tracks_hbm, *refs):
    out, (coefs, tracks, sems) = refs[:-3], refs[-3:]
    copies = [
        pltpu.make_async_copy(coefs_hbm, coefs, sems.at[0]),
        pltpu.make_async_copy(tracks_hbm, tracks, sems.at[1]),
    ]
    for copy in copies:
        copy.start()
    for copy in copies:
        copy.wait()
    capacity = tracks.shape[2]
    rows = coefs.shape[0]
    for r in range(len(out)):
        plane = (me[0] // 4) ^ r
        kept = []
        for k in (0, 2):
            tr = jnp.concatenate([tracks[plane * 4 + k], tracks[plane * 4 + k + 1]], axis=1)
            top = tr.astype(BF16).astype(F32)
            kept += [top, tr - top]
        pieces = jnp.concatenate(kept, axis=0)
        if 2 * capacity < 128:
            blank = jnp.zeros((pieces.shape[0], 128 - 2 * capacity), F32)
            pieces = jnp.concatenate([pieces, blank], axis=1)
        out[r][:rows, :] = coefs[:, :128]
        out[r][rows : 2 * rows, :] = coefs[:, 128:]
        out[r][2 * rows :, :] = pieces.astype(BF16)


def own_pair(pieces, device):
    half = pieces.shape[0] // 2
    return jnp.where(device & 2 == 0, pieces[:half, :], pieces[half:, :])


def stack_kernel(me, *refs):
    blocks, near, for_y = refs[:-3], refs[-2], refs[-1]
    table = 2 * for_y.shape[1] - near.shape[1]
    for r, block in enumerate(blocks[::-1]):
        near[r] = block[...]
        for_y[r, :table, :] = block[:table, :]
        tracks = own_pair(block[table:, :].astype(F32), me[0] ^ 2)
        for_y[r, table:, :] = tracks.astype(BF16)


def relay_kernel(block, after, out):
    out[...] = block[...]


def unpacked(mine, groups, table, rows_own, capacity):
    kept = []
    for arrived in groups:
        for r in range(arrived.shape[0]):
            at = slice(len(kept) * rows_own, (len(kept) + 1) * rows_own)
            table[at, :128] = arrived[r, :rows_own, :]
            table[at, 128:] = arrived[r, rows_own : 2 * rows_own, :]
            piece = arrived[r, 2 * rows_own :, :].astype(F32)
            if arrived.shape[1] == groups[0].shape[1] and len(groups) > 1:
                piece = own_pair(piece, mine)
            moved = jnp.where(mine & 1 == 0, piece, pltpu.roll(piece, 128 - capacity, 1))
            kept.append(moved[:, :capacity])
    per = 128 // capacity
    tiles = [jnp.concatenate(kept[n : n + per], axis=1) for n in range(0, len(kept), per)]
    return jnp.concatenate(tiles, axis=1).astype(BF16)


def early_kernel(me, near, over_core, over_y, route, pick, coef, per_sub, table, *, capacity):
    places = 3 * near.shape[0]
    rows = table.shape[0]
    pieces = unpacked(me[0], (near, over_core, over_y), table, rows // places, capacity)
    coef[...] = dot(pick[:, :rows], table[...]).astype(BF16)
    per_sub[...] = dot(route[:, : places * capacity], pieces, NT)


def predict_kernel(
    me,
    over_both,
    route,
    back,
    pick,
    weights,
    turns,
    image,
    coef_early,
    per_sub_early,
    *refs,
):
    table, coef, wre, wim, pure, puim, zrow, hre, him, zv, interleaved = refs[-11:]
    number = image.shape[1]
    slots = back.shape[0]
    outer = over_both.shape[0]
    capacity = slots // (4 * outer)
    rows = table.shape[0]
    vis = turns.shape[1]
    kinds = per_sub_early.shape[1] // 2
    steps = kinds // 2
    chan = vis // steps
    pieces = unpacked(me[0], (over_both,), table, rows // outer, capacity)

    per_sub = per_sub_early[...] + dot(route[:, slots - outer * capacity :], pieces, NT)
    per_sub = per_sub.astype(BF16)
    wide = 2 * steps * chan
    from_row = lax.broadcasted_iota(jnp.int32, (2 * kinds, wide), 0) % kinds
    to_lane = lax.broadcasted_iota(jnp.int32, (2 * kinds, wide), 1) // chan
    spread = (from_row == to_lane).astype(F32).astype(BF16)
    uv = dot(per_sub, spread)
    ur, ui = unit_powers(uv[:, :vis] * turns[...])
    vr, vi = unit_powers(uv[:, vis:] * turns[...])

    pure[pl.ds(0, number, stride=8), :] = jnp.ones_like(ur)
    puim[pl.ds(0, number, stride=8), :] = jnp.zeros_like(ur)
    pure[pl.ds(1, number, stride=8), :] = ur
    puim[pl.ds(1, number, stride=8), :] = ui
    cr, ci = ur, ui
    for k in range(2, 8):
        cr, ci = cmul(cr, ci, ur, ui)
        pure[pl.ds(k, number, stride=8), :] = cr
        puim[pl.ds(k, number, stride=8), :] = ci
    cr, ci = cmul(cr, ci, ur, ui)
    zrow[0] = cr
    zrow[1] = ci
    cr, ci = cmul(cr, ci, cr, ci)
    zrow[2] = cr
    zrow[3] = ci
    zv[0] = vr
    zv[1] = vi
    cr, ci = vr, vi
    for _ in range(3):
        cr, ci = cmul(cr, ci, cr, ci)
    zrow[4] = cr
    zrow[5] = ci

    last = dot(pick[:, pick.shape[1] - rows :], table[...])
    coef[...] = (coef_early[...].astype(F32) + last).astype(BF16)

    block = 32
    for m in range(8):
        beams = dot(coef[...], weights[m])
        for n in range(0, number, block):
            first = beams[n : n + block, :]
            second = beams[number + n : number + n + block, :]
            f_re, f_im, s_re, s_im = first[:, :128], first[:, 128:], second[:, :128], second[:, 128:]
            g_re = f_re * s_re + f_im * s_im
            g_im = f_im * s_re - f_re * s_im
            i_re = image[m, n : n + block, :128].astype(F32)
            i_im = image[m, n : n + block, 128:].astype(F32)
            to = pl.ds(n * 8 + m, block, stride=8)
            wre[to, :] = i_re * g_re - i_im * g_im
            wim[to, :] = i_re * g_im + i_im * g_re

    unroll = 128

    def one(g):
        at = pl.ds(pl.multiple_of(g * 8, 8), 8)
        w_re, w_im = wre[at, :], wim[at, :]
        lhs = [
            jnp.concatenate([w_re[:, n : n + 32], w_im[:, n : n + 32]], axis=1)
            for n in range(0, 128, 32)
        ]
        lhs = jnp.concatenate(lhs, axis=0).astype(BF16)
        p_re, p_im = pure[at, :], puim[at, :]
        z = [jnp.broadcast_to(zrow[k, pl.ds(g, 1), :], (8, 128)) for k in range(6)]
        rr, ii, ri, ir = p_re * z[0], p_im * z[1], p_re * z[1], p_im * z[0]
        up_re, up_im = rr - ii, ri + ir
        dn_re, dn_im = rr + ii, ir - ri
        rr, ii, ri, ir = p_re * z[2], p_im * z[3], p_re * z[3], p_im * z[2]
        lo_re, lo_im = rr + ii, ir - ri
        c = jnp.concatenate([lo_re, dn_re, p_re, up_re], axis=0).astype(BF16)
        s = jnp.concatenate([lo_im, dn_im, p_im, up_im], axis=0).astype(BF16)
        top = jnp.concatenate([c, s], axis=1)
        low = jnp.concatenate([-s, c], axis=1)
        rhs = jnp.concatenate([top, low], axis=0)
        out = dot(lhs, rhs)
        h_re, h_im = out[24:32, :128], out[24:32, 128:]
        for j in (2, 1, 0):
            n_re = h_re * z[4] - h_im * z[5] + out[8 * j : 8 * j + 8, :128]
            h_im = h_re * z[5] + h_im * z[4] + out[8 * j : 8 * j + 8, 128:]
            h_re = n_re
        hre[at, :] = h_re
        him[at, :] = h_im

    @pl.loop(0, number // unroll)
    def _(n):
        for k in range(unroll):
            one(n * unroll + k)

    vr, vi = zv[0], zv[1]
    a_re = hre[pl.ds(7, number, stride=8), :]
    a_im = him[pl.ds(7, number, stride=8), :]
    for k in range(6, -1, -1):
        n_re = a_re * vr - a_im * vi + hre[pl.ds(k, number, stride=8), :]
        a_im = a_re * vi + a_im * vr + him[pl.ds(k, number, stride=8), :]
        a_re = n_re
    cr, ci = cmul(zrow[4], zrow[5], zrow[4], zrow[5])
    m_re, m_im = a_re * cr + a_im * ci, a_im * cr - a_re * ci
    models = jnp.concatenate([m_re, m_im], axis=1).astype(BF16)
    sent = dot(back[...], models)
    interleaved[pl.ds(0, slots, stride=2), :] = sent[:, :128]
    interleaved[pl.ds(1, slots, stride=2), :] = sent[:, 128:]
    along_z, in_plane = refs[:outer], refs[outer : outer + 4]
    for r in range(outer):
        for p in range(4):
            start = (p * outer + r) * (2 * capacity)
            along_z[r][p] = interleaved[start : start + capacity, :].astype(BF16)
            in_plane[p][r] = interleaved[start + capacity : start + 2 * capacity, :].astype(BF16)


def turn_kernel(*refs, order):
    blocks, out = refs[: len(order)], refs[len(order) :]
    for i, block in zip(order, blocks):
        for j in range(len(out)):
            out[j][i] = block[j]


def residual_kernel(me, observed, *refs, along_z, in_plane, outer):
    (out, kept, sems), arrived = refs[-3:], refs[:-3]
    arrived = arrived[len(arrived) - len(along_z) - len(in_plane) :]
    rows = kept.shape[1]
    pieces = [(r, p, rows, arrived[n].at[p]) for n, r in enumerate(along_z) for p in range(4)]
    pieces += [
        (r, p, 0, arrived[len(along_z) + n].at[r]) for n, p in enumerate(in_plane) for r in range(outer)
    ]
    copies = []
    for n, (r, p, start, values) in enumerate(pieces):
        source = me[0] ^ (4 * r + p)
        kept[n] = observed[source, start : start + rows, :] - values[...].astype(F32)
        copy = pltpu.make_async_copy(kept.at[n], out.at[source, pl.ds(start, rows), :], sems.at[n])
        copy.start()
        copies.append(copy)
    for copy in copies:
        copy.wait()


def exchange(value, step, tiles):
    return lax.ppermute(value, "tile", [(i, i ^ step) for i in range(tiles)])


def per_device(
    subgrids,
    stations,
    time_slots,
    assign,
    counts,
    beam_coefs,
    beam_basis,
    frequencies,
    uv_tracks,
    observed,
):
    tiles = lax.axis_size("tile")
    capacity = assign.shape[2]
    slots = tiles * capacity
    number = subgrids.shape[0]
    pixels = subgrids.shape[2]
    edge = math.isqrt(pixels)
    slot_count = beam_coefs.shape[1]
    terms2 = beam_coefs.shape[2]
    steps = uv_tracks.shape[4]
    chan = frequencies.shape[0]
    vis = steps * chan
    vmem = pl.BlockSpec(memory_space=pltpu.VMEM)
    own_tracks = jnp.transpose(uv_tracks[0], (0, 2, 3, 1)).reshape(tiles, 2 * steps, capacity)
    own_rows = beam_coefs.shape[0] * slot_count
    smem = pl.BlockSpec(memory_space=pltpu.SMEM)
    anywhere = pl.BlockSpec(memory_space=pl.ANY)
    hbm = pl.BlockSpec(memory_space=pltpu.HBM)
    outer = tiles // 4
    me = lax.axis_index("tile").astype(jnp.int32).reshape(1)
    block = jax.ShapeDtypeStruct((2 * own_rows + 8 * steps, 128), BF16)
    block_y = jax.ShapeDtypeStruct((2 * own_rows + 4 * steps, 128), BF16)
    packed = pl.pallas_call(
        pack_kernel,
        out_shape=[block] * outer,
        in_specs=[smem, hbm, hbm],
        out_specs=[vmem] * outer,
        scratch_shapes=[
            pltpu.VMEM((own_rows, terms2), BF16),
            pltpu.VMEM((tiles, 2 * steps, capacity), F32),
            pltpu.SemaphoreType.DMA((2,)),
        ],
        compiler_params=pltpu.CompilerParams(vmem_limit_bytes=56 * MIB),
        name="pack",
    )(me, beam_coefs.reshape(own_rows, terms2), own_tracks)
    along = [packed[0]] + [exchange(packed[r], 4 * r, tiles) for r in range(1, outer)]

    cells = jnp.transpose(subgrids.reshape(number, 2, 8, 128), (0, 2, 1, 3))
    cells = cells.reshape(number * 16, 128)
    row_turns, cell_turns = transform_tables(edge)
    image = pl.pallas_call(
        transform_kernel,
        out_shape=jax.ShapeDtypeStruct((8, number, 256), BF16),
        in_specs=[vmem] * 3,
        out_specs=vmem,
        scratch_shapes=[
            pltpu.VMEM((8, 256, 256), BF16),
            pltpu.VMEM((8, 256, 256), BF16),
            pltpu.VMEM((number * 16, 128), F32),
            pltpu.VMEM((8, number, 512), BF16),
        ],
        compiler_params=pltpu.CompilerParams(vmem_limit_bytes=14 * MIB),
        name="transform",
    )(cells, jnp.asarray(row_turns), jnp.asarray(cell_turns))

    near, for_y = pl.pallas_call(
        stack_kernel,
        out_shape=[
            jax.ShapeDtypeStruct((outer,) + block.shape, BF16),
            jax.ShapeDtypeStruct((outer,) + block_y.shape, BF16),
        ],
        in_specs=[smem] + [vmem] * outer + [anywhere],
        out_specs=[vmem] * 2,
        compiler_params=pltpu.CompilerParams(vmem_limit_bytes=3 * MIB * (tiles // 16)),
        name="stack",
    )(me, *along[::-1], image)
    over_core = exchange(near, 1, tiles)
    over_y = exchange(for_y, 2, tiles)
    route, back, pick, weights, turns = pl.pallas_call(
        functools.partial(prepare_kernel, slot_count=slot_count),
        out_shape=[
            jax.ShapeDtypeStruct((number, slots), BF16),
            jax.ShapeDtypeStruct((slots, number), BF16),
            jax.ShapeDtypeStruct((2 * number, tiles * own_rows), BF16),
            jax.ShapeDtypeStruct((8, terms2, 256), BF16),
            jax.ShapeDtypeStruct((1, vis), F32),
        ],
        in_specs=[smem] * 2 + [vmem] * 5 + [anywhere],
        out_specs=[vmem] * 5,
        compiler_params=pltpu.CompilerParams(vmem_limit_bytes=8 * MIB * (1 + tiles // 64)),
        name="prepare",
    )(
        me,
        counts,
        assign[0],
        stations.T,
        time_slots.reshape(1, number),
        beam_basis,
        frequencies.reshape(1, chan),
        near,
    )

    over_y = pl.pallas_call(
        relay_kernel,
        out_shape=jax.ShapeDtypeStruct((outer,) + block_y.shape, BF16),
        in_specs=[vmem, anywhere],
        out_specs=vmem,
        compiler_params=pltpu.CompilerParams(vmem_limit_bytes=2 * MIB * (tiles // 16)),
        name="relay",
    )(over_y, weights)
    over_both = exchange(over_y, 1, tiles)
    coef_early, per_sub_early = pl.pallas_call(
        functools.partial(early_kernel, capacity=capacity),
        out_shape=[
            jax.ShapeDtypeStruct((2 * number, terms2), BF16),
            jax.ShapeDtypeStruct((number, 4 * steps), F32),
        ],
        in_specs=[smem] + [vmem] * 5,
        out_specs=[vmem] * 2,
        scratch_shapes=[pltpu.VMEM((3 * outer * own_rows, terms2), BF16)],
        compiler_params=pltpu.CompilerParams(vmem_limit_bytes=8 * MIB * (1 + tiles // 64)),
        name="early",
    )(me, near, over_core, over_y, route, pick)

    for_z = jax.ShapeDtypeStruct((4, capacity, vis), BF16)
    for_plane = jax.ShapeDtypeStruct((outer, capacity, vis), BF16)
    models = pl.pallas_call(
        predict_kernel,
        out_shape=[for_z] * outer + [for_plane] * 4,
        in_specs=[smem] + [vmem] * 9,
        out_specs=[vmem] * (outer + 4),
        scratch_shapes=[
            pltpu.VMEM((outer * own_rows, terms2), BF16),
            pltpu.VMEM((2 * number, terms2), BF16),
            pltpu.VMEM((number * 8, 128), F32),
            pltpu.VMEM((number * 8, 128), F32),
            pltpu.VMEM((number * 8, vis), F32),
            pltpu.VMEM((number * 8, vis), F32),
            pltpu.VMEM((6, number, vis), F32),
            pltpu.VMEM((number * 8, vis), F32),
            pltpu.VMEM((number * 8, vis), F32),
            pltpu.VMEM((2, number, vis), F32),
            pltpu.VMEM((2 * slots, vis), F32),
        ],
        compiler_params=pltpu.CompilerParams(vmem_limit_bytes=20 * MIB * (1 + tiles // 64)),
        name="predict",
    )(
        me,
        over_both,
        route,
        back,
        pick,
        weights,
        turns,
        image,
        coef_early,
        per_sub_early,
    )
    def turned(blocks, order, out_shape):
        return pl.pallas_call(
            functools.partial(turn_kernel, order=order),
            out_shape=out_shape,
            in_specs=[vmem] * len(blocks),
            out_specs=[vmem] * len(out_shape),
            compiler_params=pltpu.CompilerParams(vmem_limit_bytes=2 * MIB),
            name="turn",
        )(*[blocks[i] for i in order])

    first, second = models[:outer], models[outer:]
    second = [second[0]] + [exchange(second[p], p, tiles) for p in range(1, 4)]
    first = [first[0]] + [exchange(first[r], 4 * r, tiles) for r in range(1, outer)]
    second = turned(second, (1, 2, 3, 0), [for_z] * outer)
    second = [second[0]] + [exchange(second[r], 4 * r, tiles) for r in range(1, outer)]
    first = turned(first, tuple(range(outer))[::-1], [for_plane] * 4)
    first = [first[0]] + [exchange(first[p], p, tiles) for p in range(1, 4)]
    ours = observed.reshape(tiles, 2 * capacity, vis)

    def finish(name, along_z, in_plane, held):
        count = 4 * len(along_z) + outer * len(in_plane)
        arrived = [second[r] for r in along_z] + [first[p] for p in in_plane]
        return pl.pallas_call(
            functools.partial(residual_kernel, along_z=along_z, in_plane=in_plane, outer=outer),
            out_shape=jax.ShapeDtypeStruct(ours.shape, F32),
            in_specs=[smem, vmem] + [anywhere] * len(held) + [vmem] * len(arrived),
            out_specs=anywhere,
            scratch_shapes=[
                pltpu.VMEM((count, capacity, vis), F32),
                pltpu.SemaphoreType.DMA((count,)),
            ],
            input_output_aliases={2: 0} if held else {},
            compiler_params=pltpu.CompilerParams(vmem_limit_bytes=6 * MIB),
            name=name,
        )(me, ours, *held, *arrived)

    residual = finish("residual_early", (0, outer - 1), (0,), ())
    residual = finish("residual_next", tuple(range(1, outer - 1))[::-1], (3,), (residual,))
    residual = finish("residual_last", (), (2, 1), (residual,))
    return residual.reshape(observed.shape)


def solution(mesh):
    return jax.shard_map(
        per_device,
        mesh=mesh,
        in_specs=(
            P(("grp", "tile"), None, None),
            P(("grp", "tile"), None),
            P(("grp", "tile")),
            P(("grp", "tile"), None, None),
            P(("grp", "tile"), None),
            P(("grp", "tile"), None, None),
            P(),
            P("grp"),
            P(("grp", "tile"), None, None, None, None),
            P(("grp", "tile"), None, None, None, None),
        ),
        out_specs=P(("grp", "tile"), None, None, None, None),
        check_vma=False,
    )
```

```python
import functools
import math

import jax
import jax.numpy as jnp
import numpy as np
from jax import lax
from jax.experimental import pallas as pl
from jax.experimental.pallas import tpu as pltpu
from jax.sharding import PartitionSpec as P

TWO_PI = 2.0 * math.pi
F32 = jnp.float32
BF16 = jnp.bfloat16
MIB = 1024 * 1024
NT = (((1,), (1,)), ((), ()))


def dot(a, b, dims=(((1,), (0,)), ((), ()))):
    return lax.dot_general(a, b, dims, preferred_element_type=F32)


def transform_tables(edge):
    low = edge // 8
    outer = np.arange(8)[:, None, None, None]
    b = np.arange(low)[None, :, None, None]
    inner = np.arange(low)[None, None, :, None]
    x = np.arange(edge)
    turns = np.broadcast_to(b * (outer + 8 * inner) % edge, (8, low, low, edge))
    rows = TWO_PI / edge * turns.reshape(8, low, low * edge)
    cells = TWO_PI / edge * np.tile(x[:, None] * x[None, :] % edge, (1, low))
    rows = np.stack([np.cos(rows), np.sin(rows)]).astype(np.float32)
    cells = (np.stack([np.cos(cells), np.sin(cells)]) / edge**2).astype(np.float32)
    return rows.reshape(2, 8 * low, low * edge), cells


def eight_point(re, im):
    half = math.sqrt(0.5)

    def four(r, i):
        s0r, s0i, d0r, d0i = r[0] + r[2], i[0] + i[2], r[0] - r[2], i[0] - i[2]
        s1r, s1i, d1r, d1i = r[1] + r[3], i[1] + i[3], r[1] - r[3], i[1] - i[3]
        return (
            [s0r + s1r, d0r - d1i, s0r - s1r, d0r + d1i],
            [s0i + s1i, d0i + d1r, s0i - s1i, d0i - d1r],
        )

    er, ei = four(re[0::2], im[0::2])
    orr, oi = four(re[1::2], im[1::2])
    tr = [orr[0], half * (orr[1] - oi[1]), -oi[2], -half * (orr[3] + oi[3])]
    ti = [oi[0], half * (orr[1] + oi[1]), orr[2], half * (orr[3] - oi[3])]
    out_re = [er[m] + tr[m] for m in range(4)] + [er[m] - tr[m] for m in range(4)]
    out_im = [ei[m] + ti[m] for m in range(4)] + [ei[m] - ti[m] for m in range(4)]
    return out_re, out_im


def transform_kernel(cells, row_turns, cell_turns, image, high, rest, wide, sums):
    number = image.shape[1]
    edge, span = cell_turns.shape[1:]
    low = span // edge
    cell_c, cell_s = cell_turns[0], cell_turns[1]
    for m in range(8):
        for k in range(low):
            at = m * low + k
            row_c, row_s = row_turns[0, at : at + 1, :], row_turns[1, at : at + 1, :]
            c = row_c * cell_c - row_s * cell_s
            s = row_s * cell_c + row_c * cell_s
            c_top, s_top = c.astype(BF16), s.astype(BF16)
            c_left = (c - c_top.astype(F32)).astype(BF16)
            s_left = (s - s_top.astype(F32)).astype(BF16)
            re = slice(k * edge, (k + 1) * edge)
            im = slice(span + k * edge, span + (k + 1) * edge)
            for held, cos_part, sin_part in ((high, c_top, s_top), (rest, c_left, s_left)):
                held[m, re, :span] = cos_part
                held[m, re, span:] = sin_part
                held[m, im, :span] = -sin_part
                held[m, im, span:] = cos_part
    step = 16

    @pl.loop(0, number // step, unroll=8)
    def _(n):
        rows = pl.ds(pl.multiple_of(n * step, step), step)
        span = pl.ds(pl.multiple_of(n * step * 16, step * 16), step * 16)
        wide[span, :] = cells[span, :].astype(F32)
        re = [wide[pl.ds(n * step * 16 + 2 * k, step, stride=16), :] for k in range(8)]
        im = [wide[pl.ds(n * step * 16 + 2 * k + 1, step, stride=16), :] for k in range(8)]
        out_re, out_im = eight_point(re, im)
        for m in range(8):
            value = jnp.concatenate([out_re[m], out_im[m]], axis=1)
            top = value.astype(BF16)
            sums[m, rows, :256] = top
            sums[m, rows, 256:] = (value - top.astype(F32)).astype(BF16)

    for m in range(8):
        both = sums[m]
        left = jnp.concatenate([both, both[:, :256]], axis=1)
        right = jnp.concatenate([high[m], high[m], rest[m]], axis=0)
        image[m] = dot(left, right).astype(BF16)


def relative(mine, place, tiles):
    outer = tiles // 4
    return mine ^ (4 * (place % outer) + place // outer)


def prepare_kernel(
    me, counts, assign, stations, time_slots, basis, freq, after, route, back, pick, weights, turns, *, slot_count
):
    number = route.shape[0]
    tiles, capacity = assign.shape
    outer = tiles // 4
    mine = me[0]
    scaled = freq[...] * (-1.0 / 32.0)
    turns[...] = jnp.concatenate([scaled] * (turns.shape[1] // freq.shape[1]), axis=1)

    per = 128 // capacity
    down = lax.broadcasted_iota(jnp.int32, (number, 128), 0)
    slot = lax.broadcasted_iota(jnp.int32, (1, capacity), 1)
    for n in range(tiles // per):
        chosen = []
        for place in range(n * per, (n + 1) * per):
            d = relative(mine, place, tiles)
            chosen.append(jnp.where(slot < counts[0, d], assign[pl.ds(d, 1), :], -1))
        hot = (jnp.concatenate(chosen, axis=1) == down).astype(F32)
        route[:, n * 128 : (n + 1) * 128] = hot.astype(BF16)
        back[n * 128 : (n + 1) * 128, :] = hot.T.astype(BF16)

    rows_own = pick.shape[1] // tiles
    each = rows_own // slot_count
    away = (stations[...] // each) ^ mine
    place = away % 4 * outer + away // 4
    index = place * rows_own + stations[...] % each * slot_count + time_slots[...]
    index = jnp.concatenate([index.astype(F32), jnp.zeros((6, number), F32)], axis=0).T
    index = index.astype(jnp.int32)
    across = lax.broadcasted_iota(jnp.int32, (number, pick.shape[1]), 1)
    for which in range(2):
        hot = (index[:, which : which + 1] == across).astype(F32)
        pick[which * number : (which + 1) * number, :] = hot.astype(BF16)

    terms = basis.shape[1]
    edge = math.isqrt(basis.shape[2])
    for m in range(8):
        starts = [(8 * n + m) * edge for n in range(edge // 8)]
        b_re = jnp.concatenate([basis[0, :, n : n + edge] for n in starts], axis=1)
        b_im = jnp.concatenate([basis[1, :, n : n + edge] for n in starts], axis=1)
        weights[m, :terms, :128] = b_re
        weights[m, :terms, 128:] = b_im
        weights[m, terms:, :128] = -b_im
        weights[m, terms:, 128:] = b_re


def unit_powers(turns):
    turns = turns - jnp.round(turns)
    angle = (0.5 * math.pi) * turns
    sq = angle * angle
    s = angle * (
        1.0 + sq * (-1.0 / 6 + sq * (1.0 / 120 + sq * (-1.0 / 5040 + sq * (1.0 / 362880))))
    )
    c = 1.0 + sq * (
        -0.5 + sq * (1.0 / 24 + sq * (-1.0 / 720 + sq * (1.0 / 40320 - sq * (1.0 / 3628800))))
    )
    for _ in range(2):
        c, s = 1.0 - 2.0 * (s * s), 2.0 * (s * c)
    return c, s


def cmul(ar, ai, br, bi):
    return ar * br - ai * bi, ar * bi + ai * br


def pack_kernel(me, coefs_hbm, tracks_hbm, *refs):
    out, (coefs, tracks, sems) = refs[:-3], refs[-3:]
    copies = [
        pltpu.make_async_copy(coefs_hbm, coefs, sems.at[0]),
        pltpu.make_async_copy(tracks_hbm, tracks, sems.at[1]),
    ]
    for copy in copies:
        copy.start()
    for copy in copies:
        copy.wait()
    capacity = tracks.shape[2]
    rows = coefs.shape[0]
    for r in range(len(out)):
        plane = (me[0] // 4) ^ r
        kept = []
        for k in (0, 2):
            tr = jnp.concatenate([tracks[plane * 4 + k], tracks[plane * 4 + k + 1]], axis=1)
            top = tr.astype(BF16).astype(F32)
            kept += [top, tr - top]
        pieces = jnp.concatenate(kept, axis=0)
        if 2 * capacity < 128:
            blank = jnp.zeros((pieces.shape[0], 128 - 2 * capacity), F32)
            pieces = jnp.concatenate([pieces, blank], axis=1)
        out[r][:rows, :] = coefs[:, :128]
        out[r][rows : 2 * rows, :] = coefs[:, 128:]
        out[r][2 * rows :, :] = pieces.astype(BF16)


def own_pair(pieces, device):
    half = pieces.shape[0] // 2
    return jnp.where(device & 2 == 0, pieces[:half, :], pieces[half:, :])


def stack_kernel(me, *refs):
    blocks, near, for_y = refs[:-3], refs[-2], refs[-1]
    table = 2 * for_y.shape[1] - near.shape[1]
    for r, block in enumerate(blocks[::-1]):
        near[r] = block[...]
        for_y[r, :table, :] = block[:table, :]
        tracks = own_pair(block[table:, :].astype(F32), me[0] ^ 2)
        for_y[r, table:, :] = tracks.astype(BF16)


def relay_kernel(block, after, out):
    out[...] = block[...]


def unpacked(mine, groups, table, rows_own, capacity):
    kept = []
    for arrived in groups:
        for r in range(arrived.shape[0]):
            at = slice(len(kept) * rows_own, (len(kept) + 1) * rows_own)
            table[at, :128] = arrived[r, :rows_own, :]
            table[at, 128:] = arrived[r, rows_own : 2 * rows_own, :]
            piece = arrived[r, 2 * rows_own :, :].astype(F32)
            if arrived.shape[1] == groups[0].shape[1] and len(groups) > 1:
                piece = own_pair(piece, mine)
            moved = jnp.where(mine & 1 == 0, piece, pltpu.roll(piece, 128 - capacity, 1))
            kept.append(moved[:, :capacity])
    per = 128 // capacity
    tiles = [jnp.concatenate(kept[n : n + per], axis=1) for n in range(0, len(kept), per)]
    return jnp.concatenate(tiles, axis=1).astype(BF16)


def early_kernel(me, near, over_core, over_y, route, pick, coef, per_sub, table, *, capacity):
    places = 3 * near.shape[0]
    rows = table.shape[0]
    pieces = unpacked(me[0], (near, over_core, over_y), table, rows // places, capacity)
    coef[...] = dot(pick[:, :rows], table[...]).astype(BF16)
    per_sub[...] = dot(route[:, : places * capacity], pieces, NT)


def predict_kernel(
    me,
    over_both,
    route,
    back,
    pick,
    weights,
    turns,
    image,
    coef_early,
    per_sub_early,
    *refs,
):
    table, coef, wre, wim, pure, puim, zrow, hre, him, zv = refs[-10:]
    number = image.shape[1]
    slots = back.shape[0]
    outer = over_both.shape[0]
    capacity = slots // (4 * outer)
    rows = table.shape[0]
    vis = turns.shape[1]
    kinds = per_sub_early.shape[1] // 2
    steps = kinds // 2
    chan = vis // steps
    pieces = unpacked(me[0], (over_both,), table, rows // outer, capacity)

    per_sub = per_sub_early[...] + dot(route[:, slots - outer * capacity :], pieces, NT)
    per_sub = per_sub.astype(BF16)
    wide = 2 * steps * chan
    from_row = lax.broadcasted_iota(jnp.int32, (2 * kinds, wide), 0) % kinds
    to_lane = lax.broadcasted_iota(jnp.int32, (2 * kinds, wide), 1) // chan
    spread = (from_row == to_lane).astype(F32).astype(BF16)
    uv = dot(per_sub, spread)
    ur, ui = unit_powers(uv[:, :vis] * turns[...])
    vr, vi = unit_powers(uv[:, vis:] * turns[...])

    pure[pl.ds(0, number, stride=8), :] = jnp.ones_like(ur)
    puim[pl.ds(0, number, stride=8), :] = jnp.zeros_like(ur)
    pure[pl.ds(1, number, stride=8), :] = ur
    puim[pl.ds(1, number, stride=8), :] = ui
    cr, ci = ur, ui
    for k in range(2, 8):
        cr, ci = cmul(cr, ci, ur, ui)
        pure[pl.ds(k, number, stride=8), :] = cr
        puim[pl.ds(k, number, stride=8), :] = ci
    cr, ci = cmul(cr, ci, ur, ui)
    zrow[0] = cr
    zrow[1] = ci
    cr, ci = cmul(cr, ci, cr, ci)
    zrow[2] = cr
    zrow[3] = ci
    zv[0] = vr
    zv[1] = vi
    cr, ci = vr, vi
    for _ in range(3):
        cr, ci = cmul(cr, ci, cr, ci)
    zrow[4] = cr
    zrow[5] = ci

    last = dot(pick[:, pick.shape[1] - rows :], table[...])
    coef[...] = (coef_early[...].astype(F32) + last).astype(BF16)

    block = 32
    for m in range(8):
        beams = dot(coef[...], weights[m])
        for n in range(0, number, block):
            first = beams[n : n + block, :]
            second = beams[number + n : number + n + block, :]
            f_re, f_im, s_re, s_im = first[:, :128], first[:, 128:], second[:, :128], second[:, 128:]
            g_re = f_re * s_re + f_im * s_im
            g_im = f_im * s_re - f_re * s_im
            i_re = image[m, n : n + block, :128].astype(F32)
            i_im = image[m, n : n + block, 128:].astype(F32)
            to = pl.ds(n * 8 + m, block, stride=8)
            wre[to, :] = i_re * g_re - i_im * g_im
            wim[to, :] = i_re * g_im + i_im * g_re

    unroll = 128

    def one(g):
        at = pl.ds(pl.multiple_of(g * 8, 8), 8)
        w_re, w_im = wre[at, :], wim[at, :]
        lhs = [
            jnp.concatenate([w_re[:, n : n + 32], w_im[:, n : n + 32]], axis=1)
            for n in range(0, 128, 32)
        ]
        lhs = jnp.concatenate(lhs, axis=0).astype(BF16)
        p_re, p_im = pure[at, :], puim[at, :]
        z = [jnp.broadcast_to(zrow[k, pl.ds(g, 1), :], (8, 128)) for k in range(6)]
        rr, ii, ri, ir = p_re * z[0], p_im * z[1], p_re * z[1], p_im * z[0]
        up_re, up_im = rr - ii, ri + ir
        dn_re, dn_im = rr + ii, ir - ri
        rr, ii, ri, ir = p_re * z[2], p_im * z[3], p_re * z[3], p_im * z[2]
        lo_re, lo_im = rr + ii, ir - ri
        c = jnp.concatenate([lo_re, dn_re, p_re, up_re], axis=0).astype(BF16)
        s = jnp.concatenate([lo_im, dn_im, p_im, up_im], axis=0).astype(BF16)
        top = jnp.concatenate([c, s], axis=1)
        low = jnp.concatenate([-s, c], axis=1)
        rhs = jnp.concatenate([top, low], axis=0)
        out = dot(lhs, rhs)
        h_re, h_im = out[24:32, :128], out[24:32, 128:]
        for j in (2, 1, 0):
            n_re = h_re * z[4] - h_im * z[5] + out[8 * j : 8 * j + 8, :128]
            h_im = h_re * z[5] + h_im * z[4] + out[8 * j : 8 * j + 8, 128:]
            h_re = n_re
        hre[at, :] = h_re
        him[at, :] = h_im

    @pl.loop(0, number // unroll)
    def _(n):
        for k in range(unroll):
            one(n * unroll + k)

    vr, vi = zv[0], zv[1]
    a_re = hre[pl.ds(7, number, stride=8), :]
    a_im = him[pl.ds(7, number, stride=8), :]
    for k in range(6, -1, -1):
        n_re = a_re * vr - a_im * vi + hre[pl.ds(k, number, stride=8), :]
        a_im = a_re * vi + a_im * vr + him[pl.ds(k, number, stride=8), :]
        a_re = n_re
    cr, ci = cmul(zrow[4], zrow[5], zrow[4], zrow[5])
    m_re, m_im = a_re * cr + a_im * ci, a_im * cr - a_re * ci
    models = jnp.concatenate([m_re, m_im], axis=1).astype(BF16)
    sent = dot(back[...], models)
    along_z, in_plane = refs[:outer], refs[outer : outer + 4]
    half = capacity // 2
    for r in range(outer):
        for p in range(4):
            for start, out in ((0, along_z[r].at[p]), (half, in_plane[p].at[r])):
                at = (p * outer + r) * capacity + start
                block = sent[at : at + half, :]
                block = jnp.concatenate([block[:, :vis], block[:, vis:]], axis=0)
                out[...] = block.astype(BF16)


def turn_kernel(*refs, order):
    blocks, out = refs[: len(order)], refs[len(order) :]
    for i, block in zip(order, blocks):
        for j in range(len(out)):
            out[j][i] = block[j]


def residual_kernel(me, observed, *refs, along_z, in_plane, outer):
    (out, kept, sems), arrived = refs[-3:], refs[:-3]
    arrived = arrived[len(arrived) - len(along_z) - len(in_plane) :]
    rows = kept.shape[1]
    pieces = [(r, p, rows, arrived[n].at[p]) for n, r in enumerate(along_z) for p in range(4)]
    pieces += [
        (r, p, 0, arrived[len(along_z) + n].at[r]) for n, p in enumerate(in_plane) for r in range(outer)
    ]
    copies = []
    for n, (r, p, start, values) in enumerate(pieces):
        source = me[0] ^ (4 * r + p)
        models = values[...].astype(F32)
        for part in range(2):
            own = observed[source, pl.ds(start + part, rows // 2, stride=2), :]
            kept[n, pl.ds(part, rows // 2, stride=2), :] = (
                own - models[part * (rows // 2) : (part + 1) * (rows // 2), :]
            )
        copy = pltpu.make_async_copy(kept.at[n], out.at[source, pl.ds(start, rows), :], sems.at[n])
        copy.start()
        copies.append(copy)
    for copy in copies:
        copy.wait()


def exchange(value, step, tiles):
    return lax.ppermute(value, "tile", [(i, i ^ step) for i in range(tiles)])


def per_device(
    subgrids,
    stations,
    time_slots,
    assign,
    counts,
    beam_coefs,
    beam_basis,
    frequencies,
    uv_tracks,
    observed,
):
    tiles = lax.axis_size("tile")
    capacity = assign.shape[2]
    slots = tiles * capacity
    number = subgrids.shape[0]
    pixels = subgrids.shape[2]
    edge = math.isqrt(pixels)
    slot_count = beam_coefs.shape[1]
    terms2 = beam_coefs.shape[2]
    steps = uv_tracks.shape[4]
    chan = frequencies.shape[0]
    vis = steps * chan
    vmem = pl.BlockSpec(memory_space=pltpu.VMEM)
    own_tracks = jnp.transpose(uv_tracks[0], (0, 2, 3, 1)).reshape(tiles, 2 * steps, capacity)
    own_rows = beam_coefs.shape[0] * slot_count
    smem = pl.BlockSpec(memory_space=pltpu.SMEM)
    anywhere = pl.BlockSpec(memory_space=pl.ANY)
    hbm = pl.BlockSpec(memory_space=pltpu.HBM)
    outer = tiles // 4
    me = lax.axis_index("tile").astype(jnp.int32).reshape(1)
    block = jax.ShapeDtypeStruct((2 * own_rows + 8 * steps, 128), BF16)
    block_y = jax.ShapeDtypeStruct((2 * own_rows + 4 * steps, 128), BF16)
    packed = pl.pallas_call(
        pack_kernel,
        out_shape=[block] * outer,
        in_specs=[smem, hbm, hbm],
        out_specs=[vmem] * outer,
        scratch_shapes=[
            pltpu.VMEM((own_rows, terms2), BF16),
            pltpu.VMEM((tiles, 2 * steps, capacity), F32),
            pltpu.SemaphoreType.DMA((2,)),
        ],
        compiler_params=pltpu.CompilerParams(vmem_limit_bytes=56 * MIB),
        name="pack",
    )(me, beam_coefs.reshape(own_rows, terms2), own_tracks)
    along = [packed[0]] + [exchange(packed[r], 4 * r, tiles) for r in range(1, outer)]

    cells = jnp.transpose(subgrids.reshape(number, 2, 8, 128), (0, 2, 1, 3))
    cells = cells.reshape(number * 16, 128)
    row_turns, cell_turns = transform_tables(edge)
    image = pl.pallas_call(
        transform_kernel,
        out_shape=jax.ShapeDtypeStruct((8, number, 256), BF16),
        in_specs=[vmem] * 3,
        out_specs=vmem,
        scratch_shapes=[
            pltpu.VMEM((8, 256, 256), BF16),
            pltpu.VMEM((8, 256, 256), BF16),
            pltpu.VMEM((number * 16, 128), F32),
            pltpu.VMEM((8, number, 512), BF16),
        ],
        compiler_params=pltpu.CompilerParams(vmem_limit_bytes=14 * MIB),
        name="transform",
    )(cells, jnp.asarray(row_turns), jnp.asarray(cell_turns))

    near, for_y = pl.pallas_call(
        stack_kernel,
        out_shape=[
            jax.ShapeDtypeStruct((outer,) + block.shape, BF16),
            jax.ShapeDtypeStruct((outer,) + block_y.shape, BF16),
        ],
        in_specs=[smem] + [vmem] * outer + [anywhere],
        out_specs=[vmem] * 2,
        compiler_params=pltpu.CompilerParams(vmem_limit_bytes=3 * MIB * (tiles // 16)),
        name="stack",
    )(me, *along[::-1], image)
    over_core = exchange(near, 1, tiles)
    over_y = exchange(for_y, 2, tiles)
    route, back, pick, weights, turns = pl.pallas_call(
        functools.partial(prepare_kernel, slot_count=slot_count),
        out_shape=[
            jax.ShapeDtypeStruct((number, slots), BF16),
            jax.ShapeDtypeStruct((slots, number), BF16),
            jax.ShapeDtypeStruct((2 * number, tiles * own_rows), BF16),
            jax.ShapeDtypeStruct((8, terms2, 256), BF16),
            jax.ShapeDtypeStruct((1, vis), F32),
        ],
        in_specs=[smem] * 2 + [vmem] * 5 + [anywhere],
        out_specs=[vmem] * 5,
        compiler_params=pltpu.CompilerParams(vmem_limit_bytes=8 * MIB * (1 + tiles // 64)),
        name="prepare",
    )(
        me,
        counts,
        assign[0],
        stations.T,
        time_slots.reshape(1, number),
        beam_basis,
        frequencies.reshape(1, chan),
        near,
    )

    over_y = pl.pallas_call(
        relay_kernel,
        out_shape=jax.ShapeDtypeStruct((outer,) + block_y.shape, BF16),
        in_specs=[vmem, anywhere],
        out_specs=vmem,
        compiler_params=pltpu.CompilerParams(vmem_limit_bytes=2 * MIB * (tiles // 16)),
        name="relay",
    )(over_y, weights)
    over_both = exchange(over_y, 1, tiles)
    coef_early, per_sub_early = pl.pallas_call(
        functools.partial(early_kernel, capacity=capacity),
        out_shape=[
            jax.ShapeDtypeStruct((2 * number, terms2), BF16),
            jax.ShapeDtypeStruct((number, 4 * steps), F32),
        ],
        in_specs=[smem] + [vmem] * 5,
        out_specs=[vmem] * 2,
        scratch_shapes=[pltpu.VMEM((3 * outer * own_rows, terms2), BF16)],
        compiler_params=pltpu.CompilerParams(vmem_limit_bytes=8 * MIB * (1 + tiles // 64)),
        name="early",
    )(me, near, over_core, over_y, route, pick)

    for_z = jax.ShapeDtypeStruct((4, capacity, vis), BF16)
    for_plane = jax.ShapeDtypeStruct((outer, capacity, vis), BF16)
    models = pl.pallas_call(
        predict_kernel,
        out_shape=[for_z] * outer + [for_plane] * 4,
        in_specs=[smem] + [vmem] * 9,
        out_specs=[vmem] * (outer + 4),
        scratch_shapes=[
            pltpu.VMEM((outer * own_rows, terms2), BF16),
            pltpu.VMEM((2 * number, terms2), BF16),
            pltpu.VMEM((number * 8, 128), F32),
            pltpu.VMEM((number * 8, 128), F32),
            pltpu.VMEM((number * 8, vis), F32),
            pltpu.VMEM((number * 8, vis), F32),
            pltpu.VMEM((6, number, vis), F32),
            pltpu.VMEM((number * 8, vis), F32),
            pltpu.VMEM((number * 8, vis), F32),
            pltpu.VMEM((2, number, vis), F32),
        ],
        compiler_params=pltpu.CompilerParams(vmem_limit_bytes=20 * MIB * (1 + tiles // 64)),
        name="predict",
    )(
        me,
        over_both,
        route,
        back,
        pick,
        weights,
        turns,
        image,
        coef_early,
        per_sub_early,
    )
    def turned(blocks, order, out_shape):
        return pl.pallas_call(
            functools.partial(turn_kernel, order=order),
            out_shape=out_shape,
            in_specs=[vmem] * len(blocks),
            out_specs=[vmem] * len(out_shape),
            compiler_params=pltpu.CompilerParams(vmem_limit_bytes=2 * MIB),
            name="turn",
        )(*[blocks[i] for i in order])

    first, second = models[:outer], models[outer:]
    second = [second[0]] + [exchange(second[p], p, tiles) for p in range(1, 4)]
    first = [first[0]] + [exchange(first[r], 4 * r, tiles) for r in range(1, outer)]
    second = turned(second, (1, 2, 3, 0), [for_z] * outer)
    second = [second[0]] + [exchange(second[r], 4 * r, tiles) for r in range(1, outer)]
    first = turned(first, tuple(range(outer))[::-1], [for_plane] * 4)
    first = [first[0]] + [exchange(first[p], p, tiles) for p in range(1, 4)]
    ours = observed.reshape(tiles, 2 * capacity, vis)

    def finish(name, along_z, in_plane, held):
        count = 4 * len(along_z) + outer * len(in_plane)
        arrived = [second[r] for r in along_z] + [first[p] for p in in_plane]
        return pl.pallas_call(
            functools.partial(residual_kernel, along_z=along_z, in_plane=in_plane, outer=outer),
            out_shape=jax.ShapeDtypeStruct(ours.shape, F32),
            in_specs=[smem, vmem] + [anywhere] * len(held) + [vmem] * len(arrived),
            out_specs=anywhere,
            scratch_shapes=[
                pltpu.VMEM((count, capacity, vis), F32),
                pltpu.SemaphoreType.DMA((count,)),
            ],
            input_output_aliases={2: 0} if held else {},
            compiler_params=pltpu.CompilerParams(vmem_limit_bytes=6 * MIB),
            name=name,
        )(me, ours, *held, *arrived)

    residual = finish("residual_early", (0, outer - 1), (0,), ())
    residual = finish("residual_next", tuple(range(1, outer - 1))[::-1], (3,), (residual,))
    residual = finish("residual_last", (), (2, 1), (residual,))
    return residual.reshape(observed.shape)


def solution(mesh):
    return jax.shard_map(
        per_device,
        mesh=mesh,
        in_specs=(
            P(("grp", "tile"), None, None),
            P(("grp", "tile"), None),
            P(("grp", "tile")),
            P(("grp", "tile"), None, None),
            P(("grp", "tile"), None),
            P(("grp", "tile"), None, None),
            P(),
            P("grp"),
            P(("grp", "tile"), None, None, None, None),
            P(("grp", "tile"), None, None, None, None),
        ),
        out_specs=P(("grp", "tile"), None, None, None, None),
        check_vma=False,
    )
```
